128 devices in a mesh: fsdp: 64 (over z, y_lo, x, core), rep: 2 (over y_hi).
Axes of the slice: x: 4, y: 4 (y_hi: 2, y_lo: 2; y = y_hi * 2 + y_lo), z: 4, core: 2. Of those that a mesh axis runs over, the one named last changes fastest.
Arguments:
- tokens: bfloat16 [16384, 1536], P(('fsdp', 'rep')), may hold values from -6 to 6
- segment_ids: int32 [128, 128], P(('fsdp', 'rep')), may hold values from 0 to 31, never falling along the last dimension, each value on 1 to 64 neighbouring positions
- routes: int32 [16384, 6], P(('fsdp', 'rep')), may hold values from 0 to 63, all different within a row; in each aligned block of 128 rows (0 to 127, 128 to 255, ...) at most 24 rows name the same one
- cotangent: bfloat16 [16384, 1536], P(('fsdp', 'rep')), may hold values from -6 to 6
- query_weight: bfloat16 [1536, 1536], P(('fsdp', 'rep')), may hold values from -0.15625 to 0.15625
- key_weight: bfloat16 [1536, 512], P(('fsdp', 'rep')), may hold values from -0.15625 to 0.15625
- value_weight: bfloat16 [1536, 512], P(('fsdp', 'rep')), may hold values from -0.15625 to 0.15625
- output_weight: bfloat16 [1536, 1536], P(('fsdp', 'rep')), may hold values from -0.625 to 0.625
- shared_gate: bfloat16 [1536, 1024], P(('fsdp', 'rep')), may hold values from -0.15625 to 0.15625
- shared_up: bfloat16 [1536, 1024], P(('fsdp', 'rep')), may hold values from -0.15625 to 0.15625
- shared_down: bfloat16 [1024, 1536], P(('fsdp', 'rep')), may hold values from -0.25 to 0.25
- router_weight: bfloat16 [1536, 64], P(('fsdp', 'rep')), may hold values from -0.078125 to 0.078125
- first_gain: bfloat16 [1536], P(('fsdp', 'rep')), may hold values from 0.099609375 to 1.8984375
- second_gain: bfloat16 [1536], P(('fsdp', 'rep')), may hold values from 0.099609375 to 1.8984375
- expert_gate: bfloat16 [64, 1536, 512], P('fsdp', None, 'rep'), may hold values from -0.15625 to 0.15625
- expert_up: bfloat16 [64, 1536, 512], P('fsdp', None, 'rep'), may hold values from -0.15625 to 0.15625
- expert_down: bfloat16 [64, 512, 1536], P('fsdp', 'rep'), may hold values from -0.75 to 0.75
Outputs:
- block_out: bfloat16 [16384, 1536], P(('fsdp', 'rep'))
- grad_tokens: float32 [16384, 1536], P(('fsdp', 'rep'))
- grad_query_weight: float32 [1536, 1536], P(('fsdp', 'rep'))
- grad_key_weight: float32 [1536, 512], P(('fsdp', 'rep'))
- grad_value_weight: float32 [1536, 512], P(('fsdp', 'rep'))
- grad_output_weight: float32 [1536, 1536], P(('fsdp', 'rep'))
- grad_shared_gate: float32 [1536, 1024], P(('fsdp', 'rep'))
- grad_shared_up: float32 [1536, 1024], P(('fsdp', 'rep'))
- grad_shared_down: float32 [1024, 1536], P(('fsdp', 'rep'))
- grad_router_weight: float32 [1536, 64], P(('fsdp', 'rep'))
- grad_first_gain: float32 [1536], P(('fsdp', 'rep'))
- grad_second_gain: float32 [1536], P(('fsdp', 'rep'))
- grad_expert_gate: float32 [64, 1536, 512], P('fsdp', None, 'rep')
- grad_expert_up: float32 [64, 1536, 512], P('fsdp', None, 'rep')
- grad_expert_down: float32 [64, 512, 1536], P('fsdp', 'rep')
The draws below stay inside these ranges and needn't reach their ends.
Inputs may be any that keep to these rules, and one draw needn't show every extreme that they name: `routes`: among the 128 rows of one device no expert is named by more than 24 rows, a bound that some block reaches; a row names 6 different experts. `segment_ids`: within a device's row the numbers never fall; a sequence holds 1 to 64 tokens, one exactly 64.
All inputs are finite; a program needn't handle non-finite values.
Results may differ from the reference program's by a relative error of at most 0.024.
Values may be sent and summed in bfloat16 or wider, within the bound.
A program may use at most 256 MiB of HBM per device.

```python
import math
import jax
import jax.numpy as jnp
import numpy as np
from jax import lax

D = 1536
HEADS = 12
KV_HEADS = 4
HEAD_DIM = 128
EXP_HID = 512
SHARED_HID = 1024
TOP = 6
TOK_DEV = 128
EXPERTS = 64
KVD = 512
CAP = 24
TOKENS = 16384
N_FSDP = 64
N_REP = 2


def level_of(rng, dims, shards, low, top_value):
    level = 1.0
    for dim, blocks in shards:
        draws = jax.random.uniform(jax.random.fold_in(jax.random.fold_in(rng, 6), dim), (blocks,), jnp.float32, low / len(shards), top_value / len(shards))
        level = level * jnp.repeat(jnp.exp(draws), dims[dim] // blocks).reshape((-1,) + (1,) * (len(dims) - 1 - dim))
    return level


def length_profile(amount, total, bound, slope):
    loads = [(1 << 20) // math.isqrt(standing ** slope) + 1 for standing in range(2, amount + 1)]
    surplus, counts = total - bound - (amount - 1), [1] * (amount - 1)
    while surplus > 0:
        candidates = [i for i in range(amount - 1) if counts[i] < bound]
        mass, remaining = sum([loads[i] for i in candidates]), surplus
        for i in candidates:
            extra = min(bound - counts[i], max(1, remaining * loads[i] // mass), surplus)
            counts[i] = counts[i] + extra
            surplus = surplus - extra
    return np.array([bound] + counts)


def ragged_sizes(key, number_of, total, most, skew):
    if number_of == 2:
        one = jax.random.randint(key, (), max(1, total - most), min(most, total - 1) + 1)
        return jnp.stack([one, total - one])
    tallies = jnp.asarray(length_profile(number_of, total, most, skew), jnp.int32)
    couples = (number_of - 1) // 2
    source_of, receiver = tallies[1:1 + 2 * couples:2], tallies[2:2 + 2 * couples:2]
    room = jnp.minimum(source_of - 1, most - receiver)
    passed = jax.random.randint(jax.random.fold_in(key, 1), (couples,), 0, 1 << 20) % (room + 1)
    tallies = tallies.at[1:1 + 2 * couples:2].set(source_of - passed).at[2:2 + 2 * couples:2].set(receiver + passed)
    return tallies[jax.random.permutation(jax.random.fold_in(key, 2), number_of)]


def assign_block(stream_key, own, number, rows, amount, top, bound, slope):
    order = jax.random.permutation(stream_key, amount)
    packed, usual = shares(amount, rows * top, bound, slope, True), shares(amount, rows * top, bound, slope, False)
    places = jnp.arange(amount)

    def named(lengths, rotation):
        used = int((lengths > 0).sum())
        fixed = max(1, used // 4)
        shifted = fixed + (places - fixed + rotation * (used - fixed)) % max(1, amount - fixed)
        return jnp.zeros((amount,), jnp.int32).at[order[jnp.where(places < fixed, places, shifted)]].set(jnp.asarray(lengths, jnp.int32))

    lengths = jnp.where(number % 4 == 0, named(packed, number // 4), named(usual, number - number // 4 - 1))
    mixed = jax.random.permutation(jax.random.fold_in(own, 3), amount)
    donor, taker = mixed[0:amount // 2 * 2:2], mixed[1:amount // 2 * 2:2]
    margin = jnp.minimum(lengths[donor] - 1, bound - lengths[taker]) // 2
    margin = jnp.where((donor == order[0]) | (taker == order[0]) | (lengths[taker] == 0), 0, jnp.maximum(margin, 0))
    shifted = jax.random.randint(jax.random.fold_in(own, 4), (amount // 2,), 0, 1 << 20) % (margin + 1)
    lengths = lengths.at[donor].add(-shifted).at[taker].add(shifted)
    labels = jnp.searchsorted(jnp.cumsum(lengths), jnp.arange(rows * top), side="right").astype(jnp.int32)
    listing = labels.reshape(top, rows).T
    listing = listing[jax.random.permutation(jax.random.fold_in(own, 1), rows)]
    rotation = jax.random.randint(jax.random.fold_in(own, 2), (rows, 1), 0, top)
    return jnp.take_along_axis(listing, (jnp.arange(top)[None, :] + rotation) % top, axis=1)


def shares(number_of, total, bound, skew, full):
    portions = [(1 << 20) // math.isqrt(grade ** skew) + 1 for grade in range(1, number_of + 1)]
    largest = bound if full else min(bound, max(-(-total // number_of), total * portions[0] // sum(portions)))
    least = 1 if total - largest >= number_of - 1 else 0
    counts, rest = [largest] + [least] * (number_of - 1), total - largest - least * (number_of - 1)
    while rest > 0:
        movable = [i for i in range(1, number_of) if counts[i] < largest] or [i for i in range(1, number_of) if counts[i] < bound]
        mass, budget = sum([portions[i] for i in movable]), rest
        for i in movable:
            extra = min(bound - counts[i], max(1, budget * portions[i] // mass), rest)
            counts[i] = counts[i] + extra
            rest = rest - extra
    return np.array(counts)


def scatter_about(own_key, extent, spread, bound, split=(), held_as=jnp.bfloat16):
    entries = spread * jax.random.normal(own_key, extent, jnp.float32)
    if split:
        entries = entries * level_of(own_key, extent, split, -0.22, 0.18)
    return jnp.clip(entries, -bound, bound).astype(held_as)


def setup_inputs(seed: int = 0) -> dict:
    key_of = jax.random.split(jax.random.key(seed), 18)
    tokens = scatter_about(key_of[0], (TOKENS, D), 1.0, 6.0, ((0, 128),))
    segment_ids = jax.vmap(lambda own: jnp.searchsorted(jnp.cumsum(ragged_sizes(own, TOK_DEV // 4, TOK_DEV, TOK_DEV // 2, 2)), jnp.arange(TOK_DEV), side="right"))(jax.random.split(key_of[1], (N_FSDP * N_REP))).reshape((N_FSDP * N_REP, TOK_DEV)).astype(jnp.int32)
    routes_keys = jax.random.split(jax.random.fold_in(key_of[2], 1), TOKENS // TOK_DEV)
    routes_turns = jax.random.permutation(jax.random.fold_in(key_of[2], 3), TOKENS // TOK_DEV)
    routes = jax.vmap(lambda own, number: assign_block(jax.random.fold_in(key_of[2], 2), own, number, TOK_DEV, EXPERTS, TOP, CAP, 2))(routes_keys, routes_turns).reshape((TOKENS, TOP))
    cotangent = scatter_about(key_of[3], (TOKENS, D), 1.0, 6.0, ((0, 128),))
    query_weight = scatter_about(key_of[4], (D, D), D ** -0.5, 0.15625, ((0, 128),))
    key_weight = scatter_about(key_of[5], (D, KVD), D ** -0.5, 0.15625, ((0, 128),))
    value_weight = scatter_about(key_of[6], (D, KVD), D ** -0.5, 0.15625, ((0, 128),))
    output_weight = scatter_about(key_of[7], (D, D), (D // 16) ** -0.5, 0.625, ((0, 128),))
    shared_gate = scatter_about(key_of[8], (D, SHARED_HID), D ** -0.5, 0.15625, ((0, 128),))
    shared_up = scatter_about(key_of[9], (D, SHARED_HID), D ** -0.5, 0.15625, ((0, 128),))
    shared_down = scatter_about(key_of[10], (SHARED_HID, D), (SHARED_HID // 2) ** -0.5, 0.25, ((0, 128),))
    router_weight = scatter_about(key_of[11], (D, EXPERTS), (4 * D) ** -0.5, 0.078125, ((0, 128),))
    first_gain = jnp.clip(1.0 + 0.18 * jax.random.normal(key_of[12], (D,), jnp.float32), 0.099609375, 1.8984375).astype(jnp.bfloat16)
    second_gain = jnp.clip(1.0 + 0.18 * jax.random.normal(key_of[13], (D,), jnp.float32), 0.099609375, 1.8984375).astype(jnp.bfloat16)
    expert_gate = scatter_about(key_of[14], (EXPERTS, D, EXP_HID), D ** -0.5, 0.15625, ((0, 64), (2, 2)))
    expert_up = scatter_about(key_of[15], (EXPERTS, D, EXP_HID), D ** -0.5, 0.15625, ((0, 64), (2, 2)))
    expert_down = scatter_about(key_of[16], (EXPERTS, EXP_HID, D), (EXP_HID // 8) ** -0.5, 0.75, ((0, 64), (1, 2)))
    return dict(tokens=tokens, segment_ids=segment_ids, routes=routes, cotangent=cotangent, query_weight=query_weight, key_weight=key_weight, value_weight=value_weight, output_weight=output_weight, shared_gate=shared_gate, shared_up=shared_up, shared_down=shared_down, router_weight=router_weight, first_gain=first_gain, second_gain=second_gain, expert_gate=expert_gate, expert_up=expert_up, expert_down=expert_down)


@jax.custom_vjp
def low(v):
    return lax.optimization_barrier(v.astype(jnp.bfloat16)).astype(jnp.float32)

@jax.custom_vjp
def low_back(v):
    return v

def low_keep(v):
    return (low(v), None)

def low_pass(kept, grad):
    return (grad,)

def back_keep(v):
    return (v, None)

def back_low(kept, grad):
    return (low(grad),)
low.defvjp(low_keep, low_pass)
low_back.defvjp(back_keep, back_low)
epsilon = 1e-06
highest = lax.Precision.HIGHEST

def product(left, right):
    return jnp.dot(left, right, precision=highest)

def rms_norm(values, gain):
    return values * lax.rsqrt(lax.optimization_barrier(jnp.mean(values * values, axis=-1, keepdims=True)) + epsilon) * gain

def attend_block(pieces):
    query, keys, values, segment = pieces
    rows = query.shape[0]
    groups = HEADS // KV_HEADS
    query_heads = query.reshape(rows, KV_HEADS, groups, HEAD_DIM)
    key_heads = keys.reshape(rows, KV_HEADS, HEAD_DIM)
    value_heads = values.reshape(rows, KV_HEADS, HEAD_DIM)
    scores = jnp.einsum('tkgd,skd->kgts', query_heads, key_heads, precision=highest) * (1.0 / math.sqrt(HEAD_DIM))
    scores = low_back(scores)
    position = jnp.arange(rows, dtype=jnp.int32)
    allowed = (segment[:, None] == segment[None, :]) & (position[:, None] >= position[None, :])
    scores = jnp.where(allowed, scores, -1e+30)
    probs = low(jax.nn.softmax(scores, axis=-1))
    mixed = jnp.einsum('kgts,skd->tkgd', probs, value_heads, precision=highest)
    return mixed.reshape(rows, D)

def slot_table(routes):
    devices = N_FSDP * N_REP
    per_device = TOK_DEV * TOP
    flat = routes.reshape(devices, per_device)
    onehot = (flat[:, :, None] == jnp.arange(EXPERTS, dtype=jnp.int32)[None, None, :]).astype(jnp.int32)
    place = lax.optimization_barrier(jnp.sum((jnp.cumsum(onehot, axis=1) - onehot) * onehot, axis=-1)).astype(jnp.int32)
    device_ids = jnp.arange(devices, dtype=jnp.int32)[:, None]
    column = device_ids * CAP + place
    assign = device_ids * per_device + jnp.arange(per_device, dtype=jnp.int32)[None, :]
    table = jnp.full((EXPERTS, devices * CAP), TOKENS * TOP, jnp.int32)
    return table.at[flat, column].set(assign)

def reference(tokens, segment_ids, routes, cotangent, query_weight, key_weight, value_weight, output_weight, shared_gate, shared_up, shared_down, router_weight, first_gain, second_gain, expert_gate, expert_up, expert_down):
    table = slot_table(routes)
    devices = N_FSDP * N_REP

    def forward(source, w_query, w_key, w_value, w_output, w_sgate, w_sup, w_sdown, w_router, gain_one, gain_two, gate_all, up_all, down_all):
        normed = low(rms_norm(source, gain_one))
        query = low(low_back(product(normed, w_query)))
        keys = low(low_back(product(normed, w_key)))
        values = low(low_back(product(normed, w_value)))
        attended = lax.map(jax.checkpoint(attend_block), (query.reshape(devices, TOK_DEV, D), keys.reshape(devices, TOK_DEV, KVD), values.reshape(devices, TOK_DEV, KVD), segment_ids))
        attended = low(low_back(attended.reshape(TOKENS, D)))
        resid = source + low_back(product(attended, w_output))
        normed_two = low(rms_norm(resid, gain_two))
        logits = low_back(product(normed_two, w_router))
        gates = jax.nn.softmax(jnp.take_along_axis(logits, routes, axis=1), axis=-1)
        shared_pre_gate = low_back(product(normed_two, w_sgate))
        shared_pre_up = low_back(product(normed_two, w_sup))
        shared_hidden = low(low_back(jax.nn.silu(shared_pre_gate) * shared_pre_up))
        shared_out = low_back(product(shared_hidden, w_sdown))
        normed_ext = jnp.concatenate([normed_two, jnp.zeros((1, D), jnp.float32)], axis=0)
        gates_ext = jnp.concatenate([gates.reshape(-1), jnp.zeros((1,), jnp.float32)], axis=0)

        def produce(assign, weight_gate, weight_up, weight_down):
            token = assign // TOP
            rows = low_back(normed_ext[token])
            pre_gate = low_back(product(rows, weight_gate))
            pre_up = low_back(product(rows, weight_up))
            hidden = low(low_back(jax.nn.silu(pre_gate) * pre_up))
            made = low(low_back(product(hidden, weight_down)))
            return gates_ext[assign][:, None] * made
        checked = jax.checkpoint(produce)

        def expert_step(total, piece):
            assign, weight_gate, weight_up, weight_down = piece
            return (total.at[assign // TOP].add(checked(assign, weight_gate, weight_up, weight_down)), None)
        mixture, unused = lax.scan(expert_step, jnp.zeros((TOKENS + 1, D), jnp.float32), (table, gate_all, up_all, down_all))
        return resid + shared_out + mixture[:TOKENS]
    floats = tuple((item.astype(jnp.float32) for item in (tokens, query_weight, key_weight, value_weight, output_weight, shared_gate, shared_up, shared_down, router_weight, first_gain, second_gain, expert_gate, expert_up, expert_down)))
    final, pullback = jax.vjp(forward, *floats)
    grads = pullback(cotangent.astype(jnp.float32))
    return (final.astype(jnp.bfloat16), grads[0], grads[1], grads[2], grads[3], grads[4], grads[5], grads[6], grads[7], grads[8], grads[9], grads[10], grads[11], grads[12], grads[13])
```

```python
import functools
import math

import jax
import jax.numpy as jnp
from jax import lax
from jax.experimental import pallas as pl
from jax.experimental.pallas import tpu as pltpu
from jax.sharding import PartitionSpec as P

MESH = pl.DeviceIdType.MESH
ANY = pl.BlockSpec(memory_space=pl.ANY)
VM = pl.BlockSpec(memory_space=pltpu.VMEM)
ORDERS = ("xyz", "yzx", "zxy", "xyz", "yzx", "zxy")
PIECE = [12, 12, 12, 12, 12, 8]


def place():
    f, r = lax.axis_index("fsdp"), lax.axis_index("rep")
    return dict(x=(f // 2) % 4, y=2 * r + (f // 8) % 2, z=f // 16, core=f % 2)


def device(at):
    return (((at["z"] * 2 + at["y"] % 2) * 4 + at["x"]) * 2 + at["core"], at["y"] // 2)


def moved(at, axis, by):
    return {**at, axis: (at[axis] + by) % (2 if axis == "core" else 4)}


def region(at, order, done, coordinate=None, half=None):
    first = done[0] if done else None
    spot = {}
    for axis in "xyz":
        whole = axis in done
        at_axis = at[axis]
        if axis == "y":
            if whole:
                spot["yhi"] = (half if (half is not None and first == "y") else slice(None))
                spot["ylo"] = slice(None)
            else:
                spot["yhi"], spot["ylo"] = at_axis // 2, at_axis % 2
        else:
            if whole:
                spot[axis] = pl.ds(2 * half, 2) if (half is not None and first == axis) else slice(None)
            else:
                spot[axis] = at_axis
    return (at["core"], spot["yhi"], spot["z"], spot["ylo"], spot["x"])


def gather_kernel(*refs, n, rows, piece):
    ins, outs = refs[:n], refs[n:2 * n]
    got, stage = refs[2 * n:3 * n], refs[3 * n:4 * n]
    mix_send, mix_recv, own_sem, send, recv, dsend, drecv = refs[4 * n:]
    at = place()
    mine = at["core"] * 2 + at["y"] // 2
    peers = [moved(at, "core", 1), moved(at, "y", 2), moved(moved(at, "core", 1), "y", 2)]
    around = [moved(at, axis, by) for axis in "xyz" for by in (1, -1)]
    barrier = pltpu.get_barrier_semaphore()
    for other in peers + around:
        pl.semaphore_signal(barrier, inc=1, device_id=device(other), device_id_type=MESH)
    pl.semaphore_wait(barrier, len(peers) + len(around))

    def remote(src, dst, s, r, to):
        return pltpu.make_async_remote_copy(src_ref=src, dst_ref=dst, send_sem=s, recv_sem=r, device_id=device(to), device_id_type=MESH)

    started = []

    def go(copy):
        copy.start()
        started.append(copy)
        return copy

    mixes = []
    for i in range(n):
        own = pltpu.make_async_copy(ins[i].at[mine], got[i].at[mine], own_sem.at[i])
        own.start()
        copies = []
        for k, to in enumerate(peers):
            quarter = to["core"] * 2 + to["y"] // 2
            copies.append(go(remote(ins[i].at[quarter], got[i].at[mine], mix_send.at[i, k], mix_recv.at[i, k], to)))
        mixes.append((own, copies))
    keep = []
    for i in range(n):
        own, copies = mixes[i]
        own.wait()
        for copy in copies:
            copy.wait_recv()
        size, take = rows[i], piece[i]
        to_row = lax.broadcasted_iota(jnp.int32, (size, 64), 0)
        from_row = lax.broadcasted_iota(jnp.int32, (size, 64), 1)
        pick = ((to_row // take) * 16 + to_row % take == from_row).astype(jnp.bfloat16)
        whole = got[i][...].reshape(64, got[i].shape[2])
        stage[i][...] = jnp.dot(pick, whole, preferred_element_type=jnp.float32).astype(jnp.bfloat16)
        local = pltpu.make_async_copy(stage[i], outs[i].at[region(at, ORDERS[i], "")], own_sem.at[i])
        local.start()
        keep.append(local)
    sibling = moved(at, "core", 1)
    for phase in range(3):
        firsts, seconds = [], []
        if phase == 1:
            for local in keep:
                local.wait()
        for i in range(n):
            order = ORDERS[i]
            axis, done = order[phase], order[:phase]
            here = region(at, order, done)
            src = stage[i] if phase == 0 else outs[i].at[here]
            up = go(remote(src, outs[i].at[here], send.at[i, phase, 0], recv.at[i, phase, 0], moved(at, axis, 1)))
            down = go(remote(src, outs[i].at[here], send.at[i, phase, 1], recv.at[i, phase, 1], moved(at, axis, -1)))
            firsts.append((up, down))
            if phase == 0:
                go(remote(src, outs[i].at[here], dsend.at[i, 0, 4], drecv.at[i, 0, 4], sibling))
        for i in range(n):
            order = ORDERS[i]
            axis, done = order[phase], order[:phase]
            up, down = firsts[i]
            pair = []
            for k, (copy, step) in enumerate(((up, 1), (down, -1))):
                copy.wait_recv()
                block = moved(at, axis, -step)
                if phase == 0:
                    low = 16 if rows[i] == 48 else rows[i] // 2
                    part = pl.ds(0, low) if k == 0 else pl.ds(low, rows[i] - low)
                    where = region(block, order, done) + (part,)
                else:
                    where = region(block, order, done, half=k)
                pair.append(go(remote(outs[i].at[where], outs[i].at[where], send.at[i, phase, 2 + k], recv.at[i, phase, 2 + k], moved(at, axis, step))))
                whole = region(block, order, done)
                go(remote(outs[i].at[whole], outs[i].at[whole], dsend.at[i, phase, k], drecv.at[i, phase, k], sibling))
            seconds.append(pair)
        for i in range(n):
            order = ORDERS[i]
            axis, done = order[phase], order[:phase]
            for k in range(2):
                seconds[i][k].wait_recv()
            far = region(moved(at, axis, 2), order, done)
            go(remote(outs[i].at[far], outs[i].at[far], dsend.at[i, phase, 2], drecv.at[i, phase, 2], sibling))
    for copy in started:
        copy.wait_send()
    for i in range(n):
        order = ORDERS[i]
        for phase in range(3):
            axis, done = order[phase], order[:phase]
            for k, by in enumerate((-1, 1, 2)):
                there = moved(moved(at, axis, by), "core", 1)
                where = outs[i].at[region(there, order, done)]
                remote(where, where, dsend.at[i, phase, k], drecv.at[i, phase, k], sibling).wait_recv()
        where = outs[i].at[region(sibling, order, "")]
        remote(where, where, dsend.at[i, 0, 4], drecv.at[i, 0, 4], sibling).wait_recv()


def gather(shards, piece, cid=1):
    n = len(shards)
    rows = [4 * p for p in piece]
    outs = pl.pallas_call(
        functools.partial(gather_kernel, n=n, rows=rows, piece=piece),
        out_shape=[jax.ShapeDtypeStruct((2, 2, 4, 2, 4, rows[i], shards[i].shape[2]), jnp.bfloat16) for i in range(n)],
        in_specs=[VM] * n,
        out_specs=[ANY] * n,
        scratch_shapes=[pltpu.VMEM((4, 16, s.shape[2]), jnp.bfloat16) for s in shards]
        + [pltpu.VMEM((rows[i], shards[i].shape[2]), jnp.bfloat16) for i in range(n)]
        + [pltpu.SemaphoreType.DMA((n, 3)), pltpu.SemaphoreType.DMA((n, 3)), pltpu.SemaphoreType.DMA((n,)),
           pltpu.SemaphoreType.DMA((n, 3, 4)), pltpu.SemaphoreType.DMA((n, 3, 4)),
           pltpu.SemaphoreType.DMA((n, 3, 5)), pltpu.SemaphoreType.DMA((n, 3, 5))],
        compiler_params=pltpu.CompilerParams(collective_id=cid, has_side_effects=True, vmem_limit_bytes=40 << 20),
        name="gather_weights",
    )(*shards)
    return [o.reshape(4, 32 * rows[i], o.shape[-1]) for i, o in enumerate(outs)]


def pack(local, piece):
    p, n = local.shape
    q = local.reshape(p, 4, n // 4).transpose(1, 0, 2)
    return jnp.pad(q, ((0, 0), (0, 16 - p), (0, 0)))


def half_shape(order, phase):
    if phase == 0:
        return ()
    if phase == 1:
        return (2,)
    return {"xyz": (2, 2, 2), "yzx": (4, 2), "zxy": (2, 4)}[order]


def scatter_kernel(*refs, n, rows, piece, orders):
    ins, outs = refs[:n], refs[n:2 * n]
    total, other = refs[2 * n:3 * n], refs[3 * n:4 * n]
    landing = [refs[4 * n + 3 * i:4 * n + 3 * i + 3] for i in range(n)]
    spread = refs[7 * n:8 * n]
    own_sem, dsend, drecv, send, recv, msend, mrecv = refs[8 * n:]
    at = place()
    mine = at["core"] * 2 + at["y"] // 2
    sibling = moved(at, "core", 1)
    peers = [sibling, moved(at, "y", 2), moved(sibling, "y", 2)]
    around = [moved(at, axis, by) for axis in "xyz" for by in (1, -1)]
    barrier = pltpu.get_barrier_semaphore()
    for to in peers + around:
        pl.semaphore_signal(barrier, inc=1, device_id=device(to), device_id_type=MESH)
    pl.semaphore_wait(barrier, len(peers) + len(around))

    def remote(src, dst, s, r, to):
        return pltpu.make_async_remote_copy(src_ref=src, dst_ref=dst, send_sem=s, recv_sem=r, device_id=device(to), device_id_type=MESH)

    started = []

    def go(copy):
        copy.start()
        started.append(copy)
        return copy

    def add(to, where, ref, spot):
        to[where] = (to[where].astype(jnp.float32) + ref[spot].astype(jnp.float32)).astype(jnp.bfloat16)

    firsts = []
    for i in range(n):
        own = pltpu.make_async_copy(ins[i].at[at["core"]], total[i], own_sem.at[i])
        own.start()
        firsts.append((own, go(remote(ins[i].at[1 - at["core"]], other[i], dsend.at[i], drecv.at[i], sibling))))

    def cut(i, k):
        low = 16
        return pl.ds(0, low) if k == 0 else pl.ds(low, rows[i] - low)

    def part(i, phase, spot, k):
        done = orders[i][:phase]
        if phase == 0:
            return region(spot, orders[i], done)[1:] + (cut(i, k),)
        return region(spot, orders[i], done, half=k)[1:]

    def box(i, phase, side, k, message):
        ref = landing[i][phase]
        if phase == 0:
            return (side, message, cut(i, k))
        return (side, message)

    def message(i, phase, side, number):
        axis = orders[i][phase]
        step = 1 if side == 0 else -1
        spot, k = ((moved(at, axis, 2), side), (moved(at, axis, step), 1 - side), (moved(at, axis, step), side))[number]
        src = total[i].at[part(i, phase, spot, k)]
        dst = landing[i][phase].at[box(i, phase, side, k, number)]
        return remote(src, dst, send.at[i, phase, side, number], recv.at[i, phase, side, number], moved(at, axis, step))

    sent = {}
    for i in range(n):
        own, copy = firsts[i]
        own.wait()
        copy.wait_recv()

        def both(z, carry, i=i):
            for h in range(2):
                for l in range(2):
                    for x in range(4):
                        add(total[i], (h, z, l, x), other[i], (h, z, l, x))
            return carry
        lax.fori_loop(0, 4, both, 0)
        for number in range(2):
            for side in range(2):
                sent[i, 2, side, number] = go(message(i, 2, side, number))
    for phase in (2, 1, 0):
        for i in range(n):
            axis = orders[i][phase]
            for side in range(2):
                step = 1 if side == 0 else -1
                sent[i, phase, side, 0].wait_recv()
                add(total[i], part(i, phase, moved(at, axis, step), side), landing[i][phase], box(i, phase, side, side, 0))
                sent[i, phase, side, 2] = go(message(i, phase, side, 2))
        for i in range(n):
            for side in range(2):
                for number in (1, 2):
                    sent[i, phase, side, number].wait_recv()
            if phase > 0:
                for side in range(2):
                    add(total[i], part(i, phase, at, 1 - side), landing[i][phase], box(i, phase, side, 1 - side, 1))
                    add(total[i], part(i, phase, at, side), landing[i][phase], box(i, phase, side, side, 2))
                for number in range(2):
                    for side in range(2):
                        sent[i, phase - 1, side, number] = go(message(i, phase - 1, side, number))
            else:
                here = region(at, orders[i], "")[1:]
                def rows_of(k):
                    s = cut(i, k)
                    whole = total[i][here + (s,)].astype(jnp.float32)
                    for side in range(2):
                        whole = whole + landing[i][0][box(i, 0, side, k, 1 if k == 1 - side else 2)].astype(jnp.float32)
                    return whole
                chunk = jnp.concatenate([rows_of(0), rows_of(1)], axis=0).astype(jnp.bfloat16)
                size, take = rows[i], piece[i]
                to_row = lax.broadcasted_iota(jnp.int32, (64, size), 0)
                from_row = lax.broadcasted_iota(jnp.int32, (64, size), 1)
                pick = ((from_row // take) * 16 + from_row % take == to_row).astype(jnp.bfloat16)
                laid = jnp.dot(pick, chunk, preferred_element_type=jnp.float32).astype(jnp.bfloat16)
                spread[i][...] = laid.reshape(4, 16, laid.shape[-1])
                own = pltpu.make_async_copy(spread[i].at[mine], outs[i].at[mine], own_sem.at[i])
                own.start()
                finals = [own]
                for k, to in enumerate(peers):
                    quarter = to["core"] * 2 + to["y"] // 2
                    finals.append(go(remote(spread[i].at[quarter], outs[i].at[mine], msend.at[i, k], mrecv.at[i, k], to)))
                sent[i, "final"] = finals
    for i in range(n):
        own, *copies = sent[i, "final"]
        own.wait()
        for copy in copies:
            copy.wait_recv()
    for copy in started:
        copy.wait_send()


def scatter(parts, piece, orders, cid=2):
    n = len(parts)
    rows = [4 * p for p in piece]
    wide = [p.shape[-1] for p in parts]
    ins = [p.reshape(2, 2, 4, 2, 4, rows[i], wide[i]) for i, p in enumerate(parts)]
    scratch = [pltpu.VMEM((2, 4, 2, 4, rows[i], wide[i]), jnp.bfloat16) for i in range(n)] * 2
    for i in range(n):
        for phase in range(3):
            scratch.append(pltpu.VMEM((2, 3) + half_shape(orders[i], phase) + (rows[i], wide[i]), jnp.bfloat16))
    scratch += [pltpu.VMEM((4, 16, wide[i]), jnp.bfloat16) for i in range(n)]
    dma = pltpu.SemaphoreType.DMA
    scratch += [dma((n,)), dma((n,)), dma((n,)), dma((n, 3, 2, 3)), dma((n, 3, 2, 3)), dma((n, 3)), dma((n, 3))]
    return pl.pallas_call(
        functools.partial(scatter_kernel, n=n, rows=rows, piece=piece, orders=orders),
        out_shape=[jax.ShapeDtypeStruct((4, 16, w), jnp.bfloat16) for w in wide],
        in_specs=[ANY] * n,
        out_specs=[VM] * n,
        scratch_shapes=scratch,
        compiler_params=pltpu.CompilerParams(collective_id=cid, has_side_effects=True, vmem_limit_bytes=56 << 20),
        name="scatter_grads",
    )(*ins)


def unpack(out, piece):
    return out[:, :piece].transpose(1, 0, 2).reshape(piece, -1).astype(jnp.float32)


D = 1536
TOK = 128
TOP = 6
EXPERTS = 64
CAP = 24
SLOTS = EXPERTS * CAP
CHUNK = 384
epsilon = 1e-06
SCALE = 1.0 / math.sqrt(128)
f32, bf16, i32 = jnp.float32, jnp.bfloat16, jnp.int32


def dot(a, b):
    return jnp.dot(a, b, preferred_element_type=f32)


def dot_t(a, b):
    return lax.dot_general(a, b, (((1,), (1,)), ((), ())), preferred_element_type=f32)


def t_dot(a, b):
    return lax.dot_general(a, b, (((0,), (0,)), ((), ())), preferred_element_type=f32)


def flip(a):
    return a.astype(f32).T.astype(bf16)


def rms_scale(v):
    return lax.rsqrt(jnp.mean(v * v, axis=-1, keepdims=True) + epsilon)


def silu_parts(pre):
    s = jax.nn.sigmoid(pre)
    return pre * s, s * (1.0 + pre * (1.0 - s))


def norm_back(grad, source, scale, gain):
    weighted = grad * gain
    inner = jnp.mean(weighted * source, axis=-1, keepdims=True)
    return scale * weighted - source * (scale * scale * scale) * inner


def iota(shape, dim):
    return lax.broadcasted_iota(i32, shape, dim)


def gain_row(misc, lane):
    pick = (iota((16, 128), 1) == lane).astype(bf16)
    return dot_t(pick, misc)[0:1]


def chosen(routes):
    lanes = iota((TOK, 128), 1)
    hit = jnp.zeros((TOK, 128), f32)
    for k in range(TOP):
        hit = hit + (routes[:, k : k + 1] == lanes).astype(f32)
    return hit


def attend_body(tokens, seg, routes, wq, wkv, wo, normed_o, q_o, kv_o, p_o, att_o, resid_o, nt_o, code_o):
    source = tokens[...].astype(f32)
    gain = gain_row(wkv[0, :, 256:], 64)
    normed_o[...] = (source * rms_scale(source) * gain).astype(bf16)
    row = jnp.broadcast_to(seg[...].astype(f32), (TOK, TOK))
    allowed = (row == row.T) & (iota((TOK, TOK), 1) <= iota((TOK, TOK), 0))
    allowed = jnp.concatenate([allowed.astype(f32)] * 3, axis=0)

    def heads(j, carry):
        normed = normed_o[...]
        q = dot(normed, wq[j]).astype(bf16)
        kv = dot(normed, wkv[j, :, :256]).astype(bf16)
        q_o[j] = q
        kv_o[j] = kv
        q3 = jnp.concatenate([q[:, :128], q[:, 128:256], q[:, 256:]], axis=0)
        scores = jnp.where(allowed > 0, dot_t(q3, kv[:, :128]) * SCALE, -1e30)
        expo = jnp.exp(scores - jnp.max(scores, axis=-1, keepdims=True))
        p = expo / jnp.sum(expo, axis=-1, keepdims=True)
        p_o[j] = p
        mixed = dot(p.astype(bf16), kv[:, 128:]).astype(bf16)
        att_o[j] = jnp.concatenate([mixed[:128], mixed[128:256], mixed[256:]], axis=1)
        return carry

    lax.fori_loop(0, 4, heads, 0)
    attended = jnp.concatenate([att_o[j] for j in range(4)], axis=1)
    for j in range(4):
        resid_o[:, j * 384 : (j + 1) * 384] = source[:, j * 384 : (j + 1) * 384] + dot(attended, wo[j])
    resid = resid_o[...]
    nt = (resid * rms_scale(resid) * gain_row(wkv[0, :, 256:], 65)).astype(bf16)
    nt_o[...] = nt
    logits = dot(nt, wkv[0, :, 256:])
    hit = chosen(routes[...])
    earlier = (iota((TOK, TOK), 1) < iota((TOK, TOK), 0)).astype(bf16)
    code_o[0] = hit * (dot(earlier, hit.astype(bf16)) + 1.0)
    masked = jnp.where(hit > 0, logits, -1e30)
    expo = jnp.where(hit > 0, jnp.exp(masked - jnp.max(masked, axis=-1, keepdims=True)), 0.0)
    code_o[1] = expo / jnp.sum(expo, axis=-1, keepdims=True)


def back_body(gnt, resid_r, cot, tokens, normed_r, q_r, kv_r, p_r, att_r, wq, wkv, wo, misc_in, gtok_o, gwq_o, gwkv_o, gwo_o, gq_s, gkv_s, goo_s, gatt_s, nt_s):
    total = gnt[...]
    resid = resid_r[...]
    scale = rms_scale(resid)
    z_two = (total * resid * scale).astype(bf16)
    grad_resid = cot[...].astype(f32) + norm_back(total, resid, scale, gain_row(wkv[0, :, 256:], 65))
    goo_s[...] = grad_resid.astype(bf16)
    att_t = flip(jnp.concatenate([att_r[j] for j in range(4)], axis=1))
    gatt = jnp.zeros((TOK, D), f32)
    for j in range(4):
        cols = slice(j * 384, (j + 1) * 384)
        gatt = gatt + dot_t(goo_s[:, cols], wo[j])
        gwo_o[j] = dot(att_t, goo_s[:, cols]).astype(bf16)
    for j in range(4):
        gatt_s[j] = gatt[:, j * 384 : (j + 1) * 384].astype(bf16)

    def heads(j, carry):
        ga, q, kv, p = gatt_s[j], q_r[j], kv_r[j], p_r[j]
        ga3 = jnp.concatenate([ga[:, :128], ga[:, 128:256], ga[:, 256:]], axis=0)
        q3 = jnp.concatenate([q[:, :128], q[:, 128:256], q[:, 256:]], axis=0)
        gp = dot_t(ga3, kv[:, 128:])
        gs = (p * (gp - jnp.sum(p * gp, axis=-1, keepdims=True))).astype(bf16)
        gq3 = (dot(gs, kv[:, :128]) * SCALE).astype(bf16)
        gk = (t_dot(gs, q3) * SCALE).astype(bf16)
        gv = t_dot(p.astype(bf16), ga3).astype(bf16)
        gq_s[j] = jnp.concatenate([gq3[:128], gq3[128:256], gq3[256:]], axis=1)
        gkv_s[j] = jnp.concatenate([gk, gv], axis=1)
        return carry

    lax.fori_loop(0, 4, heads, 0)
    nt_s[...] = flip(normed_r[...])
    gn = jnp.zeros((TOK, D), f32)
    for j in range(4):
        gn = gn + dot_t(gq_s[j], wq[j]) + dot_t(gkv_s[j], wkv[j, :, :256])
        gwq_o[j] = dot(nt_s[...], gq_s[j]).astype(bf16)
        gwkv_o[j, :, :256] = dot(nt_s[...], gkv_s[j]).astype(bf16)
        if j:
            gwkv_o[j, :, 256:] = jnp.zeros((D, 128), bf16)
    source = tokens[...].astype(f32)
    scale = rms_scale(source)
    z_one = (gn * source * scale).astype(bf16)
    gtok_o[...] = grad_resid + norm_back(gn, source, scale, gain_row(wkv[0, :, 256:], 64))
    lane = iota((TOK, 128), 1)
    gwkv_o[0, :, 256:] = (misc_in[...] + t_dot(z_one, (lane == 64).astype(bf16)) + t_dot(z_two, (lane == 65).astype(bf16))).astype(bf16)


def sds(shape, dtype=bf16):
    return jax.ShapeDtypeStruct(shape, dtype)


def whole(body, outs, scratch=(), name=None):
    def call(*args):
        return pl.pallas_call(
            body,
            out_shape=outs,
            in_specs=[pl.BlockSpec(memory_space=pltpu.VMEM)] * len(args),
            out_specs=[pl.BlockSpec(memory_space=pltpu.VMEM)] * len(outs),
            scratch_shapes=[pltpu.VMEM(s.shape, s.dtype) for s in scratch],
            compiler_params=pltpu.CompilerParams(vmem_limit_bytes=60 << 20),
            name=name,
        )(*args)

    return call


attend = whole(
    attend_body,
    [sds((TOK, D)), sds((4, TOK, 384)), sds((4, TOK, 256)), sds((4, 384, TOK), f32), sds((4, TOK, 384)), sds((TOK, D), f32), sds((TOK, D)), sds((2, TOK, 128), f32)],
    name="attend",
)
back = whole(
    back_body,
    [sds((TOK, D), f32), sds((4, D, 384)), sds((4, D, 384)), sds((4, D, 384))],
    [sds((4, TOK, 384)), sds((4, TOK, 256)), sds((TOK, D)), sds((4, TOK, 384)), sds((D, TOK))],
    name="back",
)


STRIDE = 11
PEERS = 32
BLOCK = 2 * CAP
GROUP = CHUNK // BLOCK


def shift_of(s):
    t = (s * STRIDE) % PEERS
    return t // 8, (t // 2) % 4, t % 2


def shifted(at, s, sign):
    dz, dx, dc = shift_of(s)
    return {
        **at,
        "z": (at["z"] + sign * dz + 4) % 4,
        "x": (at["x"] + sign * dx + 4) % 4,
        "core": (at["core"] + dc) % 2,
    }


def moe_kernel(
    nt_h, cot_h, code_r, resid_h, router_r, gm, um, dm, sg_h, su_h, sd_h,
    out_r, gnt_r, misc_r, gg_o, gu_o, gd_o, gsg_h, gsu_h, gsd_h,
    nt2, cot2, code2, hits, gated, owner, out_n, out_g, arr_n, arr_g, ret_m, ret_b,
    gx, ux, dx, hid, act_s, slope_s, acc, grecv_a, grecv_b, part_s, part_r, pick_s, pick_r,
    sg_v, su_v, sd_v, shid, ntt, stage,
    pair_send, pair_recv, rep_send, rep_recv, n_send, n_recv, g_send, g_recv, m_send, m_recv, b_send, b_recv, self_sem, load_sem, store_sem,
):
    at = place()
    partner = {**at, "y": at["y"] + 1 - 2 * (at["y"] % 2)}
    twin = moved(at, "y", 2)
    barrier = pltpu.get_barrier_semaphore()
    for to in (partner, twin):
        pl.semaphore_signal(barrier, inc=1, device_id=device(to), device_id_type=MESH)

    def hello(s, carry):
        pl.semaphore_signal(barrier, inc=1, device_id=device(shifted(at, s, 1)), device_id_type=MESH)
        return carry

    lax.fori_loop(1, PEERS, hello, 0)
    pl.semaphore_wait(barrier, PEERS + 1)

    def remote(src, dst, s, r, to):
        return pltpu.make_async_remote_copy(src_ref=src, dst_ref=dst, send_sem=s, recv_sem=r, device_id=device(to), device_id_type=MESH)

    started = []

    def go(copy):
        copy.start()
        started.append(copy)
        return copy

    nt_r, cot = nt2.at[0], cot2.at[0]
    first = [pltpu.make_async_copy(nt_h, nt_r, load_sem.at[5]), pltpu.make_async_copy(cot_h, cot, load_sem.at[6])]
    for copy in first:
        copy.start()
    pair = [go(remote(src, dst, pair_send.at[k], pair_recv.at[k], partner)) for k, (src, dst) in enumerate(((nt_h, nt2.at[1]), (code_r, code2), (cot_h, cot2.at[1])))]
    swaps = [go(remote(src, dst, rep_send.at[k], rep_recv.at[k], twin)) for k, (src, dst) in enumerate(((gm, gx), (um, ux), (dm, dx)))]

    def load(src, dst, k):
        copy = pltpu.make_async_copy(src, dst, load_sem.at[k])
        copy.start()
        return copy

    sd_copy = load(sd_h, sd_v, 4)
    loads = {}
    for j in range(2):
        loads[j] = (load(sg_h.at[j], sg_v.at[j], j), load(su_h.at[j], su_v.at[j], 2 + j))
    lane = iota((1, SLOTS), 1)
    block, spot = lane // BLOCK, lane % BLOCK
    there = shifted(at, block, 1)
    expert = ((there["z"] * 2 + at["y"] % 2) * 4 + there["x"]) * 2 + there["core"]
    owner[...] = (iota((128, SLOTS), 0) == expert).astype(bf16)
    for copy in first:
        copy.wait()
    ntt[...] = flip(nt_r[...])

    def fill(k, code, gates):
        wide = dot(code.astype(bf16), owner[...])
        hit = (wide == (spot - k * CAP + 1).astype(f32)) & (wide > 0)
        rows = slice(k * TOK, (k + 1) * TOK)
        hits[rows] = hit.astype(f32).astype(bf16)
        gated[rows] = jnp.where(hit, dot(gates.astype(bf16), owner[...]), 0.0).astype(bf16)

    fill(0, code_r[0], code_r[1])
    for copy in pair[:2]:
        copy.wait_recv()
    fill(1, code2[0], code2[1])

    def send_rows(box, land, c, ssem, rsem, sign):
        def one(s, carry):
            remote(box.at[s], land.at[s], ssem.at[s], rsem.at[s], shifted(at, s, sign)).start()
            return carry
        if c == 0:
            pltpu.make_async_copy(box.at[0], land.at[0], self_sem).start()
        lax.fori_loop(max(1, c * GROUP), (c + 1) * GROUP, one, 0)

    def wait_rows(box, land, c, ssem, rsem, sign, sent):
        def one(s, carry):
            copy = remote(box.at[s], land.at[s], ssem.at[s], rsem.at[s], shifted(at, s, sign))
            if sent:
                copy.wait_send()
            else:
                copy.wait_recv()
            return carry
        if c == 0 and not sent:
            pltpu.make_async_copy(box.at[0], land.at[0], self_sem).wait()
        lax.fori_loop(max(1, c * GROUP), (c + 1) * GROUP, one, 0)

    chunks = range(SLOTS // CHUNK)

    def lanes_of(c):
        return slice(c * CHUNK, (c + 1) * CHUNK)

    def blocks_of(c):
        return slice(c * GROUP, (c + 1) * GROUP)

    for c in chunks:
        rows = t_dot(hits[:, lanes_of(c)], nt2[...].reshape(2 * TOK, D))
        out_n[blocks_of(c)] = rows.astype(bf16).reshape(GROUP, BLOCK, D)
        send_rows(out_n, arr_n, c, n_send, n_recv, 1)
    wait_rows(out_n, arr_n, 0, n_send, n_recv, 1, False)
    pair[2].wait_recv()
    for c in chunks:
        rows = t_dot(gated[:, lanes_of(c)], cot2[...].reshape(2 * TOK, D))
        out_g[blocks_of(c)] = rows.astype(bf16).reshape(GROUP, BLOCK, D)
        send_rows(out_g, arr_g, c, g_send, g_recv, 1)

    sd_copy.wait()
    gh = jnp.zeros((TOK, 1024), f32)
    for j in range(4):
        gh = gh + dot_t(cot[:, j * 384 : (j + 1) * 384], sd_v[j])
    stores = []

    def store(k, value, dst):
        while len(stores) >= 2:
            stores.pop(0).wait()
        stage[k % 2] = value.astype(bf16)
        copy = pltpu.make_async_copy(stage.at[k % 2], dst, store_sem.at[k % 2])
        copy.start()
        stores.append(copy)

    acc[...] = jnp.zeros((2 * TOK, D), f32)
    for j in range(4):
        for copy in loads[j]:
            copy.wait()
        cols = slice(j * 256, (j + 1) * 256)
        gate, up = dot(nt_r[...], sg_v[j % 2]), dot(nt_r[...], su_v[j % 2])
        act, slope = silu_parts(gate)
        shid[:, cols] = (act * up).astype(bf16)
        dgate = (gh[:, cols] * up * slope).astype(bf16)
        dup = (gh[:, cols] * act).astype(bf16)
        acc[:TOK] += dot_t(dgate, sg_v[j % 2]) + dot_t(dup, su_v[j % 2])
        if j < 2:
            loads[j + 2] = (load(sg_h.at[j + 2], sg_v.at[j], j), load(su_h.at[j + 2], su_v.at[j], 2 + j))
        store(2 * j, dot(ntt[...], dgate), gsg_h.at[j])
        store(2 * j + 1, dot(ntt[...], dup), gsu_h.at[j])
    gnt_r[...] = acc[:TOK]
    resid_copy = load(resid_h, acc.at[pl.ds(0, TOK)], 5)
    for copy in stores:
        copy.wait()
    stores.clear()
    shid_t = flip(shid[...])
    finals = []
    resid_copy.wait()
    for j in range(4):
        cols = slice(j * 384, (j + 1) * 384)
        acc[:TOK, cols] += dot(shid[...], sd_v[j])
    acc[TOK:] = jnp.zeros((TOK, D), f32)
    for j in range(4):
        sd_v[j] = dot(shid_t, cot[:, j * 384 : (j + 1) * 384]).astype(bf16)
        copy = pltpu.make_async_copy(sd_v.at[j], gsd_h.at[j], load_sem.at[j])
        copy.start()
        finals.append(copy)

    for copy in swaps:
        copy.wait_recv()
    halves = ((gm, um, dm), (gx, ux, dx))
    for c in chunks:
        if c:
            wait_rows(out_n, arr_n, c, n_send, n_recv, 1, False)
        x = arr_n[blocks_of(c)].reshape(CHUNK, D)
        total = None
        for k, (g, u, d) in enumerate(halves):
            cols = slice(k * 256, (k + 1) * 256)
            gate, up = dot(x, g[...]), dot(x, u[...])
            act, slope = silu_parts(gate)
            hidden = (act * up).astype(bf16)
            hid[lanes_of(c), cols] = hidden
            act_s[lanes_of(c), cols] = act.astype(bf16)
            slope_s[lanes_of(c), cols] = (up * slope).astype(bf16)
            part = dot(hidden, d[...])
            total = part if total is None else total + part
        wait_rows(out_n, arr_n, c, n_send, n_recv, 1, True)
        out_n[blocks_of(c)] = total.astype(bf16).reshape(GROUP, BLOCK, D)
        send_rows(out_n, ret_m, c, m_send, m_recv, -1)
    wait_rows(out_n, ret_m, 0, m_send, m_recv, -1, False)
    send_self = None
    for c in chunks:
        wait_rows(out_g, arr_g, c, g_send, g_recv, 1, False)
        slot = arr_g[blocks_of(c)].reshape(CHUNK, D)
        total = None
        for k, (g, u, d) in enumerate(halves):
            cols = slice(k * 256, (k + 1) * 256)
            gh = dot_t(slot, d[...])
            dgate = (gh * slope_s[lanes_of(c), cols].astype(f32)).astype(bf16)
            dup = (gh * act_s[lanes_of(c), cols].astype(f32)).astype(bf16)
            slope_s[lanes_of(c), cols], act_s[lanes_of(c), cols] = dgate, dup
            part = dot_t(dgate, g[...]) + dot_t(dup, u[...])
            total = part if total is None else total + part
        wait_rows(out_g, arr_g, c, g_send, g_recv, 1, True)
        out_g[blocks_of(c)] = total.astype(bf16).reshape(GROUP, BLOCK, D)
        send_rows(out_g, ret_b, c, b_send, b_recv, -1)
    for b in range(4):
        cols = slice(b * 384, (b + 1) * 384)
        xt = flip(jnp.concatenate([arr_n[blocks_of(c), :, cols].reshape(CHUNK, 384) for c in chunks], axis=0))
        gg = dot(xt, slope_s[...])
        gu = dot(xt, act_s[...])
        gg_o[cols], gu_o[cols] = gg[:, :256], gu[:, :256]
        sg_v[0, cols], sg_v[1, cols] = gg[:, 256:].astype(bf16), gu[:, 256:].astype(bf16)
    trade = [go(remote(sg_v, grecv_a, rep_send.at[3], rep_recv.at[3], twin))]
    for copy in finals:
        copy.wait()
    hid_t = flip(hid[...])
    for b in range(4):
        cols = slice(b * 384, (b + 1) * 384)
        gd = dot(hid_t, jnp.concatenate([arr_g[blocks_of(c), :, cols].reshape(CHUNK, 384) for c in chunks], axis=0))
        gd_o[:, cols] = gd[:256]
        sd_v[0, b * 256 : (b + 1) * 256] = gd[256:].astype(bf16)
    trade.append(go(remote(sd_v.at[0], grecv_b, rep_send.at[4], rep_recv.at[4], twin)))

    picked = jnp.zeros((2 * TOK, 128), f32)
    for c in chunks:
        if c:
            wait_rows(out_n, ret_m, c, m_send, m_recv, -1, False)
        rows = ret_m[blocks_of(c)].reshape(CHUNK, D)
        acc[...] += dot(gated[:, lanes_of(c)], rows)
        grads = dot_t(cot2[...].reshape(2 * TOK, D), rows) * hits[:, lanes_of(c)].astype(f32)
        high = grads.astype(bf16)
        low = (grads - high.astype(f32)).astype(bf16)
        own = owner[:, lanes_of(c)]
        picked = picked + dot_t(high, own) + dot_t(low, own)
    part_s[0] = acc[TOK:].astype(bf16)
    pick_s[...] = picked[TOK:]
    pair.append(go(remote(part_s.at[0], part_r.at[0], pair_send.at[3], pair_recv.at[3], partner)))
    pair.append(go(remote(pick_s, pick_r, pair_send.at[4], pair_recv.at[4], partner)))
    pair[3].wait_recv()
    out_r[...] = (acc[:TOK] + part_r[0].astype(f32)).astype(bf16)
    pair[4].wait_recv()
    picked = picked[:TOK] + pick_r[...]
    gates = code_r[1]
    mean = jnp.sum(gates * picked, axis=-1, keepdims=True)
    gl = (gates * (picked - mean)).astype(bf16)
    misc_r[...] = dot(ntt[...], gl)
    acc[:TOK] = gnt_r[...] + dot_t(gl, router_r[...])
    acc[TOK:] = jnp.zeros((TOK, D), f32)
    for c in chunks:
        wait_rows(out_g, ret_b, c, b_send, b_recv, -1, False)
        acc[...] += dot(hits[:, lanes_of(c)], ret_b[blocks_of(c)].reshape(CHUNK, D))
    part_s[1] = acc[TOK:].astype(bf16)
    pair.append(go(remote(part_s.at[1], part_r.at[1], pair_send.at[5], pair_recv.at[5], partner)))
    trade[0].wait_recv()
    gg_o[...] += grecv_a[0].astype(f32)
    gu_o[...] += grecv_a[1].astype(f32)
    trade[1].wait_recv()
    for b in range(4):
        gd_o[:, b * 384 : (b + 1) * 384] += grecv_b[b * 256 : (b + 1) * 256].astype(f32)
    pair[5].wait_recv()
    gnt_r[...] = acc[:TOK] + part_r[1].astype(f32)
    for c in chunks:
        wait_rows(out_n, ret_m, c, m_send, m_recv, -1, True)
        wait_rows(out_g, ret_b, c, b_send, b_recv, -1, True)
    for copy in started:
        copy.wait_send()


def moe(nt, cot, code, resid, router, mine, sg, su, sd):
    dma = pltpu.SemaphoreType.DMA
    vm = lambda shape, dtype=bf16: pltpu.VMEM(shape, dtype)
    rows = (PEERS, BLOCK, D)
    return pl.pallas_call(
        moe_kernel,
        out_shape=[sds((TOK, D)), sds((TOK, D), f32), sds((D, 128), f32), sds((D, 256), f32), sds((D, 256), f32), sds((256, D), f32), sds((4, D, 256)), sds((4, D, 256)), sds((4, 1024, 384))],
        in_specs=[ANY, ANY, VM, ANY, VM, VM, VM, VM, ANY, ANY, ANY],
        out_specs=[VM] * 6 + [ANY] * 3,
        scratch_shapes=[vm((2, TOK, D)), vm((2, TOK, D)), vm((2, TOK, 128), f32), vm((2 * TOK, SLOTS)), vm((2 * TOK, SLOTS)), vm((128, SLOTS))]
        + [vm(rows)] * 6
        + [vm((D, 256)), vm((D, 256)), vm((256, D)), vm((SLOTS, 512)), vm((SLOTS, 512)), vm((SLOTS, 512)), vm((2 * TOK, D), f32)]
        + [vm((2, D, 256)), vm((1024, 384)), vm((2, TOK, D)), vm((2, TOK, D)), vm((TOK, 128), f32), vm((TOK, 128), f32)]
        + [vm((2, D, 256)), vm((2, D, 256)), vm((4, 1024, 384)), vm((TOK, 1024)), vm((D, TOK)), vm((2, D, 256))]
        + [dma((6,)), dma((6,)), dma((5,)), dma((5,))] + [dma((PEERS,))] * 8 + [dma, dma((7,)), dma((2,))],
        compiler_params=pltpu.CompilerParams(collective_id=3, has_side_effects=True, vmem_limit_bytes=63 << 20),
        name="moe",
    )(nt, cot, code, resid, router, *mine, sg, su, sd)


def local(tokens, segment_ids, routes, cotangent, query_weight, key_weight, value_weight, output_weight, shared_gate, shared_up, shared_down, router_weight, first_gain, second_gain, expert_gate, expert_up, expert_down):
    misc = jnp.concatenate([router_weight, first_gain[:, None], second_gain[:, None], jnp.zeros((12, 62), bf16)], axis=1)
    kvm = jnp.concatenate([key_weight.reshape(12, 4, 128), value_weight.reshape(12, 4, 128), jnp.broadcast_to(misc[:, None], (12, 4, 128))], axis=2)
    wq, wo, wkv, sg, su, sd = gather(
        [pack(query_weight, 12), pack(output_weight, 12), pack(kvm.reshape(12, D), 12), pack(shared_gate, 12), pack(shared_up, 12), pack(shared_down, 8)], PIECE)
    normed, q, kv, p, att, resid, nt, code = attend(tokens, segment_ids, routes, wq, wkv, wo)
    mine = [expert_gate[0], expert_up[0], expert_down[0]]
    block_out, gnt, gmisc, gg, gu, gd, *shared_grads = moe(nt, cotangent, code, resid, wkv[0, :, 256:], mine, sg, su, sd)
    gtok, gwq, gwkv, gwo = back(gnt, resid, cotangent, tokens, normed, q, kv, p, att, wq, wkv, wo, gmisc)
    shared_pieces = scatter(shared_grads, PIECE[3:], ORDERS[3:], cid=2)
    pq, po, pkv = scatter([gwq, gwo, gwkv], PIECE[:3], ORDERS[:3], cid=4)
    pm = pkv[0, :12, 256:].astype(f32)
    return (
        block_out,
        gtok,
        unpack(pq, 12),
        unpack(pkv[:, :, :128], 12),
        unpack(pkv[:, :, 128:256], 12),
        unpack(po, 12),
        unpack(shared_pieces[0], 12),
        unpack(shared_pieces[1], 12),
        unpack(shared_pieces[2], 8),
        pm[:, :64],
        pm[:, 64],
        pm[:, 65],
        gg[None],
        gu[None],
        gd[None],
    )


def solution(mesh):
    in_specs = (
        P(("fsdp", "rep"), None),
        P(("fsdp", "rep"), None),
        P(("fsdp", "rep"), None),
        P(("fsdp", "rep"), None),
        P(("fsdp", "rep"), None),
        P(("fsdp", "rep"), None),
        P(("fsdp", "rep"), None),
        P(("fsdp", "rep"), None),
        P(("fsdp", "rep"), None),
        P(("fsdp", "rep"), None),
        P(("fsdp", "rep"), None),
        P(("fsdp", "rep"), None),
        P(("fsdp", "rep")),
        P(("fsdp", "rep")),
        P("fsdp", None, "rep"),
        P("fsdp", None, "rep"),
        P("fsdp", "rep", None),
    )
    out_specs = (
        P(("fsdp", "rep"), None),
        P(("fsdp", "rep"), None),
        P(("fsdp", "rep"), None),
        P(("fsdp", "rep"), None),
        P(("fsdp", "rep"), None),
        P(("fsdp", "rep"), None),
        P(("fsdp", "rep"), None),
        P(("fsdp", "rep"), None),
        P(("fsdp", "rep"), None),
        P(("fsdp", "rep"), None),
        P(("fsdp", "rep")),
        P(("fsdp", "rep")),
        P("fsdp", None, "rep"),
        P("fsdp", None, "rep"),
        P("fsdp", "rep", None),
    )
    return jax.shard_map(local, mesh=mesh, in_specs=in_specs, out_specs=out_specs, check_vma=False)
```

```python
import math

import jax
import jax.numpy as jnp
from jax import lax
from jax.experimental import pallas as pl
from jax.experimental.pallas import tpu as pltpu
from jax.sharding import PartitionSpec as P

MESH = pl.DeviceIdType.MESH
ANY = pl.BlockSpec(memory_space=pl.ANY)
VM = pl.BlockSpec(memory_space=pltpu.VMEM)


def place():
    f, r = lax.axis_index("fsdp"), lax.axis_index("rep")
    return dict(x=(f // 2) % 4, y=2 * r + (f // 8) % 2, z=f // 16, core=f % 2)


def device(at):
    return (((at["z"] * 2 + at["y"] % 2) * 4 + at["x"]) * 2 + at["core"], at["y"] // 2)


def moved(at, axis, by):
    return {**at, axis: (at[axis] + by) % (2 if axis == "core" else 4)}


def region(at, order, done, coordinate=None, half=None):
    first = done[0] if done else None
    spot = {}
    for axis in "xyz":
        whole = axis in done
        at_axis = at[axis]
        if axis == "y":
            if whole:
                spot["yhi"] = (half if (half is not None and first == "y") else slice(None))
                spot["ylo"] = slice(None)
            else:
                spot["yhi"], spot["ylo"] = at_axis // 2, at_axis % 2
        else:
            if whole:
                spot[axis] = pl.ds(2 * half, 2) if (half is not None and first == axis) else slice(None)
            else:
                spot[axis] = at_axis
    return (at["core"], spot["yhi"], spot["z"], spot["ylo"], spot["x"])


D = 1536
TOK = 128
TOP = 6
EXPERTS = 64
CAP = 24
SLOTS = EXPERTS * CAP
CHUNK = 384
epsilon = 1e-06
SCALE = 1.0 / math.sqrt(128)
f32, bf16, i32 = jnp.float32, jnp.bfloat16, jnp.int32


def dot(a, b):
    return jnp.dot(a, b, preferred_element_type=f32)


def dot_t(a, b):
    return lax.dot_general(a, b, (((1,), (1,)), ((), ())), preferred_element_type=f32)


def t_dot(a, b):
    return lax.dot_general(a, b, (((0,), (0,)), ((), ())), preferred_element_type=f32)


def flip(a):
    return a.astype(f32).T.astype(bf16)


def rms_scale(v):
    return lax.rsqrt(jnp.mean(v * v, axis=-1, keepdims=True) + epsilon)


def silu_parts(pre):
    s = jax.nn.sigmoid(pre)
    return pre * s, s * (1.0 + pre * (1.0 - s))


def norm_back(grad, source, scale, gain):
    weighted = grad * gain
    inner = jnp.mean(weighted * source, axis=-1, keepdims=True)
    return scale * weighted - source * (scale * scale * scale) * inner


def iota(shape, dim):
    return lax.broadcasted_iota(i32, shape, dim)


def gain_row(misc, lane):
    pick = (iota((16, 128), 1) == lane).astype(bf16)
    return dot_t(pick, misc)[0:1]


def chosen(routes):
    lanes = iota((TOK, 128), 1)
    hit = jnp.zeros((TOK, 128), f32)
    for k in range(TOP):
        hit = hit + (routes[:, k : k + 1] == lanes).astype(f32)
    return hit


def sds(shape, dtype=bf16):
    return jax.ShapeDtypeStruct(shape, dtype)


ORDERS = ("xyz", "yzx", "zxy") * 3
PIECE = (12, 12, 12, 12, 12, 12, 12, 12, 8)
WIDE = (256, 256, 256, 128, 128, 128, 256, 256, 384)
N = len(ORDERS)
QKV, OUT, SHARED = (0, 1, 2), (3, 4, 5), (6, 7, 8)
STEPS = (1, -1, 2)


def rows_of(i):
    return 4 * PIECE[i]


def core_box(i):
    return (2, 4, 2, 4, rows_of(i), WIDE[i])


def axis_box(axis):
    return (2, 2) if axis == "y" else (4,)


class Links:
    def __init__(self):
        self.at = place()
        self.core = self.at["core"]
        self.mine = self.core * 2 + self.at["y"] // 2
        self.sibling = moved(self.at, "core", 1)
        self.peers = [self.sibling, moved(self.at, "y", 2), moved(self.sibling, "y", 2)]
        self.started, self.sent = [], {}

    def greet(self):
        barrier = pltpu.get_barrier_semaphore()
        ring = [moved(self.at, axis, by) for axis in "xyz" for by in STEPS if (axis, by) != ("y", 2)]
        for to in self.peers + ring:
            pl.semaphore_signal(barrier, inc=1, device_id=device(to), device_id_type=MESH)
        pl.semaphore_wait(barrier, len(self.peers) + len(ring))

    def remote(self, src, dst, s, r, to):
        return pltpu.make_async_remote_copy(src_ref=src, dst_ref=dst, send_sem=s, recv_sem=r, device_id=device(to), device_id_type=MESH)

    def go(self, *args):
        copy = self.remote(*args)
        copy.start()
        self.started.append(copy)
        return copy

    def end(self):
        for copy in self.started:
            copy.wait_send()


class Gather(Links):
    def __init__(self, shards, got, stage, bufs, mix_send, mix_recv, own_sem, send, recv, rsend, rrecv, dsend, drecv):
        super().__init__()
        self.shards, self.got, self.stage, self.bufs = shards, got, stage, bufs
        self.mix_send, self.mix_recv, self.own_sem = mix_send, mix_recv, own_sem
        self.send, self.recv, self.rsend, self.rrecv, self.dsend, self.drecv = send, recv, rsend, rrecv, dsend, drecv

    def here(self, i, done, spot=None, half=None):
        return self.bufs[i].at[region(self.at if spot is None else spot, ORDERS[i], done, half=half)]

    def mix(self, i):
        own = pltpu.make_async_copy(self.shards[i].at[self.mine], self.got[i].at[self.mine], self.own_sem.at[i])
        own.start()
        copies = []
        for k, to in enumerate(self.peers):
            quarter = to["core"] * 2 + to["y"] // 2
            copies.append(self.go(self.shards[i].at[quarter], self.got[i].at[self.mine], self.mix_send.at[i, k], self.mix_recv.at[i, k], to))
        self.sent[i, "mix"] = (own, copies)

    def direct(self, i, phase, src):
        axis, done = ORDERS[i][phase], ORDERS[i][:phase]
        self.sent[i, phase] = [
            self.go(src, self.here(i, done), self.send.at[i, phase, k], self.recv.at[i, phase, k], moved(self.at, axis, by))
            for k, by in enumerate(STEPS)
        ]

    def enter(self, i):
        own, copies = self.sent[i, "mix"]
        own.wait()
        for copy in copies:
            copy.wait_recv()
        size, take = rows_of(i), PIECE[i]
        to_row, from_row = iota((size, 64), 0), iota((size, 64), 1)
        pick = ((to_row // take) * 16 + to_row % take == from_row).astype(bf16)
        self.stage[i][...] = dot(pick, self.got[i][...].reshape(64, WIDE[i])).astype(bf16)
        local = pltpu.make_async_copy(self.stage[i], self.here(i, ""), self.own_sem.at[i])
        local.start()
        self.sent[i, "own"] = local
        self.direct(i, 0, self.stage[i])

    def second(self, i):
        self.sent[i, "own"].wait()
        for copy in self.sent[i, 0]:
            copy.wait_recv()
        self.direct(i, 1, self.here(i, ORDERS[i][:1]))

    def third(self, i):
        for copy in self.sent[i, 1]:
            copy.wait_recv()
        axis, done = ORDERS[i][2], ORDERS[i][:2]
        src = self.here(i, done)
        self.sent[i, 2] = [self.go(src, src, self.rsend.at[i, k], self.rrecv.at[i, k], moved(self.at, axis, STEPS[k])) for k in range(2)]
        self.go(src, src, self.dsend.at[i, 3], self.drecv.at[i, 3], self.sibling)

    def relay(self, i):
        axis, done = ORDERS[i][2], ORDERS[i][:2]
        halves = []
        for k in range(2):
            self.sent[i, 2][k].wait_recv()
            block = moved(self.at, axis, -STEPS[k])
            part = self.here(i, done, block, half=k)
            halves.append(self.go(part, part, self.rsend.at[i, 2 + k], self.rrecv.at[i, 2 + k], moved(self.at, axis, STEPS[k])))
            whole = self.here(i, done, block)
            self.go(whole, whole, self.dsend.at[i, k], self.drecv.at[i, k], self.sibling)
        self.sent[i, "far"] = halves

    def far(self, i):
        for copy in self.sent[i, "far"]:
            copy.wait_recv()
        whole = self.here(i, ORDERS[i][:2], moved(self.at, ORDERS[i][2], 2))
        self.go(whole, whole, self.dsend.at[i, 2], self.drecv.at[i, 2], self.sibling)

    def done(self, i):
        axis, done = ORDERS[i][2], ORDERS[i][:2]
        for k, by in ((3, 0), (0, -1), (1, 1), (2, 2)):
            where = self.here(i, done, moved(moved(self.at, axis, by) if by else self.at, "core", 1))
            self.remote(where, where, self.dsend.at[i, k], self.drecv.at[i, k], self.sibling).wait_recv()


def front_kernel(*refs):
    tokens, seg, routes, w_query, w_key, w_value, w_output, w_router, gain_one, gain_two = refs[:10]
    normed_o, q_o, kv_o, p_o, att_o, resid_o, nt_o, code_o, misc_o = refs[13:22]
    outs = refs[22:31]
    shards, got, stage = refs[31:40], refs[40:49], refs[49:58]
    held = refs[58:64]
    out_sem, *sems = refs[64:]
    zero = jnp.zeros((4, 16, 384), bf16)
    for shard in shards:
        shard[...] = zero[:, :, : shard.shape[2]]
    eye = iota((12, 12), 0) == iota((12, 12), 1)
    router = w_router[...]
    for j in range(4):
        for p in range(3):
            at_lane = j * 384 + p * 128
            block = w_query[:, at_lane : at_lane + 128]
            if p < 2:
                shards[0][j, :12, p * 128 : (p + 1) * 128] = block
            else:
                shards[1][j, :12, :128] = block
            shards[3 + p][j, :12] = w_output[:, at_lane : at_lane + 128]
        shards[1][j, :12, 128:] = w_key[:, j * 128 : (j + 1) * 128]
        shards[2][j, :12, :128] = w_value[:, j * 128 : (j + 1) * 128]
        shards[2][j, :12, 128:192] = router
        for k, gain in enumerate((gain_one, gain_two)):
            column = jnp.sum(jnp.where(eye, gain[...].astype(f32), 0.0), axis=1, keepdims=True)
            shards[2][j, :12, 192 + k : 193 + k] = column.astype(bf16)
        for i, weight in zip(SHARED, refs[10:13]):
            shards[i][j, : PIECE[i]] = weight[:, j * WIDE[i] : (j + 1) * WIDE[i]]
    g = Gather(shards, got, stage, list(held) + list(outs[6:]), *sems)
    g.greet()
    for i in range(N):
        g.mix(i)
    source = tokens[...].astype(f32)
    row = jnp.broadcast_to(seg[...].astype(f32), (TOK, TOK))
    allowed = (row == row.T) & (iota((TOK, TOK), 1) <= iota((TOK, TOK), 0))
    allowed = jnp.concatenate([allowed.astype(f32)] * 3, axis=0)
    hit = jnp.zeros((TOK, TOK), f32)
    for k in range(TOP):
        hit = hit + (routes[k : k + 1] == iota((TOK, TOK), 0)).astype(f32)
    hit = hit.T
    earlier = (iota((TOK, TOK), 1) < iota((TOK, TOK), 0)).astype(bf16)
    code_o[0] = hit * (dot(earlier, hit.astype(bf16)) + 1.0)
    scaled = source * rms_scale(source)
    for group in (QKV, OUT):
        for i in group:
            g.enter(i)
    for i in QKV:
        g.second(i)
    for i in QKV:
        g.third(i)
    for i in OUT:
        g.second(i)
    for i in QKV:
        g.relay(i)
    for i in OUT:
        g.third(i)
    for i in SHARED:
        g.enter(i)
    for i in QKV:
        g.far(i)
    for i in OUT:
        g.relay(i)
    for i in SHARED:
        g.second(i)
    for i in QKV:
        g.done(i)
    keeps = []

    def weight(i, j):
        return held[i][j // 2, j % 2].reshape(D, WIDE[i])

    def keep(i):
        copy = pltpu.make_async_copy(held[i], outs[i], out_sem.at[i])
        copy.start()
        keeps.append(copy)

    normed_o[...] = (scaled * gain_row(weight(2, 0)[:, 128:], 64)).astype(bf16)
    for i in OUT:
        g.far(i)
    for j in range(4):
        normed = normed_o[...]
        q01 = dot(normed, weight(0, j)).astype(bf16)
        q2k = dot(normed, weight(1, j)).astype(bf16)
        v = dot(normed, weight(2, j)[:, :128]).astype(bf16)
        q_o[j] = jnp.concatenate([q01, q2k[:, :128]], axis=1)
        kv_o[j] = jnp.concatenate([q2k[:, 128:], v], axis=1)
        q3 = jnp.concatenate([q01[:, :128], q01[:, 128:], q2k[:, :128]], axis=0)
        scores = jnp.where(allowed > 0, dot_t(q3, q2k[:, 128:]) * SCALE, -1e30)
        expo = jnp.exp(scores - jnp.max(scores, axis=-1, keepdims=True))
        p = expo / jnp.sum(expo, axis=-1, keepdims=True)
        p_o[j] = p
        mixed = dot(p.astype(bf16), v).astype(bf16)
        att_o[j] = jnp.concatenate([mixed[:128], mixed[128:256], mixed[256:]], axis=1)
        if j == 0:
            for i in SHARED:
                g.third(i)
        if j == 2:
            for i in SHARED:
                g.relay(i)
    for i in QKV:
        keep(i)
    for i in OUT:
        g.done(i)
    attended = jnp.concatenate([att_o[j] for j in range(4)], axis=1)
    for j in range(4):
        for p in range(3):
            cols = slice(j * 384 + p * 128, j * 384 + (p + 1) * 128)
            resid_o[:, cols] = source[:, cols] + dot(attended, weight(3 + p, j))
    for i in OUT:
        keep(i)
    resid = resid_o[...]
    misc = weight(2, 0)[:, 128:]
    misc_o[...] = misc
    nt = (resid * rms_scale(resid) * gain_row(misc, 65)).astype(bf16)
    nt_o[...] = nt
    logits = dot(nt, misc)
    masked = jnp.where(hit > 0, logits, -1e30)
    expo = jnp.where(hit > 0, jnp.exp(masked - jnp.max(masked, axis=-1, keepdims=True)), 0.0)
    code_o[1] = expo / jnp.sum(expo, axis=-1, keepdims=True)
    for i in SHARED:
        g.far(i)
    for i in SHARED:
        g.done(i)
    for copy in keeps:
        copy.wait()
    g.end()


def front(*args):
    dma = pltpu.SemaphoreType.DMA
    full = lambda i: (2,) + core_box(i)
    res = pl.pallas_call(
        front_kernel,
        out_shape=[sds((TOK, D)), sds((4, TOK, 384)), sds((4, TOK, 256)), sds((4, 384, TOK), f32), sds((4, TOK, 384)), sds((TOK, D), f32), sds((TOK, D)), sds((2, TOK, 128), f32), sds((D, 128))]
        + [sds(full(i)) for i in range(N)],
        in_specs=[VM] * 13,
        out_specs=[VM] * 9 + [ANY] * N,
        scratch_shapes=[pltpu.VMEM((4, 16, WIDE[i]), bf16) for i in range(N)] * 2
        + [pltpu.VMEM((rows_of(i), WIDE[i]), bf16) for i in range(N)]
        + [pltpu.VMEM(full(i), bf16) for i in QKV + OUT]
        + [dma((6,)), dma((N, 3)), dma((N, 3)), dma((N,)), dma((N, 2, 3)), dma((N, 2, 3)), dma((N, 4)), dma((N, 4)), dma((N, 4)), dma((N, 4))],
        compiler_params=pltpu.CompilerParams(collective_id=1, has_side_effects=True, vmem_limit_bytes=60 << 20),
        name="front",
    )(*args)
    return res[:9], [o.reshape(4, 32 * rows_of(i), WIDE[i]) for i, o in enumerate(res[9:])]


STRIDE = 11
PEERS = 32
BLOCK = 2 * CAP
GROUP = CHUNK // BLOCK


def shift_of(s):
    t = (s * STRIDE) % PEERS
    return t // 8, (t // 2) % 4, t % 2


def shifted(at, s, sign):
    dz, dx, dc = shift_of(s)
    return {
        **at,
        "z": (at["z"] + sign * dz + 4) % 4,
        "x": (at["x"] + sign * dx + 4) % 4,
        "core": (at["core"] + dc) % 2,
    }


def moe_kernel(
    nt_h, cot_h, code_r, resid_h, router_r, gm, um, dm, sg_h, su_h, sd_h,
    out_r, gnt_r, misc_r, gg_o, gu_o, gd_o, gsg_h, gsu_h, gsd_h,
    nt2, cot2, code2, hits, gated, owner, out_n, out_g, arr_n, arr_g, ret_m, ret_b,
    gx, ux, dx, hid, act_s, slope_s, acc, grecv_a, grecv_b, part_s, part_r, pick_s, pick_r,
    sg_v, su_v, sd_v, shid, ntt, stage,
    pair_send, pair_recv, rep_send, rep_recv, n_send, n_recv, g_send, g_recv, m_send, m_recv, b_send, b_recv, self_sem, load_sem, store_sem,
):
    at = place()
    partner = {**at, "y": at["y"] + 1 - 2 * (at["y"] % 2)}
    twin = moved(at, "y", 2)
    barrier = pltpu.get_barrier_semaphore()
    for to in (partner, twin):
        pl.semaphore_signal(barrier, inc=1, device_id=device(to), device_id_type=MESH)

    def hello(s, carry):
        pl.semaphore_signal(barrier, inc=1, device_id=device(shifted(at, s, 1)), device_id_type=MESH)
        return carry

    lax.fori_loop(1, PEERS, hello, 0)
    pl.semaphore_wait(barrier, PEERS + 1)

    def remote(src, dst, s, r, to):
        return pltpu.make_async_remote_copy(src_ref=src, dst_ref=dst, send_sem=s, recv_sem=r, device_id=device(to), device_id_type=MESH)

    started = []

    def go(copy):
        copy.start()
        started.append(copy)
        return copy

    nt_r, cot = nt2.at[0], cot2.at[0]
    first = [pltpu.make_async_copy(nt_h, nt_r, load_sem.at[5]), pltpu.make_async_copy(cot_h, cot, load_sem.at[6])]
    for copy in first:
        copy.start()
    pair = [go(remote(src, dst, pair_send.at[k], pair_recv.at[k], partner)) for k, (src, dst) in enumerate(((nt_h, nt2.at[1]), (code_r, code2), (cot_h, cot2.at[1])))]
    swaps = [go(remote(src, dst, rep_send.at[k], rep_recv.at[k], twin)) for k, (src, dst) in enumerate(((gm, gx), (um, ux), (dm, dx)))]

    def load(src, dst, k):
        copy = pltpu.make_async_copy(src, dst, load_sem.at[k])
        copy.start()
        return copy

    sd_copy = load(sd_h, sd_v, 4)
    loads = {}
    for j in range(2):
        loads[j] = (load(sg_h.at[j], sg_v.at[j], j), load(su_h.at[j], su_v.at[j], 2 + j))
    lane = iota((1, SLOTS), 1)
    block, spot = lane // BLOCK, lane % BLOCK
    there = shifted(at, block, 1)
    expert = ((there["z"] * 2 + at["y"] % 2) * 4 + there["x"]) * 2 + there["core"]
    owner[...] = (iota((128, SLOTS), 0) == expert).astype(bf16)
    for copy in first:
        copy.wait()
    ntt[...] = flip(nt_r[...])

    def fill(k, code, gates):
        wide = dot(code.astype(bf16), owner[...])
        hit = (wide == (spot - k * CAP + 1).astype(f32)) & (wide > 0)
        rows = slice(k * TOK, (k + 1) * TOK)
        hits[rows] = hit.astype(f32).astype(bf16)
        gated[rows] = jnp.where(hit, dot(gates.astype(bf16), owner[...]), 0.0).astype(bf16)

    fill(0, code_r[0], code_r[1])
    for copy in pair[:2]:
        copy.wait_recv()
    fill(1, code2[0], code2[1])

    def send_rows(box, land, c, ssem, rsem, sign):
        def one(s, carry):
            remote(box.at[s], land.at[s], ssem.at[s], rsem.at[s], shifted(at, s, sign)).start()
            return carry
        if c == 0:
            pltpu.make_async_copy(box.at[0], land.at[0], self_sem).start()
        lax.fori_loop(max(1, c * GROUP), (c + 1) * GROUP, one, 0)

    def wait_rows(box, land, c, ssem, rsem, sign, sent):
        def one(s, carry):
            copy = remote(box.at[s], land.at[s], ssem.at[s], rsem.at[s], shifted(at, s, sign))
            if sent:
                copy.wait_send()
            else:
                copy.wait_recv()
            return carry
        if c == 0 and not sent:
            pltpu.make_async_copy(box.at[0], land.at[0], self_sem).wait()
        lax.fori_loop(max(1, c * GROUP), (c + 1) * GROUP, one, 0)

    chunks = range(SLOTS // CHUNK)

    def lanes_of(c):
        return slice(c * CHUNK, (c + 1) * CHUNK)

    def blocks_of(c):
        return slice(c * GROUP, (c + 1) * GROUP)

    for c in chunks:
        rows = t_dot(hits[:, lanes_of(c)], nt2[...].reshape(2 * TOK, D))
        out_n[blocks_of(c)] = rows.astype(bf16).reshape(GROUP, BLOCK, D)
        send_rows(out_n, arr_n, c, n_send, n_recv, 1)
    wait_rows(out_n, arr_n, 0, n_send, n_recv, 1, False)
    pair[2].wait_recv()
    for c in chunks:
        rows = t_dot(gated[:, lanes_of(c)], cot2[...].reshape(2 * TOK, D))
        out_g[blocks_of(c)] = rows.astype(bf16).reshape(GROUP, BLOCK, D)
        send_rows(out_g, arr_g, c, g_send, g_recv, 1)

    sd_copy.wait()
    gh = jnp.zeros((TOK, 1024), f32)
    for j in range(4):
        gh = gh + dot_t(cot[:, j * 384 : (j + 1) * 384], sd_v[j])
    stores = []

    def store(k, value, dst):
        while len(stores) >= 2:
            stores.pop(0).wait()
        stage[k % 2] = value.astype(bf16)
        copy = pltpu.make_async_copy(stage.at[k % 2], dst, store_sem.at[k % 2])
        copy.start()
        stores.append(copy)

    acc[...] = jnp.zeros((2 * TOK, D), f32)
    for j in range(4):
        for copy in loads[j]:
            copy.wait()
        cols = slice(j * 256, (j + 1) * 256)
        gate, up = dot(nt_r[...], sg_v[j % 2]), dot(nt_r[...], su_v[j % 2])
        act, slope = silu_parts(gate)
        shid[:, cols] = (act * up).astype(bf16)
        dgate = (gh[:, cols] * up * slope).astype(bf16)
        dup = (gh[:, cols] * act).astype(bf16)
        acc[:TOK] += dot_t(dgate, sg_v[j % 2]) + dot_t(dup, su_v[j % 2])
        if j < 2:
            loads[j + 2] = (load(sg_h.at[j + 2], sg_v.at[j], j), load(su_h.at[j + 2], su_v.at[j], 2 + j))
        store(2 * j, dot(ntt[...], dgate), gsg_h.at[j])
        store(2 * j + 1, dot(ntt[...], dup), gsu_h.at[j])
    gnt_r[...] = acc[:TOK]
    resid_copy = load(resid_h, acc.at[pl.ds(0, TOK)], 5)
    for copy in stores:
        copy.wait()
    stores.clear()
    shid_t = flip(shid[...])
    finals = []
    resid_copy.wait()
    for j in range(4):
        cols = slice(j * 384, (j + 1) * 384)
        acc[:TOK, cols] += dot(shid[...], sd_v[j])
    acc[TOK:] = jnp.zeros((TOK, D), f32)
    for j in range(4):
        sd_v[j] = dot(shid_t, cot[:, j * 384 : (j + 1) * 384]).astype(bf16)
        copy = pltpu.make_async_copy(sd_v.at[j], gsd_h.at[j], load_sem.at[j])
        copy.start()
        finals.append(copy)

    for copy in swaps:
        copy.wait_recv()
    halves = ((gm, um, dm), (gx, ux, dx))
    for c in chunks:
        if c:
            wait_rows(out_n, arr_n, c, n_send, n_recv, 1, False)
        x = arr_n[blocks_of(c)].reshape(CHUNK, D)
        total = None
        for k, (g, u, d) in enumerate(halves):
            cols = slice(k * 256, (k + 1) * 256)
            gate, up = dot(x, g[...]), dot(x, u[...])
            act, slope = silu_parts(gate)
            hidden = (act * up).astype(bf16)
            hid[lanes_of(c), cols] = hidden
            act_s[lanes_of(c), cols] = act.astype(bf16)
            slope_s[lanes_of(c), cols] = (up * slope).astype(bf16)
            part = dot(hidden, d[...])
            total = part if total is None else total + part
        wait_rows(out_n, arr_n, c, n_send, n_recv, 1, True)
        out_n[blocks_of(c)] = total.astype(bf16).reshape(GROUP, BLOCK, D)
        send_rows(out_n, ret_m, c, m_send, m_recv, -1)
    wait_rows(out_n, ret_m, 0, m_send, m_recv, -1, False)
    send_self = None
    for c in chunks:
        wait_rows(out_g, arr_g, c, g_send, g_recv, 1, False)
        slot = arr_g[blocks_of(c)].reshape(CHUNK, D)
        total = None
        for k, (g, u, d) in enumerate(halves):
            cols = slice(k * 256, (k + 1) * 256)
            gh = dot_t(slot, d[...])
            dgate = (gh * slope_s[lanes_of(c), cols].astype(f32)).astype(bf16)
            dup = (gh * act_s[lanes_of(c), cols].astype(f32)).astype(bf16)
            slope_s[lanes_of(c), cols], act_s[lanes_of(c), cols] = dgate, dup
            part = dot_t(dgate, g[...]) + dot_t(dup, u[...])
            total = part if total is None else total + part
        wait_rows(out_g, arr_g, c, g_send, g_recv, 1, True)
        out_g[blocks_of(c)] = total.astype(bf16).reshape(GROUP, BLOCK, D)
        send_rows(out_g, ret_b, c, b_send, b_recv, -1)
    for b in range(4):
        cols = slice(b * 384, (b + 1) * 384)
        xt = flip(jnp.concatenate([arr_n[blocks_of(c), :, cols].reshape(CHUNK, 384) for c in chunks], axis=0))
        gg = dot(xt, slope_s[...])
        gu = dot(xt, act_s[...])
        gg_o[cols], gu_o[cols] = gg[:, :256], gu[:, :256]
        sg_v[0, cols], sg_v[1, cols] = gg[:, 256:].astype(bf16), gu[:, 256:].astype(bf16)
    trade = [go(remote(sg_v, grecv_a, rep_send.at[3], rep_recv.at[3], twin))]
    for copy in finals:
        copy.wait()
    hid_t = flip(hid[...])
    for b in range(4):
        cols = slice(b * 384, (b + 1) * 384)
        gd = dot(hid_t, jnp.concatenate([arr_g[blocks_of(c), :, cols].reshape(CHUNK, 384) for c in chunks], axis=0))
        gd_o[:, cols] = gd[:256]
        sd_v[0, b * 256 : (b + 1) * 256] = gd[256:].astype(bf16)
    trade.append(go(remote(sd_v.at[0], grecv_b, rep_send.at[4], rep_recv.at[4], twin)))

    picked = jnp.zeros((2 * TOK, 128), f32)
    for c in chunks:
        if c:
            wait_rows(out_n, ret_m, c, m_send, m_recv, -1, False)
        rows = ret_m[blocks_of(c)].reshape(CHUNK, D)
        acc[...] += dot(gated[:, lanes_of(c)], rows)
        grads = dot_t(cot2[...].reshape(2 * TOK, D), rows) * hits[:, lanes_of(c)].astype(f32)
        high = grads.astype(bf16)
        low = (grads - high.astype(f32)).astype(bf16)
        own = owner[:, lanes_of(c)]
        picked = picked + dot_t(high, own) + dot_t(low, own)
    part_s[0] = acc[TOK:].astype(bf16)
    pick_s[...] = picked[TOK:]
    pair.append(go(remote(part_s.at[0], part_r.at[0], pair_send.at[3], pair_recv.at[3], partner)))
    pair.append(go(remote(pick_s, pick_r, pair_send.at[4], pair_recv.at[4], partner)))
    pair[3].wait_recv()
    out_r[...] = (acc[:TOK] + part_r[0].astype(f32)).astype(bf16)
    pair[4].wait_recv()
    picked = picked[:TOK] + pick_r[...]
    gates = code_r[1]
    mean = jnp.sum(gates * picked, axis=-1, keepdims=True)
    gl = (gates * (picked - mean)).astype(bf16)
    misc_r[...] = dot(ntt[...], gl)
    acc[:TOK] = gnt_r[...] + dot_t(gl, router_r[...])
    acc[TOK:] = jnp.zeros((TOK, D), f32)
    for c in chunks:
        wait_rows(out_g, ret_b, c, b_send, b_recv, -1, False)
        acc[...] += dot(hits[:, lanes_of(c)], ret_b[blocks_of(c)].reshape(CHUNK, D))
    part_s[1] = acc[TOK:].astype(bf16)
    pair.append(go(remote(part_s.at[1], part_r.at[1], pair_send.at[5], pair_recv.at[5], partner)))
    trade[0].wait_recv()
    gg_o[...] += grecv_a[0].astype(f32)
    gu_o[...] += grecv_a[1].astype(f32)
    trade[1].wait_recv()
    for b in range(4):
        gd_o[:, b * 384 : (b + 1) * 384] += grecv_b[b * 256 : (b + 1) * 256].astype(f32)
    pair[5].wait_recv()
    gnt_r[...] = acc[:TOK] + part_r[1].astype(f32)
    for c in chunks:
        wait_rows(out_n, ret_m, c, m_send, m_recv, -1, True)
        wait_rows(out_g, ret_b, c, b_send, b_recv, -1, True)
    for copy in started:
        copy.wait_send()


def moe(nt, cot, code, resid, router, mine, sg, su, sd):
    dma = pltpu.SemaphoreType.DMA
    vm = lambda shape, dtype=bf16: pltpu.VMEM(shape, dtype)
    rows = (PEERS, BLOCK, D)
    return pl.pallas_call(
        moe_kernel,
        out_shape=[sds((TOK, D)), sds((TOK, D), f32), sds((D, 128), f32), sds((D, 256), f32), sds((D, 256), f32), sds((256, D), f32), sds((4, D, 256)), sds((4, D, 256)), sds((4, 1024, 384))],
        in_specs=[ANY, ANY, VM, ANY, VM, VM, VM, VM, ANY, ANY, ANY],
        out_specs=[VM] * 6 + [ANY] * 3,
        scratch_shapes=[vm((2, TOK, D)), vm((2, TOK, D)), vm((2, TOK, 128), f32), vm((2 * TOK, SLOTS)), vm((2 * TOK, SLOTS)), vm((128, SLOTS))]
        + [vm(rows)] * 6
        + [vm((D, 256)), vm((D, 256)), vm((256, D)), vm((SLOTS, 512)), vm((SLOTS, 512)), vm((SLOTS, 512)), vm((2 * TOK, D), f32)]
        + [vm((2, D, 256)), vm((1024, 384)), vm((2, TOK, D)), vm((2, TOK, D)), vm((TOK, 128), f32), vm((TOK, 128), f32)]
        + [vm((2, D, 256)), vm((2, D, 256)), vm((4, 1024, 384)), vm((TOK, 1024)), vm((D, TOK)), vm((2, D, 256))]
        + [dma((6,)), dma((6,)), dma((5,)), dma((5,))] + [dma((PEERS,))] * 8 + [dma, dma((7,)), dma((2,))],
        compiler_params=pltpu.CompilerParams(collective_id=3, has_side_effects=True, vmem_limit_bytes=63 << 20),
        name="moe",
    )(nt, cot, code, resid, router, *mine, sg, su, sd)


class Scatter(Links):
    def __init__(self, total, other, landing, spread, outs, own_sem, dsend, drecv, rsend, rrecv, send, recv, msend, mrecv):
        super().__init__()
        self.total, self.other, self.landing, self.spread, self.outs = total, other, landing, spread, outs
        self.own_sem, self.dsend, self.drecv, self.rsend, self.rrecv = own_sem, dsend, drecv, rsend, rrecv
        self.send, self.recv, self.msend, self.mrecv = send, recv, msend, mrecv

    def spot(self, i, done, where, half=None):
        return region(where, ORDERS[i], done, half=half)[1:]

    def add(self, i, where, ref, *spots):
        to = self.total[i]
        total = to[where].astype(f32)
        for spot in spots:
            total = total + ref[spot].astype(f32)
        to[where] = total.astype(bf16)

    def start(self, i, src, own=None):
        local = None
        if own is not None:
            local = pltpu.make_async_copy(own, self.total[i], self.own_sem.at[i])
            local.start()
        self.sent[i] = (local, self.go(src, self.other[i], self.dsend.at[i], self.drecv.at[i], self.sibling))

    def message(self, i, side, number):
        axis, done = ORDERS[i][2], ORDERS[i][:2]
        step = STEPS[side]
        spot, k = ((moved(self.at, axis, 2), side), (moved(self.at, axis, step), 1 - side), (moved(self.at, axis, step), side))[number]
        src = self.total[i].at[self.spot(i, done, spot, k)]
        dst = self.landing[i][0].at[side, number]
        self.sent[i, 2, side, number] = self.go(src, dst, self.rsend.at[i, side, number], self.rrecv.at[i, side, number], moved(self.at, axis, step))

    def enter(self, i):
        local, copy = self.sent[i]
        if local is not None:
            local.wait()
        copy.wait_recv()

        def both(z, carry):
            for h in range(2):
                for l in range(2):
                    for x in range(4):
                        self.add(i, (h, z, l, x), self.other[i], (h, z, l, x))
            return carry

        lax.fori_loop(0, 4, both, 0)
        for number in range(2):
            for side in range(2):
                self.message(i, side, number)

    def relay(self, i):
        axis, done = ORDERS[i][2], ORDERS[i][:2]
        for side in range(2):
            self.sent[i, 2, side, 0].wait_recv()
            self.add(i, self.spot(i, done, moved(self.at, axis, STEPS[side]), side), self.landing[i][0], (side, 0))
            self.message(i, side, 2)

    def direct(self, i, phase):
        axis, done = ORDERS[i][phase], ORDERS[i][:phase]
        self.sent[i, phase] = [
            self.go(self.total[i].at[self.spot(i, done, moved(self.at, axis, by))], self.landing[i][2 - phase].at[k], self.send.at[i, phase, k], self.recv.at[i, phase, k], moved(self.at, axis, by))
            for k, by in enumerate(STEPS)
        ]

    def second(self, i):
        done = ORDERS[i][:2]
        for side in range(2):
            for number in (1, 2):
                self.sent[i, 2, side, number].wait_recv()
        for k in range(2):
            self.add(i, self.spot(i, done, self.at, k), self.landing[i][0], (k, 2), (1 - k, 1))
        self.direct(i, 1)

    def third(self, i):
        for copy in self.sent[i, 1]:
            copy.wait_recv()
        self.add(i, self.spot(i, ORDERS[i][:1], self.at), self.landing[i][1], 0, 1, 2)
        self.direct(i, 0)

    def spread_rows(self, i):
        for copy in self.sent[i, 0]:
            copy.wait_recv()
        chunk = self.total[i][self.spot(i, "", self.at)].astype(f32)
        for k in range(3):
            chunk = chunk + self.landing[i][2][k].astype(f32)
        size, take = rows_of(i), PIECE[i]
        to_row, from_row = iota((64, size), 0), iota((64, size), 1)
        pick = ((from_row // take) * 16 + from_row % take == to_row).astype(bf16)
        laid = dot(pick, chunk.astype(bf16)).astype(bf16)
        self.spread[i][...] = laid.reshape(4, 16, WIDE[i])
        own = pltpu.make_async_copy(self.spread[i].at[self.mine], self.outs[i].at[self.mine], self.own_sem.at[i])
        own.start()
        finals = [own]
        for k, to in enumerate(self.peers):
            quarter = to["core"] * 2 + to["y"] // 2
            finals.append(self.go(self.spread[i].at[quarter], self.outs[i].at[self.mine], self.msend.at[i, k], self.mrecv.at[i, k], to))
        self.sent[i, "final"] = finals

    def finish(self):
        for i in range(N):
            own, *copies = self.sent[i, "final"]
            own.wait()
            for copy in copies:
                copy.wait_recv()
        self.end()


def half_box(order):
    return {"xyz": (2, 2, 2), "yzx": (4, 2), "zxy": (2, 4)}[order]


def back_kernel(*refs):
    gnt, resid_r, cot, tokens, normed_r, q_r, kv_r, p_r, att_r, misc_in, misc_w = refs[:11]
    shared_h, weights = refs[11:14], refs[14:20]
    gtok_o, *outs = refs[20:30]
    total, other = refs[30:39], refs[39:48]
    landing = [refs[48 + 3 * i : 51 + 3 * i] for i in range(N)]
    spread, hand = refs[75:84], refs[84:90]
    left_s, right_s, gv_s, goo_s, gatt_s, turned, acc, gres, misc_s, slots, slot_sem, *sems = refs[90:]
    s = Scatter(total, other, landing, spread, outs, *sems)
    core = s.core
    loads = {}

    def load(j, parts):
        loads[j] = []
        at_lane = 0
        for k, (i, width) in enumerate(parts):
            src = weights[i].at[j] if width == WIDE[i] else weights[i].at[j, :, pl.ds(0, width)]
            copy = pltpu.make_async_copy(src, slots.at[j, :, pl.ds(at_lane, width)], slot_sem.at[j, k])
            copy.start()
            loads[j].append(copy)
            at_lane += width

    def loaded(j):
        for copy in loads[j]:
            copy.wait()

    def weight_grads(group, right):
        for k in range(2):
            for i, value in zip(group, right(2 * (1 - core) + k)):
                hand[i][k] = value.astype(bf16).reshape(core_box(i)[1:])
        for i in group:
            s.start(i, hand[i])
        for k in range(2):
            for i, value in zip(group, right(2 * core + k)):
                total[i][k] = value.astype(bf16).reshape(core_box(i)[1:])

    for j in range(4):
        load(j, [(3, 128), (4, 128), (5, 128)])
    s.greet()
    for i, src in zip(SHARED, shared_h):
        s.start(i, src.at[1 - core], src.at[core])

    resid = resid_r[...]
    scale = rms_scale(resid)
    grad = gnt[...]
    lane = iota((TOK, 128), 1)
    misc_s[...] = misc_in[...] + t_dot((grad * resid * scale).astype(bf16), (lane == 65).astype(bf16))
    gres[...] = cot[...].astype(f32) + norm_back(grad, resid, scale, gain_row(misc_w[...], 65))
    acc[...] = jnp.zeros((TOK, D), f32)
    for j in range(4):
        goo_s[j] = gres[:, j * 384 : (j + 1) * 384].astype(bf16)
        turned[j * 384 : (j + 1) * 384] = flip(att_r[j])
        loaded(j)
        acc[...] += dot_t(goo_s[j], slots[j])
        load(j, [(0, 256), (2, 128)])

    def out_grads(j):
        whole = dot(turned[...], goo_s[j])
        return whole[:, :128], whole[:, 128:256], whole[:, 256:]

    weight_grads(OUT, out_grads)
    for j in range(4):
        gatt_s[j] = acc[:, j * 384 : (j + 1) * 384].astype(bf16)
    for i in SHARED:
        s.enter(i)
    for j in range(4):
        ga, q, kv, p = gatt_s[j], q_r[j], kv_r[j], p_r[j]
        ga3 = jnp.concatenate([ga[:, :128], ga[:, 128:256], ga[:, 256:]], axis=0)
        q3 = jnp.concatenate([q[:, :128], q[:, 128:256], q[:, 256:]], axis=0)
        gp = dot_t(ga3, kv[:, 128:])
        gs = (p * (gp - jnp.sum(p * gp, axis=-1, keepdims=True))).astype(bf16)
        gq3 = (dot(gs, kv[:, :128]) * SCALE).astype(bf16)
        gk = (t_dot(gs, q3) * SCALE).astype(bf16)
        gv_s[j] = t_dot(p.astype(bf16), ga3).astype(bf16)
        left_s[j] = jnp.concatenate([gq3[:128], gq3[128:256]], axis=1)
        right_s[j] = jnp.concatenate([gq3[256:], gk], axis=1)
        if j == 1:
            for i in OUT:
                s.enter(i)
    for i in SHARED:
        s.relay(i)
    turned[...] = flip(normed_r[...])
    weight_grads((0, 1), lambda j: (dot(turned[...], left_s[j]), dot(turned[...], right_s[j])))
    for i in OUT:
        s.relay(i)
    acc[...] = jnp.zeros((TOK, D), f32)
    for j in range(4):
        loaded(j)
        acc[...] += dot_t(jnp.concatenate([left_s[j], gv_s[j]], axis=1), slots[j])
        load(j, [(1, 256)])
    for i in SHARED:
        s.second(i)
    for j in range(4):
        loaded(j)
        acc[...] += dot_t(right_s[j], slots[j, :, :256])
    source = tokens[...].astype(f32)
    scale = rms_scale(source)
    misc_s[...] += t_dot((acc[...] * source * scale).astype(bf16), (lane == 64).astype(bf16))
    weight_grads((2,), lambda j: (jnp.concatenate([dot(turned[...], gv_s[j]), misc_s[...] * jnp.where(j == 0, 1.0, 0.0)], axis=1),))
    for i in (0, 1):
        s.enter(i)
    gtok_o[...] = gres[...] + norm_back(acc[...], source, scale, gain_row(misc_w[...], 64))
    s.enter(2)
    for i in OUT:
        s.second(i)
    for i in SHARED:
        s.third(i)
    for i in QKV:
        s.relay(i)
    for i in OUT:
        s.third(i)
    for i in SHARED:
        s.spread_rows(i)
    for i in QKV:
        s.second(i)
    for i in OUT:
        s.spread_rows(i)
    for i in QKV:
        s.third(i)
    for i in QKV:
        s.spread_rows(i)
    s.finish()


def back(gnt, resid, cot, tokens, normed, q, kv, p, att, misc_in, misc_w, shared_grads, weights):
    grads = [g.reshape((2,) + core_box(i)) for i, g in zip(SHARED, shared_grads)]
    vm = lambda shape, dtype=bf16: pltpu.VMEM(shape, dtype)
    dma = pltpu.SemaphoreType.DMA
    halves = [vm(core_box(i)) for i in range(N)]
    scratch = halves * 2
    for i in range(N):
        tail = (rows_of(i), WIDE[i])
        scratch += [vm((2, 3) + half_box(ORDERS[i]) + tail), vm((3,) + axis_box(ORDERS[i][0]) + tail), vm((3,) + tail)]
    scratch += [vm((4, 16, w)) for w in WIDE] + halves[:6]
    scratch += [vm((4, TOK, 256)), vm((4, TOK, 256)), vm((4, TOK, 128)), vm((4, TOK, 384)), vm((4, TOK, 384)), vm((D, TOK)), vm((TOK, D), f32), vm((TOK, D), f32), vm((D, 128), f32), vm((4, D, 384)), dma((4, 3))]
    scratch += [dma((N,)), dma((N,)), dma((N,)), dma((N, 2, 3)), dma((N, 2, 3)), dma((N, 2, 3)), dma((N, 2, 3)), dma((N, 3)), dma((N, 3))]
    return pl.pallas_call(
        back_kernel,
        out_shape=[sds((TOK, D), f32)] + [sds((4, 16, w)) for w in WIDE],
        in_specs=[VM] * 11 + [ANY] * 9,
        out_specs=[VM] * 10,
        scratch_shapes=scratch,
        compiler_params=pltpu.CompilerParams(collective_id=2, has_side_effects=True, vmem_limit_bytes=63 << 20),
        name="back",
    )(gnt, resid, cot, tokens, normed, q, kv, p, att, misc_in, misc_w, *grads, *weights)


def final_kernel(*refs):
    gtok, block, gg, gu, gd = refs[:5]
    outs = refs[5:14]
    block_o, gtok_o, gq_o, gk_o, gv_o, go_o, gsg_o, gsu_o, gsd_o, gr_o, g1_o, g2_o, gg_o, gu_o, gd_o = refs[14:]
    for src, dst in ((gtok, gtok_o), (block, block_o), (gg, gg_o), (gu, gu_o), (gd, gd_o)):
        dst[...] = src[...]
    for j in range(4):
        block = [outs[i][j].astype(f32)[: PIECE[i]] for i in range(N)]
        gq_o[:, j * 384 : j * 384 + 256] = block[0]
        gq_o[:, j * 384 + 256 : (j + 1) * 384] = block[1][:, :128]
        gk_o[:, j * 128 : (j + 1) * 128] = block[1][:, 128:]
        gv_o[:, j * 128 : (j + 1) * 128] = block[2][:, :128]
        for p in range(3):
            go_o[:, j * 384 + p * 128 : j * 384 + (p + 1) * 128] = block[3 + p]
        gsg_o[:, j * 256 : (j + 1) * 256] = block[6]
        gsu_o[:, j * 256 : (j + 1) * 256] = block[7]
        gsd_o[:, j * 384 : (j + 1) * 384] = block[8]
    misc = outs[2][0].astype(f32)[:12, 128:]
    gr_o[...] = misc[:, :64]
    eye = iota((12, 12), 0) == iota((12, 12), 1)
    for k, out in ((64, g1_o), (65, g2_o)):
        out[...] = jnp.sum(jnp.where(eye, misc[:, k : k + 1], 0.0), axis=0, keepdims=True)


def final(gtok, block, expert, pieces):
    shapes = ((TOK, D), (12, D), (12, 512), (12, 512), (12, D), (12, 1024), (12, 1024), (8, D), (12, 64), (1, 12), (1, 12), (D, 256), (D, 256), (256, D))
    return pl.pallas_call(
        final_kernel,
        out_shape=[sds((TOK, D))] + [sds(s, f32) for s in shapes],
        in_specs=[VM] * 14,
        out_specs=[VM] * 15,
        compiler_params=pltpu.CompilerParams(vmem_limit_bytes=40 << 20),
        name="final",
    )(gtok, block, *expert, *pieces)


def local(tokens, segment_ids, routes, cotangent, query_weight, key_weight, value_weight, output_weight, shared_gate, shared_up, shared_down, router_weight, first_gain, second_gain, expert_gate, expert_up, expert_down):
    (normed, q, kv, p, att, resid, nt, code, misc_w), weights = front(
        tokens, segment_ids, routes.T, query_weight, key_weight, value_weight, output_weight, router_weight,
        first_gain[None], second_gain[None], shared_gate, shared_up, shared_down,
    )
    mine = [expert_gate[0], expert_up[0], expert_down[0]]
    block, gnt, gmisc, gg, gu, gd, *shared_grads = moe(nt, cotangent, code, resid, misc_w, mine, *weights[6:])
    gtok, *pieces = back(gnt, resid, cotangent, tokens, normed, q, kv, p, att, gmisc, misc_w, shared_grads, weights[:6])
    *outs, g1, g2, gg, gu, gd = final(gtok, block, (gg, gu, gd), pieces)
    return *outs, g1[0], g2[0], gg[None], gu[None], gd[None]


def solution(mesh):
    in_specs = (
        P(("fsdp", "rep"), None),
        P(("fsdp", "rep"), None),
        P(("fsdp", "rep"), None),
        P(("fsdp", "rep"), None),
        P(("fsdp", "rep"), None),
        P(("fsdp", "rep"), None),
        P(("fsdp", "rep"), None),
        P(("fsdp", "rep"), None),
        P(("fsdp", "rep"), None),
        P(("fsdp", "rep"), None),
        P(("fsdp", "rep"), None),
        P(("fsdp", "rep"), None),
        P(("fsdp", "rep")),
        P(("fsdp", "rep")),
        P("fsdp", None, "rep"),
        P("fsdp", None, "rep"),
        P("fsdp", "rep", None),
    )
    out_specs = (
        P(("fsdp", "rep"), None),
        P(("fsdp", "rep"), None),
        P(("fsdp", "rep"), None),
        P(("fsdp", "rep"), None),
        P(("fsdp", "rep"), None),
        P(("fsdp", "rep"), None),
        P(("fsdp", "rep"), None),
        P(("fsdp", "rep"), None),
        P(("fsdp", "rep"), None),
        P(("fsdp", "rep"), None),
        P(("fsdp", "rep")),
        P(("fsdp", "rep")),
        P("fsdp", None, "rep"),
        P("fsdp", None, "rep"),
        P("fsdp", "rep", None),
    )
    return jax.shard_map(local, mesh=mesh, in_specs=in_specs, out_specs=out_specs, check_vma=False)
```

```python
import math

import jax
import jax.numpy as jnp
from jax import lax
from jax.experimental import pallas as pl
from jax.experimental.pallas import tpu as pltpu
from jax.sharding import PartitionSpec as P

MESH = pl.DeviceIdType.MESH
ANY = pl.BlockSpec(memory_space=pl.ANY)
VM = pl.BlockSpec(memory_space=pltpu.VMEM)


def place():
    f, r = lax.axis_index("fsdp"), lax.axis_index("rep")
    return dict(x=(f // 2) % 4, y=2 * r + (f // 8) % 2, z=f // 16, core=f % 2)


def device(at):
    return (((at["z"] * 2 + at["y"] % 2) * 4 + at["x"]) * 2 + at["core"], at["y"] // 2)


def moved(at, axis, by):
    return {**at, axis: (at[axis] + by) % (2 if axis == "core" else 4)}


def region(at, order, done, coordinate=None, half=None):
    first = done[0] if done else None
    spot = {}
    for axis in "xyz":
        whole = axis in done
        at_axis = at[axis]
        if axis == "y":
            if whole:
                spot["yhi"] = (half if (half is not None and first == "y") else slice(None))
                spot["ylo"] = slice(None)
            else:
                spot["yhi"], spot["ylo"] = at_axis // 2, at_axis % 2
        else:
            if whole:
                spot[axis] = pl.ds(2 * half, 2) if (half is not None and first == axis) else slice(None)
            else:
                spot[axis] = at_axis
    return (at["core"], spot["yhi"], spot["z"], spot["ylo"], spot["x"])


D = 1536
TOK = 128
TOP = 6
EXPERTS = 64
CAP = 24
SLOTS = EXPERTS * CAP
CHUNK = 384
epsilon = 1e-06
SCALE = 1.0 / math.sqrt(128)
f32, bf16, i32 = jnp.float32, jnp.bfloat16, jnp.int32


def dot(a, b):
    return jnp.dot(a, b, preferred_element_type=f32)


def dot_t(a, b):
    return lax.dot_general(a, b, (((1,), (1,)), ((), ())), preferred_element_type=f32)


def t_dot(a, b):
    return lax.dot_general(a, b, (((0,), (0,)), ((), ())), preferred_element_type=f32)


def flip(a):
    return a.astype(f32).T.astype(bf16)


def rms_scale(v):
    return lax.rsqrt(jnp.mean(v * v, axis=-1, keepdims=True) + epsilon)


def silu_parts(pre):
    s = jax.nn.sigmoid(pre)
    return pre * s, s * (1.0 + pre * (1.0 - s))


def norm_back(grad, source, scale, gain):
    weighted = grad * gain
    inner = jnp.mean(weighted * source, axis=-1, keepdims=True)
    return scale * weighted - source * (scale * scale * scale) * inner


def iota(shape, dim):
    return lax.broadcasted_iota(i32, shape, dim)


def gain_row(misc, lane):
    pick = (iota((16, 128), 1) == lane).astype(bf16)
    return dot_t(pick, misc)[0:1]


def chosen(routes):
    lanes = iota((TOK, 128), 1)
    hit = jnp.zeros((TOK, 128), f32)
    for k in range(TOP):
        hit = hit + (routes[:, k : k + 1] == lanes).astype(f32)
    return hit


def sds(shape, dtype=bf16):
    return jax.ShapeDtypeStruct(shape, dtype)


ORDERS = ("xyz", "yzx", "zxy") * 3
PIECE = (12, 12, 12, 12, 12, 12, 12, 12, 8)
WIDE = (256, 256, 256, 128, 128, 128, 256, 256, 384)
N = len(ORDERS)
QKV, OUT, SHARED = (0, 1, 2), (3, 4, 5), (6, 7, 8)
STEPS = (1, -1, 2)


def rows_of(i):
    return 4 * PIECE[i]


def core_box(i):
    return (2, 4, 2, 4, rows_of(i), WIDE[i])


def axis_box(axis):
    return (2, 2) if axis == "y" else (4,)


class Links:
    def __init__(self):
        self.at = place()
        self.core = self.at["core"]
        self.mine = self.core * 2 + self.at["y"] // 2
        self.sibling = moved(self.at, "core", 1)
        self.peers = [self.sibling, moved(self.at, "y", 2), moved(self.sibling, "y", 2)]
        self.started, self.sent = [], {}

    def greet(self):
        barrier = pltpu.get_barrier_semaphore()
        ring = [moved(self.at, axis, by) for axis in "xyz" for by in STEPS if (axis, by) != ("y", 2)]
        for to in self.peers + ring:
            pl.semaphore_signal(barrier, inc=1, device_id=device(to), device_id_type=MESH)
        pl.semaphore_wait(barrier, len(self.peers) + len(ring))

    def remote(self, src, dst, s, r, to):
        return pltpu.make_async_remote_copy(src_ref=src, dst_ref=dst, send_sem=s, recv_sem=r, device_id=device(to), device_id_type=MESH)

    def go(self, *args):
        copy = self.remote(*args)
        copy.start()
        self.started.append(copy)
        return copy

    def end(self):
        for copy in self.started:
            copy.wait_send()


class Gather(Links):
    def __init__(self, shards, got, stage, bufs, mix_send, mix_recv, own_sem, send, recv, rsend, rrecv, dsend, drecv):
        super().__init__()
        self.shards, self.got, self.stage, self.bufs = shards, got, stage, bufs
        self.mix_send, self.mix_recv, self.own_sem = mix_send, mix_recv, own_sem
        self.send, self.recv, self.rsend, self.rrecv, self.dsend, self.drecv = send, recv, rsend, rrecv, dsend, drecv

    def here(self, i, done, spot=None, half=None):
        return self.bufs[i].at[region(self.at if spot is None else spot, ORDERS[i], done, half=half)]

    def mix(self, i):
        own = pltpu.make_async_copy(self.shards[i].at[self.mine], self.got[i].at[self.mine], self.own_sem.at[i])
        own.start()
        copies = []
        for k, to in enumerate(self.peers):
            quarter = to["core"] * 2 + to["y"] // 2
            copies.append(self.go(self.shards[i].at[quarter], self.got[i].at[self.mine], self.mix_send.at[i, k], self.mix_recv.at[i, k], to))
        self.sent[i, "mix"] = (own, copies)

    def direct(self, i, phase, src):
        axis, done = ORDERS[i][phase], ORDERS[i][:phase]
        self.sent[i, phase] = [
            self.go(src, self.here(i, done), self.send.at[i, phase, k], self.recv.at[i, phase, k], moved(self.at, axis, by))
            for k, by in enumerate(STEPS)
        ]

    def enter(self, i):
        own, copies = self.sent[i, "mix"]
        own.wait()
        for copy in copies:
            copy.wait_recv()
        size, take = rows_of(i), PIECE[i]
        to_row, from_row = iota((size, 64), 0), iota((size, 64), 1)
        pick = ((to_row // take) * 16 + to_row % take == from_row).astype(bf16)
        self.stage[i][...] = dot(pick, self.got[i][...].reshape(64, WIDE[i])).astype(bf16)
        local = pltpu.make_async_copy(self.stage[i], self.here(i, ""), self.own_sem.at[i])
        local.start()
        self.sent[i, "own"] = local
        self.direct(i, 0, self.stage[i])

    def second(self, i):
        self.sent[i, "own"].wait()
        for copy in self.sent[i, 0]:
            copy.wait_recv()
        self.direct(i, 1, self.here(i, ORDERS[i][:1]))

    def third(self, i):
        for copy in self.sent[i, 1]:
            copy.wait_recv()
        axis, done = ORDERS[i][2], ORDERS[i][:2]
        src = self.here(i, done)
        self.sent[i, 2] = [self.go(src, src, self.rsend.at[i, k], self.rrecv.at[i, k], moved(self.at, axis, STEPS[k])) for k in range(2)]
        self.go(src, src, self.dsend.at[i, 3], self.drecv.at[i, 3], self.sibling)

    def relay(self, i):
        axis, done = ORDERS[i][2], ORDERS[i][:2]
        halves = []
        for k in range(2):
            self.sent[i, 2][k].wait_recv()
            block = moved(self.at, axis, -STEPS[k])
            part = self.here(i, done, block, half=k)
            halves.append(self.go(part, part, self.rsend.at[i, 2 + k], self.rrecv.at[i, 2 + k], moved(self.at, axis, STEPS[k])))
            whole = self.here(i, done, block)
            self.go(whole, whole, self.dsend.at[i, k], self.drecv.at[i, k], self.sibling)
        self.sent[i, "far"] = halves

    def far(self, i):
        for copy in self.sent[i, "far"]:
            copy.wait_recv()
        whole = self.here(i, ORDERS[i][:2], moved(self.at, ORDERS[i][2], 2))
        self.go(whole, whole, self.dsend.at[i, 2], self.drecv.at[i, 2], self.sibling)

    def done(self, i):
        axis, done = ORDERS[i][2], ORDERS[i][:2]
        for k, by in ((3, 0), (0, -1), (1, 1), (2, 2)):
            where = self.here(i, done, moved(moved(self.at, axis, by) if by else self.at, "core", 1))
            self.remote(where, where, self.dsend.at[i, k], self.drecv.at[i, k], self.sibling).wait_recv()


def front_kernel(*refs):
    tokens, seg, routes, w_query, w_key, w_value, w_output, w_router, gain_one, gain_two = refs[:10]
    normed_o, q_o, kv_o, p_o, att_o, resid_o, nt_o, code_o, misc_o = refs[13:22]
    outs = refs[22:31]
    shards, got, stage = refs[31:40], refs[40:49], refs[49:58]
    held = refs[58:64]
    out_sem, *sems = refs[64:]
    zero = jnp.zeros((4, 16, 384), bf16)
    for shard in shards:
        shard[...] = zero[:, :, : shard.shape[2]]
    eye = iota((12, 12), 0) == iota((12, 12), 1)
    router = w_router[...]
    for j in range(4):
        for p in range(3):
            at_lane = j * 384 + p * 128
            block = w_query[:, at_lane : at_lane + 128]
            if p < 2:
                shards[0][j, :12, p * 128 : (p + 1) * 128] = block
            else:
                shards[1][j, :12, :128] = block
            shards[3 + p][j, :12] = w_output[:, at_lane : at_lane + 128]
        shards[1][j, :12, 128:] = w_key[:, j * 128 : (j + 1) * 128]
        shards[2][j, :12, :128] = w_value[:, j * 128 : (j + 1) * 128]
        shards[2][j, :12, 128:192] = router
        for k, gain in enumerate((gain_one, gain_two)):
            column = jnp.sum(jnp.where(eye, gain[...].astype(f32), 0.0), axis=1, keepdims=True)
            shards[2][j, :12, 192 + k : 193 + k] = column.astype(bf16)
        for i, weight in zip(SHARED, refs[10:13]):
            shards[i][j, : PIECE[i]] = weight[:, j * WIDE[i] : (j + 1) * WIDE[i]]
    g = Gather(shards, got, stage, list(held) + list(outs[6:]), *sems)
    g.greet()
    for i in range(N):
        g.mix(i)
    source = tokens[...].astype(f32)
    row = jnp.broadcast_to(seg[...].astype(f32), (TOK, TOK))
    allowed = (row == row.T) & (iota((TOK, TOK), 1) <= iota((TOK, TOK), 0))
    allowed = jnp.concatenate([allowed.astype(f32)] * 3, axis=0)
    hit = jnp.zeros((TOK, TOK), f32)
    for k in range(TOP):
        hit = hit + (routes[k : k + 1] == iota((TOK, TOK), 0)).astype(f32)
    hit = hit.T
    earlier = (iota((TOK, TOK), 1) < iota((TOK, TOK), 0)).astype(bf16)
    code_o[0] = hit * (dot(earlier, hit.astype(bf16)) + 1.0)
    scaled = source * rms_scale(source)
    for group in (QKV, OUT):
        for i in group:
            g.enter(i)
    for i in QKV:
        g.second(i)
    for i in QKV:
        g.third(i)
    for i in OUT:
        g.second(i)
    for i in QKV:
        g.relay(i)
    for i in OUT:
        g.third(i)
    for i in SHARED:
        g.enter(i)
    for i in QKV:
        g.far(i)
    for i in OUT:
        g.relay(i)
    for i in SHARED:
        g.second(i)
    for i in QKV:
        g.done(i)
    keeps = []

    def weight(i, j):
        return held[i][j // 2, j % 2].reshape(D, WIDE[i])

    def keep(i):
        copy = pltpu.make_async_copy(held[i], outs[i], out_sem.at[i])
        copy.start()
        keeps.append(copy)

    normed_o[...] = (scaled * gain_row(weight(2, 0)[:, 128:], 64)).astype(bf16)
    for i in OUT:
        g.far(i)
    for j in range(4):
        normed = normed_o[...]
        q01 = dot(normed, weight(0, j)).astype(bf16)
        q2k = dot(normed, weight(1, j)).astype(bf16)
        v = dot(normed, weight(2, j)[:, :128]).astype(bf16)
        q_o[j] = jnp.concatenate([q01, q2k[:, :128]], axis=1)
        kv_o[j] = jnp.concatenate([q2k[:, 128:], v], axis=1)
        q3 = jnp.concatenate([q01[:, :128], q01[:, 128:], q2k[:, :128]], axis=0)
        scores = jnp.where(allowed > 0, dot_t(q3, q2k[:, 128:]) * SCALE, -1e30)
        expo = jnp.exp(scores - jnp.max(scores, axis=-1, keepdims=True))
        p = expo / jnp.sum(expo, axis=-1, keepdims=True)
        p_o[j] = p
        mixed = dot(p.astype(bf16), v).astype(bf16)
        att_o[j] = jnp.concatenate([mixed[:128], mixed[128:256], mixed[256:]], axis=1)
        if j == 0:
            for i in SHARED:
                g.third(i)
        if j == 2:
            for i in SHARED:
                g.relay(i)
    for i in QKV:
        keep(i)
    for i in OUT:
        g.done(i)
    attended = jnp.concatenate([att_o[j] for j in range(4)], axis=1)
    for j in range(4):
        for p in range(3):
            cols = slice(j * 384 + p * 128, j * 384 + (p + 1) * 128)
            resid_o[:, cols] = source[:, cols] + dot(attended, weight(3 + p, j))
    for i in OUT:
        keep(i)
    resid = resid_o[...]
    misc = weight(2, 0)[:, 128:]
    misc_o[...] = misc
    nt = (resid * rms_scale(resid) * gain_row(misc, 65)).astype(bf16)
    nt_o[...] = nt
    logits = dot(nt, misc)
    masked = jnp.where(hit > 0, logits, -1e30)
    expo = jnp.where(hit > 0, jnp.exp(masked - jnp.max(masked, axis=-1, keepdims=True)), 0.0)
    code_o[1] = expo / jnp.sum(expo, axis=-1, keepdims=True)
    for i in SHARED:
        g.far(i)
    for i in SHARED:
        g.done(i)
    for copy in keeps:
        copy.wait()
    g.end()


def front(*args):
    dma = pltpu.SemaphoreType.DMA
    full = lambda i: (2,) + core_box(i)
    res = pl.pallas_call(
        front_kernel,
        out_shape=[sds((TOK, D)), sds((4, TOK, 384)), sds((4, TOK, 256)), sds((4, 384, TOK), f32), sds((4, TOK, 384)), sds((TOK, D), f32), sds((TOK, D)), sds((2, TOK, 128), f32), sds((D, 128))]
        + [sds(full(i)) for i in range(N)],
        in_specs=[VM] * 13,
        out_specs=[VM] * 9 + [ANY] * N,
        scratch_shapes=[pltpu.VMEM((4, 16, WIDE[i]), bf16) for i in range(N)] * 2
        + [pltpu.VMEM((rows_of(i), WIDE[i]), bf16) for i in range(N)]
        + [pltpu.VMEM(full(i), bf16) for i in QKV + OUT]
        + [dma((6,)), dma((N, 3)), dma((N, 3)), dma((N,)), dma((N, 2, 3)), dma((N, 2, 3)), dma((N, 4)), dma((N, 4)), dma((N, 4)), dma((N, 4))],
        compiler_params=pltpu.CompilerParams(collective_id=1, has_side_effects=True, vmem_limit_bytes=60 << 20),
        name="front",
    )(*args)
    return res[:9], [o.reshape(4, 32 * rows_of(i), WIDE[i]) for i, o in enumerate(res[9:])]


STRIDE = 5
PEERS = 32
BLOCK = 2 * CAP
GROUP = CHUNK // BLOCK


def shift_of(s):
    t = (s * STRIDE) % PEERS
    return t // 8, (t // 2) % 4, t % 2


def shifted(at, s, sign):
    dz, dx, dc = shift_of(s)
    other = (at["core"] + dc) % 2
    way = 1 - 2 * at["core"] if sign == 1 else 2 * other - 1
    return {**at, "z": (at["z"] + way * dz + 4) % 4, "x": (at["x"] + way * dx + 4) % 4, "core": other}


def moe_kernel(
    nt_h, cot_h, code_r, resid_h, router_r, gm, um, dm, sg_h, su_h, sd_h,
    out_r, gnt_r, misc_r, gg_o, gu_o, gd_o, gsg_h, gsu_h, gsd_h,
    nt2, cot2, code2, hits, gated, owner, out_n, out_g, arr_n, arr_g, ret_m, ret_b,
    gx, ux, dx, hid, act_s, slope_s, acc, grecv_a, grecv_b, part_s, part_r, pick_s, pick_r,
    sg_v, su_v, sd_v, shid, ntt, stage,
    pair_send, pair_recv, rep_send, rep_recv, n_send, n_recv, g_send, g_recv, m_send, m_recv, b_send, b_recv, self_sem, load_sem, store_sem,
):
    at = place()
    partner = {**at, "y": at["y"] + 1 - 2 * (at["y"] % 2)}
    twin = moved(at, "y", 2)
    barrier = pltpu.get_barrier_semaphore()
    for to in (partner, twin):
        pl.semaphore_signal(barrier, inc=1, device_id=device(to), device_id_type=MESH)

    def hello(s, carry):
        pl.semaphore_signal(barrier, inc=1, device_id=device(shifted(at, s, 1)), device_id_type=MESH)
        return carry

    lax.fori_loop(1, PEERS, hello, 0)
    pl.semaphore_wait(barrier, PEERS + 1)

    def remote(src, dst, s, r, to):
        return pltpu.make_async_remote_copy(src_ref=src, dst_ref=dst, send_sem=s, recv_sem=r, device_id=device(to), device_id_type=MESH)

    started = []

    def go(copy):
        copy.start()
        started.append(copy)
        return copy

    nt_r, cot = nt2.at[0], cot2.at[0]
    first = [pltpu.make_async_copy(nt_h, nt_r, load_sem.at[5]), pltpu.make_async_copy(cot_h, cot, load_sem.at[6])]
    for copy in first:
        copy.start()
    pair = [go(remote(src, dst, pair_send.at[k], pair_recv.at[k], partner)) for k, (src, dst) in enumerate(((nt_h, nt2.at[1]), (code_r, code2), (cot_h, cot2.at[1])))]
    swaps = [go(remote(src, dst, rep_send.at[k], rep_recv.at[k], twin)) for k, (src, dst) in enumerate(((gm, gx), (um, ux), (dm, dx)))]

    def load(src, dst, k):
        copy = pltpu.make_async_copy(src, dst, load_sem.at[k])
        copy.start()
        return copy

    sd_copy = load(sd_h, sd_v, 4)
    loads = {}
    for j in range(2):
        loads[j] = (load(sg_h.at[j], sg_v.at[j], j), load(su_h.at[j], su_v.at[j], 2 + j))
    lane = iota((1, SLOTS), 1)
    block, spot = lane // BLOCK, lane % BLOCK
    there = shifted(at, block, 1)
    expert = ((there["z"] * 2 + at["y"] % 2) * 4 + there["x"]) * 2 + there["core"]
    owner[...] = (iota((128, SLOTS), 0) == expert).astype(bf16)
    for copy in first:
        copy.wait()
    ntt[...] = flip(nt_r[...])

    def fill(k, code, gates):
        wide = dot(code.astype(bf16), owner[...])
        hit = (wide == (spot - k * CAP + 1).astype(f32)) & (wide > 0)
        rows = slice(k * TOK, (k + 1) * TOK)
        hits[rows] = hit.astype(f32).astype(bf16)
        gated[rows] = jnp.where(hit, dot(gates.astype(bf16), owner[...]), 0.0).astype(bf16)

    fill(0, code_r[0], code_r[1])
    for copy in pair[:2]:
        copy.wait_recv()
    fill(1, code2[0], code2[1])

    def send_rows(box, land, c, ssem, rsem, sign):
        def one(s, carry):
            remote(box.at[s], land.at[s], ssem.at[s], rsem.at[s], shifted(at, s, sign)).start()
            return carry
        if c == 0:
            pltpu.make_async_copy(box.at[0], land.at[0], self_sem).start()
        lax.fori_loop(max(1, c * GROUP), (c + 1) * GROUP, one, 0)

    def wait_rows(box, land, c, ssem, rsem, sign, sent):
        def one(s, carry):
            copy = remote(box.at[s], land.at[s], ssem.at[s], rsem.at[s], shifted(at, s, sign))
            if sent:
                copy.wait_send()
            else:
                copy.wait_recv()
            return carry
        if c == 0 and not sent:
            pltpu.make_async_copy(box.at[0], land.at[0], self_sem).wait()
        lax.fori_loop(max(1, c * GROUP), (c + 1) * GROUP, one, 0)

    chunks = range(SLOTS // CHUNK)

    def lanes_of(c):
        return slice(c * CHUNK, (c + 1) * CHUNK)

    def blocks_of(c):
        return slice(c * GROUP, (c + 1) * GROUP)

    for c in chunks:
        rows = t_dot(hits[:, lanes_of(c)], nt2[...].reshape(2 * TOK, D))
        out_n[blocks_of(c)] = rows.astype(bf16).reshape(GROUP, BLOCK, D)
        send_rows(out_n, arr_n, c, n_send, n_recv, 1)
    wait_rows(out_n, arr_n, 0, n_send, n_recv, 1, False)
    pair[2].wait_recv()
    for c in chunks:
        rows = t_dot(gated[:, lanes_of(c)], cot2[...].reshape(2 * TOK, D))
        out_g[blocks_of(c)] = rows.astype(bf16).reshape(GROUP, BLOCK, D)
        send_rows(out_g, arr_g, c, g_send, g_recv, 1)

    sd_copy.wait()
    gh = jnp.zeros((TOK, 1024), f32)
    for j in range(4):
        gh = gh + dot_t(cot[:, j * 384 : (j + 1) * 384], sd_v[j])
    stores = []

    def store(k, value, dst):
        while len(stores) >= 2:
            stores.pop(0).wait()
        stage[k % 2] = value.astype(bf16)
        copy = pltpu.make_async_copy(stage.at[k % 2], dst, store_sem.at[k % 2])
        copy.start()
        stores.append(copy)

    acc[...] = jnp.zeros((2 * TOK, D), f32)
    for j in range(4):
        for copy in loads[j]:
            copy.wait()
        cols = slice(j * 256, (j + 1) * 256)
        gate, up = dot(nt_r[...], sg_v[j % 2]), dot(nt_r[...], su_v[j % 2])
        act, slope = silu_parts(gate)
        shid[:, cols] = (act * up).astype(bf16)
        dgate = (gh[:, cols] * up * slope).astype(bf16)
        dup = (gh[:, cols] * act).astype(bf16)
        acc[:TOK] += dot_t(dgate, sg_v[j % 2]) + dot_t(dup, su_v[j % 2])
        if j < 2:
            loads[j + 2] = (load(sg_h.at[j + 2], sg_v.at[j], j), load(su_h.at[j + 2], su_v.at[j], 2 + j))
        store(2 * j, dot(ntt[...], dgate), gsg_h.at[j])
        store(2 * j + 1, dot(ntt[...], dup), gsu_h.at[j])
    gnt_r[...] = acc[:TOK]
    resid_copy = load(resid_h, acc.at[pl.ds(0, TOK)], 5)
    for copy in stores:
        copy.wait()
    stores.clear()
    shid_t = flip(shid[...])
    finals = []
    resid_copy.wait()
    for j in range(4):
        cols = slice(j * 384, (j + 1) * 384)
        acc[:TOK, cols] += dot(shid[...], sd_v[j])
    acc[TOK:] = jnp.zeros((TOK, D), f32)
    for j in range(4):
        sd_v[j] = dot(shid_t, cot[:, j * 384 : (j + 1) * 384]).astype(bf16)
        copy = pltpu.make_async_copy(sd_v.at[j], gsd_h.at[j], load_sem.at[j])
        copy.start()
        finals.append(copy)

    for copy in swaps:
        copy.wait_recv()
    halves = ((gm, um, dm), (gx, ux, dx))
    for c in chunks:
        if c:
            wait_rows(out_n, arr_n, c, n_send, n_recv, 1, False)
        x = arr_n[blocks_of(c)].reshape(CHUNK, D)
        total = None
        for k, (g, u, d) in enumerate(halves):
            cols = slice(k * 256, (k + 1) * 256)
            gate, up = dot(x, g[...]), dot(x, u[...])
            act, slope = silu_parts(gate)
            hidden = (act * up).astype(bf16)
            hid[lanes_of(c), cols] = hidden
            act_s[lanes_of(c), cols] = act.astype(bf16)
            slope_s[lanes_of(c), cols] = (up * slope).astype(bf16)
            part = dot(hidden, d[...])
            total = part if total is None else total + part
        wait_rows(out_n, arr_n, c, n_send, n_recv, 1, True)
        out_n[blocks_of(c)] = total.astype(bf16).reshape(GROUP, BLOCK, D)
        send_rows(out_n, ret_m, c, m_send, m_recv, -1)
    wait_rows(out_n, ret_m, 0, m_send, m_recv, -1, False)
    send_self = None
    for c in chunks:
        wait_rows(out_g, arr_g, c, g_send, g_recv, 1, False)
        slot = arr_g[blocks_of(c)].reshape(CHUNK, D)
        total = None
        for k, (g, u, d) in enumerate(halves):
            cols = slice(k * 256, (k + 1) * 256)
            gh = dot_t(slot, d[...])
            dgate = (gh * slope_s[lanes_of(c), cols].astype(f32)).astype(bf16)
            dup = (gh * act_s[lanes_of(c), cols].astype(f32)).astype(bf16)
            slope_s[lanes_of(c), cols], act_s[lanes_of(c), cols] = dgate, dup
            part = dot_t(dgate, g[...]) + dot_t(dup, u[...])
            total = part if total is None else total + part
        wait_rows(out_g, arr_g, c, g_send, g_recv, 1, True)
        out_g[blocks_of(c)] = total.astype(bf16).reshape(GROUP, BLOCK, D)
        send_rows(out_g, ret_b, c, b_send, b_recv, -1)
    for b in range(4):
        cols = slice(b * 384, (b + 1) * 384)
        xt = flip(jnp.concatenate([arr_n[blocks_of(c), :, cols].reshape(CHUNK, 384) for c in chunks], axis=0))
        gg = dot(xt, slope_s[...])
        gu = dot(xt, act_s[...])
        gg_o[cols], gu_o[cols] = gg[:, :256], gu[:, :256]
        sg_v[0, cols], sg_v[1, cols] = gg[:, 256:].astype(bf16), gu[:, 256:].astype(bf16)
    trade = [go(remote(sg_v, grecv_a, rep_send.at[3], rep_recv.at[3], twin))]
    for copy in finals:
        copy.wait()
    hid_t = flip(hid[...])
    for b in range(4):
        cols = slice(b * 384, (b + 1) * 384)
        gd = dot(hid_t, jnp.concatenate([arr_g[blocks_of(c), :, cols].reshape(CHUNK, 384) for c in chunks], axis=0))
        gd_o[:, cols] = gd[:256]
        sd_v[0, b * 256 : (b + 1) * 256] = gd[256:].astype(bf16)
    trade.append(go(remote(sd_v.at[0], grecv_b, rep_send.at[4], rep_recv.at[4], twin)))

    picked = jnp.zeros((2 * TOK, 128), f32)
    for c in chunks:
        if c:
            wait_rows(out_n, ret_m, c, m_send, m_recv, -1, False)
        rows = ret_m[blocks_of(c)].reshape(CHUNK, D)
        acc[...] += dot(gated[:, lanes_of(c)], rows)
        grads = dot_t(cot2[...].reshape(2 * TOK, D), rows) * hits[:, lanes_of(c)].astype(f32)
        high = grads.astype(bf16)
        low = (grads - high.astype(f32)).astype(bf16)
        own = owner[:, lanes_of(c)]
        picked = picked + dot_t(high, own) + dot_t(low, own)
    part_s[0] = acc[TOK:].astype(bf16)
    pick_s[...] = picked[TOK:]
    pair.append(go(remote(part_s.at[0], part_r.at[0], pair_send.at[3], pair_recv.at[3], partner)))
    pair.append(go(remote(pick_s, pick_r, pair_send.at[4], pair_recv.at[4], partner)))
    pair[3].wait_recv()
    out_r[...] = (acc[:TOK] + part_r[0].astype(f32)).astype(bf16)
    pair[4].wait_recv()
    picked = picked[:TOK] + pick_r[...]
    gates = code_r[1]
    mean = jnp.sum(gates * picked, axis=-1, keepdims=True)
    gl = (gates * (picked - mean)).astype(bf16)
    misc_r[...] = dot(ntt[...], gl)
    acc[:TOK] = gnt_r[...] + dot_t(gl, router_r[...])
    acc[TOK:] = jnp.zeros((TOK, D), f32)
    for c in chunks:
        wait_rows(out_g, ret_b, c, b_send, b_recv, -1, False)
        acc[...] += dot(hits[:, lanes_of(c)], ret_b[blocks_of(c)].reshape(CHUNK, D))
    part_s[1] = acc[TOK:].astype(bf16)
    pair.append(go(remote(part_s.at[1], part_r.at[1], pair_send.at[5], pair_recv.at[5], partner)))
    trade[0].wait_recv()
    gg_o[...] += grecv_a[0].astype(f32)
    gu_o[...] += grecv_a[1].astype(f32)
    trade[1].wait_recv()
    for b in range(4):
        gd_o[:, b * 384 : (b + 1) * 384] += grecv_b[b * 256 : (b + 1) * 256].astype(f32)
    pair[5].wait_recv()
    gnt_r[...] = acc[:TOK] + part_r[1].astype(f32)
    for c in chunks:
        wait_rows(out_n, ret_m, c, m_send, m_recv, -1, True)
        wait_rows(out_g, ret_b, c, b_send, b_recv, -1, True)
    for copy in started:
        copy.wait_send()


def moe(nt, cot, code, resid, router, mine, sg, su, sd):
    dma = pltpu.SemaphoreType.DMA
    vm = lambda shape, dtype=bf16: pltpu.VMEM(shape, dtype)
    rows = (PEERS, BLOCK, D)
    return pl.pallas_call(
        moe_kernel,
        out_shape=[sds((TOK, D)), sds((TOK, D), f32), sds((D, 128), f32), sds((D, 256), f32), sds((D, 256), f32), sds((256, D), f32), sds((4, D, 256)), sds((4, D, 256)), sds((4, 1024, 384))],
        in_specs=[ANY, ANY, VM, ANY, VM, VM, VM, VM, ANY, ANY, ANY],
        out_specs=[VM] * 6 + [ANY] * 3,
        scratch_shapes=[vm((2, TOK, D)), vm((2, TOK, D)), vm((2, TOK, 128), f32), vm((2 * TOK, SLOTS)), vm((2 * TOK, SLOTS)), vm((128, SLOTS))]
        + [vm(rows)] * 6
        + [vm((D, 256)), vm((D, 256)), vm((256, D)), vm((SLOTS, 512)), vm((SLOTS, 512)), vm((SLOTS, 512)), vm((2 * TOK, D), f32)]
        + [vm((2, D, 256)), vm((1024, 384)), vm((2, TOK, D)), vm((2, TOK, D)), vm((TOK, 128), f32), vm((TOK, 128), f32)]
        + [vm((2, D, 256)), vm((2, D, 256)), vm((4, 1024, 384)), vm((TOK, 1024)), vm((D, TOK)), vm((2, D, 256))]
        + [dma((6,)), dma((6,)), dma((5,)), dma((5,))] + [dma((PEERS,))] * 8 + [dma, dma((7,)), dma((2,))],
        compiler_params=pltpu.CompilerParams(collective_id=3, has_side_effects=True, vmem_limit_bytes=63 << 20),
        name="moe",
    )(nt, cot, code, resid, router, *mine, sg, su, sd)


SUMS = (256, 256, 128, 128, 128, 256, 256, 256, 384)


def sum_box(i):
    return core_box(i)[:5] + (SUMS[i],)


class Scatter(Links):
    def __init__(self, total, other, landing, spread, outs, own_sem, dsend, drecv, rsend, rrecv, send, recv, msend, mrecv):
        super().__init__()
        self.total, self.other, self.landing, self.spread, self.outs = total, other, landing, spread, outs
        self.own_sem, self.dsend, self.drecv, self.rsend, self.rrecv = own_sem, dsend, drecv, rsend, rrecv
        self.send, self.recv, self.msend, self.mrecv = send, recv, msend, mrecv

    def spot(self, i, done, where, half=None):
        return region(where, ORDERS[i], done, half=half)[1:]

    def add(self, i, where, ref, *spots):
        to = self.total[i]
        total = to[where].astype(f32)
        for spot in spots:
            total = total + ref[spot].astype(f32)
        to[where] = total.astype(bf16)

    def start(self, i, src, own=None):
        local = None
        if own is not None:
            local = pltpu.make_async_copy(own, self.total[i], self.own_sem.at[i])
            local.start()
        self.sent[i] = (local, self.go(src, self.other[i], self.dsend.at[i], self.drecv.at[i], self.sibling))

    def message(self, i, side, number):
        axis, done = ORDERS[i][2], ORDERS[i][:2]
        step = STEPS[side]
        spot, k = ((moved(self.at, axis, 2), side), (moved(self.at, axis, step), 1 - side), (moved(self.at, axis, step), side))[number]
        src = self.total[i].at[self.spot(i, done, spot, k)]
        dst = self.landing[i][0].at[side, number]
        self.sent[i, 2, side, number] = self.go(src, dst, self.rsend.at[i, side, number], self.rrecv.at[i, side, number], moved(self.at, axis, step))

    def enter(self, i):
        local, copy = self.sent[i]
        if local is not None:
            local.wait()
        copy.wait_recv()

        def both(z, carry):
            for h in range(2):
                for l in range(2):
                    for x in range(4):
                        self.add(i, (h, z, l, x), self.other[i], (h, z, l, x))
            return carry

        lax.fori_loop(0, 4, both, 0)
        for number in range(2):
            for side in range(2):
                self.message(i, side, number)

    def relay(self, i):
        axis, done = ORDERS[i][2], ORDERS[i][:2]
        for side in range(2):
            self.sent[i, 2, side, 0].wait_recv()
            self.add(i, self.spot(i, done, moved(self.at, axis, STEPS[side]), side), self.landing[i][0], (side, 0))
            self.message(i, side, 2)

    def direct(self, i, phase):
        axis, done = ORDERS[i][phase], ORDERS[i][:phase]
        self.sent[i, phase] = [
            self.go(self.total[i].at[self.spot(i, done, moved(self.at, axis, by))], self.landing[i][2 - phase].at[k], self.send.at[i, phase, k], self.recv.at[i, phase, k], moved(self.at, axis, by))
            for k, by in enumerate(STEPS)
        ]

    def second(self, i):
        done = ORDERS[i][:2]
        for side in range(2):
            for number in (1, 2):
                self.sent[i, 2, side, number].wait_recv()
        for k in range(2):
            self.add(i, self.spot(i, done, self.at, k), self.landing[i][0], (k, 2), (1 - k, 1))
        self.direct(i, 1)

    def third(self, i):
        for copy in self.sent[i, 1]:
            copy.wait_recv()
        self.add(i, self.spot(i, ORDERS[i][:1], self.at), self.landing[i][1], 0, 1, 2)
        self.direct(i, 0)

    def spread_rows(self, i):
        for copy in self.sent[i, 0]:
            copy.wait_recv()
        chunk = self.total[i][self.spot(i, "", self.at)].astype(f32)
        for k in range(3):
            chunk = chunk + self.landing[i][2][k].astype(f32)
        size, take = rows_of(i), PIECE[i]
        to_row, from_row = iota((64, size), 0), iota((64, size), 1)
        pick = ((from_row // take) * 16 + from_row % take == to_row).astype(bf16)
        laid = dot(pick, chunk.astype(bf16)).astype(bf16)
        self.spread[i][...] = laid.reshape(4, 16, SUMS[i])
        own = pltpu.make_async_copy(self.spread[i].at[self.mine], self.outs[i].at[self.mine], self.own_sem.at[i])
        own.start()
        finals = [own]
        for k, to in enumerate(self.peers):
            quarter = to["core"] * 2 + to["y"] // 2
            finals.append(self.go(self.spread[i].at[quarter], self.outs[i].at[self.mine], self.msend.at[i, k], self.mrecv.at[i, k], to))
        self.sent[i, "final"] = finals

    def finish(self):
        for i in range(N):
            own, *copies = self.sent[i, "final"]
            own.wait()
            for copy in copies:
                copy.wait_recv()
        self.end()


def half_box(order):
    return {"xyz": (2, 2, 2), "yzx": (4, 2), "zxy": (2, 4)}[order]


def back_kernel(*refs):
    gnt, resid_r, cot, tokens, normed_r, q_r, kv_r, p_r, att_r, misc_in, misc_w = refs[:11]
    shared_h, weights = refs[11:14], refs[14:20]
    gtok_o, *outs = refs[20:30]
    total, other = refs[30:39], refs[39:48]
    landing = [refs[48 + 3 * i : 51 + 3 * i] for i in range(N)]
    spread, hand = refs[75:84], refs[84:90]
    left_s, right_s, gv_s, goo_s, gatt_s, turned, acc, gres, misc_s, slots, slot_sem, *sems = refs[90:]
    s = Scatter(total, other, landing, spread, outs, *sems)
    core = s.core
    loads = {}

    def load(j, parts):
        loads[j] = []
        at_lane = 0
        for k, (i, width) in enumerate(parts):
            src = weights[i].at[j] if width == WIDE[i] else weights[i].at[j, :, pl.ds(0, width)]
            copy = pltpu.make_async_copy(src, slots.at[j, :, pl.ds(at_lane, width)], slot_sem.at[j, k])
            copy.start()
            loads[j].append(copy)
            at_lane += width

    def loaded(j):
        for copy in loads[j]:
            copy.wait()

    def weight_grads(group, right):
        for k in range(2):
            for i, value in zip(group, right(2 * (1 - core) + k)):
                hand[i][k] = value.astype(bf16).reshape(sum_box(i)[1:])
        for i in group:
            s.start(i, hand[i])
        for k in range(2):
            for i, value in zip(group, right(2 * core + k)):
                total[i][k] = value.astype(bf16).reshape(sum_box(i)[1:])

    for j in range(4):
        load(j, [(3, 128), (4, 128), (5, 128)])
    s.greet()
    for i, src in zip(SHARED, shared_h):
        s.start(i, src.at[1 - core], src.at[core])

    resid = resid_r[...]
    scale = rms_scale(resid)
    grad = gnt[...]
    lane = iota((TOK, 128), 1)
    misc_s[...] = misc_in[...] + t_dot((grad * resid * scale).astype(bf16), (lane == 65).astype(bf16))
    gres[...] = cot[...].astype(f32) + norm_back(grad, resid, scale, gain_row(misc_w[...], 65))
    acc[...] = jnp.zeros((TOK, D), f32)
    for j in range(4):
        goo_s[j] = gres[:, j * 384 : (j + 1) * 384].astype(bf16)
        loaded(j)
        acc[...] += dot_t(goo_s[j], slots[j])
        load(j, [(0, 256), (2, 128)])
    for j in range(4):
        gatt_s[j] = acc[:, j * 384 : (j + 1) * 384].astype(bf16)
    turned[...] = flip(normed_r[...])
    for j in range(4):
        ga, q, kv, p = gatt_s[j], q_r[j], kv_r[j], p_r[j]
        ga3 = jnp.concatenate([ga[:, :128], ga[:, 128:256], ga[:, 256:]], axis=0)
        q3 = jnp.concatenate([q[:, :128], q[:, 128:256], q[:, 256:]], axis=0)
        gp = dot_t(ga3, kv[:, 128:])
        gs = (p * (gp - jnp.sum(p * gp, axis=-1, keepdims=True))).astype(bf16)
        gq3 = (dot(gs, kv[:, :128]) * SCALE).astype(bf16)
        gk = (t_dot(gs, q3) * SCALE).astype(bf16)
        gv_s[j] = t_dot(p.astype(bf16), ga3).astype(bf16)
        left_s[j] = jnp.concatenate([gq3[:128], gq3[128:256]], axis=1)
        right_s[j] = jnp.concatenate([gq3[256:], gk], axis=1)
    for i in SHARED:
        s.enter(i)
    weight_grads(QKV, lambda j: (dot(turned[...], left_s[j]), dot(turned[...], right_s[j]), dot(turned[...], gv_s[j])))
    acc[...] = jnp.zeros((TOK, D), f32)
    for j in range(4):
        loaded(j)
        acc[...] += dot_t(jnp.concatenate([left_s[j], gv_s[j]], axis=1), slots[j])
        load(j, [(1, 256)])
    for i in QKV:
        s.enter(i)
    for j in range(4):
        loaded(j)
        acc[...] += dot_t(right_s[j], slots[j, :, :256])
    source = tokens[...].astype(f32)
    scale = rms_scale(source)
    misc_s[...] += t_dot((acc[...] * source * scale).astype(bf16), (lane == 64).astype(bf16))
    for i in SHARED:
        s.relay(i)
    for j in range(4):
        turned[j * 384 : (j + 1) * 384] = flip(att_r[j])

    def out_grads(j):
        whole = dot(turned[...], goo_s[j])
        misc = misc_s[...] * jnp.where(j == 0, 1.0, 0.0)
        return whole[:, :128], whole[:, 128:256], jnp.concatenate([whole[:, 256:], misc], axis=1)

    weight_grads(OUT, out_grads)
    for i in QKV:
        s.relay(i)
    for i in OUT:
        s.enter(i)
    gtok_o[...] = gres[...] + norm_back(acc[...], source, scale, gain_row(misc_w[...], 64))
    for i in SHARED:
        s.second(i)
    for i in QKV:
        s.second(i)
    for i in OUT:
        s.relay(i)
    for i in SHARED:
        s.third(i)
    for i in QKV:
        s.third(i)
    for i in OUT:
        s.second(i)
    for i in SHARED:
        s.spread_rows(i)
    for i in QKV:
        s.spread_rows(i)
    for i in OUT:
        s.third(i)
    for i in OUT:
        s.spread_rows(i)
    s.finish()


def back(gnt, resid, cot, tokens, normed, q, kv, p, att, misc_in, misc_w, shared_grads, weights):
    grads = [g.reshape((2,) + sum_box(i)) for i, g in zip(SHARED, shared_grads)]
    vm = lambda shape, dtype=bf16: pltpu.VMEM(shape, dtype)
    dma = pltpu.SemaphoreType.DMA
    halves = [vm(sum_box(i)) for i in range(N)]
    scratch = halves * 2
    for i in range(N):
        tail = (rows_of(i), SUMS[i])
        scratch += [vm((2, 3) + half_box(ORDERS[i]) + tail), vm((3,) + axis_box(ORDERS[i][0]) + tail), vm((3,) + tail)]
    scratch += [vm((4, 16, w)) for w in SUMS] + halves[:6]
    scratch += [vm((4, TOK, 256)), vm((4, TOK, 256)), vm((4, TOK, 128)), vm((4, TOK, 384)), vm((4, TOK, 384)), vm((D, TOK)), vm((TOK, D), f32), vm((TOK, D), f32), vm((D, 128), f32), vm((4, D, 384)), dma((4, 3))]
    scratch += [dma((N,)), dma((N,)), dma((N,)), dma((N, 2, 3)), dma((N, 2, 3)), dma((N, 2, 3)), dma((N, 2, 3)), dma((N, 3)), dma((N, 3))]
    return pl.pallas_call(
        back_kernel,
        out_shape=[sds((TOK, D), f32)] + [sds((4, 16, w)) for w in SUMS],
        in_specs=[VM] * 11 + [ANY] * 9,
        out_specs=[VM] * 10,
        scratch_shapes=scratch,
        compiler_params=pltpu.CompilerParams(collective_id=2, has_side_effects=True, vmem_limit_bytes=63 << 20),
        name="back",
    )(gnt, resid, cot, tokens, normed, q, kv, p, att, misc_in, misc_w, *grads, *weights)


def final_kernel(*refs):
    gtok, block, gg, gu, gd = refs[:5]
    outs = refs[5:14]
    block_o, gtok_o, gq_o, gk_o, gv_o, go_o, gsg_o, gsu_o, gsd_o, gr_o, g1_o, g2_o, gg_o, gu_o, gd_o = refs[14:]
    for src, dst in ((gtok, gtok_o), (block, block_o), (gg, gg_o), (gu, gu_o), (gd, gd_o)):
        dst[...] = src[...]
    for j in range(4):
        block = [outs[i][j].astype(f32)[: PIECE[i]] for i in range(N)]
        gq_o[:, j * 384 : j * 384 + 256] = block[0]
        gq_o[:, j * 384 + 256 : (j + 1) * 384] = block[1][:, :128]
        gk_o[:, j * 128 : (j + 1) * 128] = block[1][:, 128:]
        gv_o[:, j * 128 : (j + 1) * 128] = block[2]
        for p in range(3):
            go_o[:, j * 384 + p * 128 : j * 384 + (p + 1) * 128] = block[3 + p][:, :128]
        gsg_o[:, j * 256 : (j + 1) * 256] = block[6]
        gsu_o[:, j * 256 : (j + 1) * 256] = block[7]
        gsd_o[:, j * 384 : (j + 1) * 384] = block[8]
    misc = outs[5][0].astype(f32)[:12, 128:]
    gr_o[...] = misc[:, :64]
    eye = iota((12, 12), 0) == iota((12, 12), 1)
    for k, out in ((64, g1_o), (65, g2_o)):
        out[...] = jnp.sum(jnp.where(eye, misc[:, k : k + 1], 0.0), axis=0, keepdims=True)


def final(gtok, block, expert, pieces):
    shapes = ((TOK, D), (12, D), (12, 512), (12, 512), (12, D), (12, 1024), (12, 1024), (8, D), (12, 64), (1, 12), (1, 12), (D, 256), (D, 256), (256, D))
    return pl.pallas_call(
        final_kernel,
        out_shape=[sds((TOK, D))] + [sds(s, f32) for s in shapes],
        in_specs=[VM] * 14,
        out_specs=[VM] * 15,
        compiler_params=pltpu.CompilerParams(vmem_limit_bytes=63 << 20),
        name="final",
    )(gtok, block, *expert, *pieces)


def local(tokens, segment_ids, routes, cotangent, query_weight, key_weight, value_weight, output_weight, shared_gate, shared_up, shared_down, router_weight, first_gain, second_gain, expert_gate, expert_up, expert_down):
    (normed, q, kv, p, att, resid, nt, code, misc_w), weights = front(
        tokens, segment_ids, routes.T, query_weight, key_weight, value_weight, output_weight, router_weight,
        first_gain[None], second_gain[None], shared_gate, shared_up, shared_down,
    )
    mine = [expert_gate[0], expert_up[0], expert_down[0]]
    block, gnt, gmisc, gg, gu, gd, *shared_grads = moe(nt, cotangent, code, resid, misc_w, mine, *weights[6:])
    gtok, *pieces = back(gnt, resid, cotangent, tokens, normed, q, kv, p, att, gmisc, misc_w, shared_grads, weights[:6])
    *outs, g1, g2, gg, gu, gd = final(gtok, block, (gg, gu, gd), pieces)
    return *outs, g1[0], g2[0], gg[None], gu[None], gd[None]


def solution(mesh):
    in_specs = (
        P(("fsdp", "rep"), None),
        P(("fsdp", "rep"), None),
        P(("fsdp", "rep"), None),
        P(("fsdp", "rep"), None),
        P(("fsdp", "rep"), None),
        P(("fsdp", "rep"), None),
        P(("fsdp", "rep"), None),
        P(("fsdp", "rep"), None),
        P(("fsdp", "rep"), None),
        P(("fsdp", "rep"), None),
        P(("fsdp", "rep"), None),
        P(("fsdp", "rep"), None),
        P(("fsdp", "rep")),
        P(("fsdp", "rep")),
        P("fsdp", None, "rep"),
        P("fsdp", None, "rep"),
        P("fsdp", "rep", None),
    )
    out_specs = (
        P(("fsdp", "rep"), None),
        P(("fsdp", "rep"), None),
        P(("fsdp", "rep"), None),
        P(("fsdp", "rep"), None),
        P(("fsdp", "rep"), None),
        P(("fsdp", "rep"), None),
        P(("fsdp", "rep"), None),
        P(("fsdp", "rep"), None),
        P(("fsdp", "rep"), None),
        P(("fsdp", "rep"), None),
        P(("fsdp", "rep")),
        P(("fsdp", "rep")),
        P("fsdp", None, "rep"),
        P("fsdp", None, "rep"),
        P("fsdp", "rep", None),
    )
    return jax.shard_map(local, mesh=mesh, in_specs=in_specs, out_specs=out_specs, check_vma=False)
```

```python
import math

import jax
import jax.numpy as jnp
from jax import lax
from jax.experimental import pallas as pl
from jax.experimental.pallas import tpu as pltpu
from jax.sharding import PartitionSpec as P

MESH = pl.DeviceIdType.MESH
ANY = pl.BlockSpec(memory_space=pl.ANY)
VM = pl.BlockSpec(memory_space=pltpu.VMEM)


def place():
    f, r = lax.axis_index("fsdp"), lax.axis_index("rep")
    return dict(x=(f // 2) % 4, y=2 * r + (f // 8) % 2, z=f // 16, core=f % 2)


def device(at):
    return (((at["z"] * 2 + at["y"] % 2) * 4 + at["x"]) * 2 + at["core"], at["y"] // 2)


def moved(at, axis, by):
    return {**at, axis: (at[axis] + by) % (2 if axis == "core" else 4)}


def region(at, order, done, coordinate=None, half=None):
    first = done[0] if done else None
    spot = {}
    for axis in "xyz":
        whole = axis in done
        at_axis = at[axis]
        if axis == "y":
            if whole:
                spot["yhi"] = (half if (half is not None and first == "y") else slice(None))
                spot["ylo"] = slice(None)
            else:
                spot["yhi"], spot["ylo"] = at_axis // 2, at_axis % 2
        else:
            if whole:
                spot[axis] = pl.ds(2 * half, 2) if (half is not None and first == axis) else slice(None)
            else:
                spot[axis] = at_axis
    return (at["core"], spot["yhi"], spot["z"], spot["ylo"], spot["x"])


D = 1536
TOK = 128
TOP = 6
EXPERTS = 64
CAP = 24
SLOTS = EXPERTS * CAP
CHUNK = 384
epsilon = 1e-06
SCALE = 1.0 / math.sqrt(128)
f32, bf16, i32 = jnp.float32, jnp.bfloat16, jnp.int32


def dot(a, b):
    return jnp.dot(a, b, preferred_element_type=f32)


def dot_t(a, b):
    return lax.dot_general(a, b, (((1,), (1,)), ((), ())), preferred_element_type=f32)


def t_dot(a, b):
    return lax.dot_general(a, b, (((0,), (0,)), ((), ())), preferred_element_type=f32)


def flip(a):
    return a.astype(f32).T.astype(bf16)


def rms_scale(v):
    return lax.rsqrt(jnp.mean(v * v, axis=-1, keepdims=True) + epsilon)


def silu_parts(pre):
    s = jax.nn.sigmoid(pre)
    return pre * s, s * (1.0 + pre * (1.0 - s))


def norm_back(grad, source, scale, gain):
    weighted = grad * gain
    inner = jnp.mean(weighted * source, axis=-1, keepdims=True)
    return scale * weighted - source * (scale * scale * scale) * inner


def iota(shape, dim):
    return lax.broadcasted_iota(i32, shape, dim)


def gain_row(misc, lane):
    pick = (iota((16, 128), 1) == lane).astype(bf16)
    return dot_t(pick, misc)[0:1]


def chosen(routes):
    lanes = iota((TOK, 128), 1)
    hit = jnp.zeros((TOK, 128), f32)
    for k in range(TOP):
        hit = hit + (routes[:, k : k + 1] == lanes).astype(f32)
    return hit


def sds(shape, dtype=bf16):
    return jax.ShapeDtypeStruct(shape, dtype)


ORDERS = ("xyz", "yzx", "zxy") * 3
PIECE = (12, 12, 12, 12, 12, 12, 12, 12, 8)
WIDE = (256, 256, 256, 128, 128, 128, 256, 256, 384)
N = len(ORDERS)
QKV, OUT, SHARED = (0, 1, 2), (3, 4, 5), (6, 7, 8)
STEPS = (1, -1, 2)


def rows_of(i):
    return 4 * PIECE[i]


def core_box(i):
    return (2, 4, 2, 4, rows_of(i), WIDE[i])


def axis_box(axis):
    return (2, 2) if axis == "y" else (4,)


def partner_of(at):
    return {**at, "y": at["y"] + 1 - 2 * (at["y"] % 2)}


def owners(at):
    there = shifted(at, iota((1, SLOTS), 1) // BLOCK, 1)
    expert = ((there["z"] * 2 + at["y"] % 2) * 4 + there["x"]) * 2 + there["core"]
    return (iota((128, SLOTS), 0) == expert).astype(bf16)


class Links:
    def __init__(self):
        self.at = place()
        self.core = self.at["core"]
        self.mine = self.core * 2 + self.at["y"] // 2
        self.sibling = moved(self.at, "core", 1)
        self.peers = [self.sibling, moved(self.at, "y", 2), moved(self.sibling, "y", 2)]
        self.started, self.sent = [], {}
        self.places = {(axis, by): moved(self.at, axis, by) for axis in "xyz" for by in STEPS}
        self.devices = [(to, device(to)) for to in [*self.peers, *self.places.values()]]

    def near(self, axis, by):
        return self.places[axis, (by + 1) % 4 - 1]

    def near_sibling(self, axis, by):
        return {**(self.near(axis, by) if by else self.at), "core": self.sibling["core"]}

    def device_of(self, to):
        for known, number in self.devices:
            if known is to:
                return number
        return device(to)

    def pull(self, refs, held, sems):
        self.pulls = []
        for k, (src, dst) in enumerate(zip(refs, held)):
            self.pulls.append(pltpu.make_async_copy(src, dst, sems.at[k]))
            self.pulls[-1].start()

    def pulled(self):
        for copy in self.pulls:
            copy.wait()

    def greet(self):
        barrier = pltpu.get_barrier_semaphore()
        ring = [self.near(axis, by) for axis in "xyz" for by in STEPS if (axis, by) != ("y", 2)]
        for to in self.peers + ring:
            pl.semaphore_signal(barrier, inc=1, device_id=device(to), device_id_type=MESH)
        pl.semaphore_wait(barrier, len(self.peers) + len(ring))

    def remote(self, src, dst, s, r, to):
        return pltpu.make_async_remote_copy(src_ref=src, dst_ref=dst, send_sem=s, recv_sem=r, device_id=self.device_of(to), device_id_type=MESH)

    def go(self, *args):
        copy = self.remote(*args)
        copy.start()
        self.started.append(copy)
        return copy

    def end(self):
        for copy in self.started:
            copy.wait_send()


class Gather(Links):
    def __init__(self, shards, got, stage, bufs, mix_send, mix_recv, own_sem, send, recv, rsend, rrecv, dsend, drecv):
        super().__init__()
        self.shards, self.got, self.stage, self.bufs = shards, got, stage, bufs
        self.mix_send, self.mix_recv, self.own_sem = mix_send, mix_recv, own_sem
        self.send, self.recv, self.rsend, self.rrecv, self.dsend, self.drecv = send, recv, rsend, rrecv, dsend, drecv

    def here(self, i, done, spot=None, half=None):
        return self.bufs[i].at[region(self.at if spot is None else spot, ORDERS[i], done, half=half)]

    def mix(self, i):
        own = pltpu.make_async_copy(self.shards[i].at[self.mine], self.got[i].at[self.mine], self.own_sem.at[i])
        own.start()
        copies = []
        for k, to in enumerate(self.peers):
            quarter = to["core"] * 2 + to["y"] // 2
            copies.append(self.go(self.shards[i].at[quarter], self.got[i].at[self.mine], self.mix_send.at[i, k], self.mix_recv.at[i, k], to))
        self.sent[i, "mix"] = (own, copies)

    def direct(self, i, phase, src):
        axis, done = ORDERS[i][phase], ORDERS[i][:phase]
        self.sent[i, phase] = [
            self.go(src, self.here(i, done), self.send.at[i, phase, k], self.recv.at[i, phase, k], self.near(axis, by))
            for k, by in enumerate(STEPS)
        ]

    def enter(self, i):
        own, copies = self.sent[i, "mix"]
        own.wait()
        for copy in copies:
            copy.wait_recv()
        size, take = rows_of(i), PIECE[i]
        to_row, from_row = iota((size, 64), 0), iota((size, 64), 1)
        pick = ((to_row // take) * 16 + to_row % take == from_row).astype(bf16)
        self.stage[i][...] = dot(pick, self.got[i][...].reshape(64, WIDE[i])).astype(bf16)
        local = pltpu.make_async_copy(self.stage[i], self.here(i, ""), self.own_sem.at[i])
        local.start()
        self.sent[i, "own"] = local
        self.direct(i, 0, self.stage[i])

    def second(self, i):
        self.sent[i, "own"].wait()
        for copy in self.sent[i, 0]:
            copy.wait_recv()
        self.direct(i, 1, self.here(i, ORDERS[i][:1]))

    def third(self, i):
        for copy in self.sent[i, 1]:
            copy.wait_recv()
        axis, done = ORDERS[i][2], ORDERS[i][:2]
        src = self.here(i, done)
        self.sent[i, 2] = [self.go(src, src, self.rsend.at[i, k], self.rrecv.at[i, k], self.near(axis, STEPS[k])) for k in range(2)]
        self.go(src, src, self.dsend.at[i, 3], self.drecv.at[i, 3], self.sibling)

    def relay(self, i):
        axis, done = ORDERS[i][2], ORDERS[i][:2]
        halves = []
        for k in range(2):
            self.sent[i, 2][k].wait_recv()
            block = self.near(axis, -STEPS[k])
            part = self.here(i, done, block, half=k)
            halves.append(self.go(part, part, self.rsend.at[i, 2 + k], self.rrecv.at[i, 2 + k], self.near(axis, STEPS[k])))
            whole = self.here(i, done, block)
            self.go(whole, whole, self.dsend.at[i, k], self.drecv.at[i, k], self.sibling)
        self.sent[i, "far"] = halves

    def far(self, i):
        for copy in self.sent[i, "far"]:
            copy.wait_recv()
        whole = self.here(i, ORDERS[i][:2], self.near(ORDERS[i][2], 2))
        self.go(whole, whole, self.dsend.at[i, 2], self.drecv.at[i, 2], self.sibling)

    def done(self, i):
        axis, done = ORDERS[i][2], ORDERS[i][:2]
        for k, by in ((3, 0), (0, -1), (1, 1), (2, 2)):
            where = self.here(i, done, self.near_sibling(axis, by))
            self.remote(where, where, self.dsend.at[i, k], self.drecv.at[i, k], self.sibling).wait_recv()


def front_kernel(*refs):
    tokens, seg, routes, w_query, w_key, w_value, w_output, w_router, gain_one, gain_two = refs[:10]
    cot = refs[13]
    results, outs = refs[14:26], refs[26:35]
    normed_o, q_o, kv_o, p_o, att_o, resid_o, nt_o, gates_o, misc_o, hits_o, owner_o, cot_o = made = refs[35:47]
    shards, got, stage = refs[47:56], refs[56:65], refs[65:74]
    held = refs[74:80]
    code_s, code_r, pair_send, pair_recv, made_sem, out_sem, *sems = refs[80:]
    zero = jnp.zeros((4, 16, 384), bf16)
    for shard in shards:
        shard[...] = zero[:, :, : shard.shape[2]]
    eye = iota((12, 12), 0) == iota((12, 12), 1)
    router = w_router[...]
    for j in range(4):
        for p in range(3):
            at_lane = j * 384 + p * 128
            block = w_query[:, at_lane : at_lane + 128]
            if p < 2:
                shards[0][j, :12, p * 128 : (p + 1) * 128] = block
            else:
                shards[1][j, :12, :128] = block
            shards[3 + p][j, :12] = w_output[:, at_lane : at_lane + 128]
        shards[1][j, :12, 128:] = w_key[:, j * 128 : (j + 1) * 128]
        shards[2][j, :12, :128] = w_value[:, j * 128 : (j + 1) * 128]
        shards[2][j, :12, 128:192] = router
        for k, gain in enumerate((gain_one, gain_two)):
            column = jnp.sum(jnp.where(eye, gain[...].astype(f32), 0.0), axis=1, keepdims=True)
            shards[2][j, :12, 192 + k : 193 + k] = column.astype(bf16)
        for i, weight in zip(SHARED, refs[10:13]):
            shards[i][j, : PIECE[i]] = weight[:, j * WIDE[i] : (j + 1) * WIDE[i]]
    g = Gather(shards, got, stage, list(held) + list(outs[6:]), *sems)
    g.greet()
    for i in range(N):
        g.mix(i)
    source = tokens[...].astype(f32)
    row = jnp.broadcast_to(seg[...].astype(f32), (TOK, TOK))
    allowed = (row == row.T) & (iota((TOK, TOK), 1) <= iota((TOK, TOK), 0))
    allowed = jnp.concatenate([allowed.astype(f32)] * 3, axis=0)
    hit = jnp.zeros((TOK, TOK), f32)
    for k in range(TOP):
        hit = hit + (routes[k : k + 1] == iota((TOK, TOK), 0)).astype(f32)
    hit = hit.T
    earlier = (iota((TOK, TOK), 1) < iota((TOK, TOK), 0)).astype(bf16)
    code_s[...] = hit * (dot(earlier, hit.astype(bf16)) + 1.0)
    partner = partner_of(g.at)
    code_copy = g.go(code_s, code_r, pair_send.at[0], pair_recv.at[0], partner)
    scaled = source * rms_scale(source)
    for group in (QKV, OUT):
        for i in group:
            g.enter(i)
    for i in QKV:
        g.second(i)
    for i in QKV:
        g.third(i)
    for i in OUT:
        g.second(i)
    owner_o[...] = owners(g.at)
    spot = iota((1, SLOTS), 1) % BLOCK

    def fill(k, code):
        wide = dot(code.astype(bf16), owner_o[...])
        hits_o[k * TOK : (k + 1) * TOK] = ((wide == (spot - k * CAP + 1).astype(f32)) & (wide > 0)).astype(f32).astype(bf16)

    fill(0, code_s[...])
    for i in QKV:
        g.relay(i)
    for i in OUT:
        g.third(i)
    for i in SHARED:
        g.enter(i)
    for i in QKV:
        g.far(i)
    for i in OUT:
        g.relay(i)
    for i in SHARED:
        g.second(i)
    code_copy.wait_recv()
    fill(1, code_r[...])
    for i in QKV:
        g.done(i)
    cot_copy = g.go(cot, cot_o, pair_send.at[1], pair_recv.at[1], partner)
    for i in SHARED:
        g.third(i)
    keeps = []
    def hand_out(*which):
        for k in which:
            copy = pltpu.make_async_copy(made[k], results[k], made_sem.at[k])
            copy.start()
            keeps.append(copy)

    def weight(i, j):
        return held[i][j // 2, j % 2].reshape(D, WIDE[i])

    def keep(i):
        copy = pltpu.make_async_copy(held[i], outs[i], out_sem.at[i])
        copy.start()
        keeps.append(copy)

    normed_o[...] = (scaled * gain_row(weight(2, 0)[:, 128:], 64)).astype(bf16)
    for i in OUT:
        g.far(i)
    for j in range(4):
        normed = normed_o[...]
        q01 = dot(normed, weight(0, j)).astype(bf16)
        q2k = dot(normed, weight(1, j)).astype(bf16)
        v = dot(normed, weight(2, j)[:, :128]).astype(bf16)
        q_o[j] = jnp.concatenate([q01, q2k[:, :128]], axis=1)
        kv_o[j] = jnp.concatenate([q2k[:, 128:], v], axis=1)
        q3 = jnp.concatenate([q01[:, :128], q01[:, 128:], q2k[:, :128]], axis=0)
        scores = jnp.where(allowed > 0, dot_t(q3, q2k[:, 128:]) * SCALE, -1e30)
        expo = jnp.exp(scores - jnp.max(scores, axis=-1, keepdims=True))
        p = expo / jnp.sum(expo, axis=-1, keepdims=True)
        p_o[j] = p
        mixed = dot(p.astype(bf16), v).astype(bf16)
        att_o[j] = jnp.concatenate([mixed[:128], mixed[128:256], mixed[256:]], axis=1)
        if j == 1:
            for i in SHARED:
                g.relay(i)
        if j == 3:
            for i in SHARED:
                g.far(i)
    for i in QKV:
        keep(i)
    hand_out(0, 1, 2, 3, 4)
    hand_out(9, 10)
    for i in OUT:
        g.done(i)
    attended = jnp.concatenate([att_o[j] for j in range(4)], axis=1)
    for j in range(4):
        for p in range(3):
            cols = slice(j * 384 + p * 128, j * 384 + (p + 1) * 128)
            resid_o[:, cols] = source[:, cols] + dot(attended, weight(3 + p, j))
    for i in OUT:
        keep(i)
    resid = resid_o[...]
    misc = weight(2, 0)[:, 128:]
    misc_o[...] = misc
    nt = (resid * rms_scale(resid) * gain_row(misc, 65)).astype(bf16)
    nt_o[...] = nt
    logits = dot(nt, misc)
    masked = jnp.where(hit > 0, logits, -1e30)
    expo = jnp.where(hit > 0, jnp.exp(masked - jnp.max(masked, axis=-1, keepdims=True)), 0.0)
    gates_o[...] = expo / jnp.sum(expo, axis=-1, keepdims=True)
    cot_copy.wait_recv()
    hand_out(5, 6, 7, 8, 11)
    for i in SHARED:
        g.done(i)
    for copy in keeps:
        copy.wait()
    g.end()


def front(*args):
    dma = pltpu.SemaphoreType.DMA
    full = lambda i: (2,) + core_box(i)
    made = [sds((TOK, D)), sds((4, TOK, 384)), sds((4, TOK, 256)), sds((4, 384, TOK), f32), sds((4, TOK, 384)), sds((TOK, D), f32), sds((TOK, D)), sds((TOK, 128), f32), sds((D, 128)), sds((2 * TOK, SLOTS)), sds((128, SLOTS)), sds((TOK, D))]
    res = pl.pallas_call(
        front_kernel,
        out_shape=made + [sds(full(i)) for i in range(N)],
        in_specs=[VM] * 14,
        out_specs=[ANY] * (12 + N),
        scratch_shapes=[pltpu.VMEM(a.shape, a.dtype) for a in made]
        + [pltpu.VMEM((4, 16, WIDE[i]), bf16) for i in range(N)] * 2
        + [pltpu.VMEM((rows_of(i), WIDE[i]), bf16) for i in range(N)]
        + [pltpu.VMEM(full(i), bf16) for i in QKV + OUT]
        + [pltpu.VMEM((TOK, 128), f32), pltpu.VMEM((TOK, 128), f32), dma((2,)), dma((2,)), dma((12,))]
        + [dma((6,)), dma((N, 3)), dma((N, 3)), dma((N,)), dma((N, 2, 3)), dma((N, 2, 3)), dma((N, 4)), dma((N, 4)), dma((N, 4)), dma((N, 4))],
        compiler_params=pltpu.CompilerParams(collective_id=1, has_side_effects=True, vmem_limit_bytes=60 << 20),
        name="front",
    )(*args)
    return res[:12], [o.reshape(4, 32 * rows_of(i), WIDE[i]) for i, o in enumerate(res[12:])]


STRIDE = 5
PEERS = 32
BLOCK = 2 * CAP
GROUP = CHUNK // BLOCK


def shift_of(s):
    t = (s * STRIDE) % PEERS
    return t // 8, (t // 2) % 4, t % 2


def shifted(at, s, sign):
    dz, dx, dc = shift_of(s)
    other = (at["core"] + dc) % 2
    way = 1 - 2 * at["core"] if sign == 1 else 2 * other - 1
    return {**at, "z": (at["z"] + way * dz + 4) % 4, "x": (at["x"] + way * dx + 4) % 4, "core": other}


def moe_kernel(*refs):
    nt_h, cot_h, cotp_h, resid_h = refs[:4]
    pulls, (sg_h, su_h, sd_h) = refs[4:11], refs[11:14]
    gates_h, router_h, hits_h, owner_h, gm_h, um_h, dm_h = pulls
    out_r, gnt_r, misc_r, gg_h, gu_h, gd_h, gsg_h, gsu_h, gsd_h = refs[14:23]
    gates_r, router_r, hits, owner, gm, um, dm = here = refs[23:30]
    (
        gg_o, gu_o, gd_o, nt2, cot2, gates2, gated, gate_out, gate_in, out_n, out_g, arr_n, arr_g, ret_m, ret_b,
        gx, ux, dx, hid, act_s, slope_s, acc, grecv_a, grecv_b, part_s, part_r, pick_s, pick_r,
        sg_v, su_v, sd_v, shid, ntt, nt_x, cot_x, shid_x, dgate_s, dup_s, dgate_x, dup_x, sib_send, sib_recv,
        pair_send, pair_recv, rep_send, rep_recv, n_send, n_recv, g_send, g_recv, m_send, m_recv, b_send, b_recv,
        gate_send, gate_recv, self_sem, load_sem, pull_sem,
    ) = refs[30:]
    at = place()
    partner = partner_of(at)
    sibling = moved(at, "core", 1)
    twin = moved(at, "y", 2)
    nt_r, cot = nt2.at[0], cot2.at[0]
    first = [
        pltpu.make_async_copy(src, dst, pull_sem.at[k])
        for k, (src, dst) in enumerate([*zip(pulls, here), (nt_h, nt_r), (cot_h, cot), (cotp_h, cot2.at[1])])
    ]
    for copy in first:
        copy.start()
    barrier = pltpu.get_barrier_semaphore()
    for to in (partner, twin):
        pl.semaphore_signal(barrier, inc=1, device_id=device(to), device_id_type=MESH)

    def hello(s, carry):
        pl.semaphore_signal(barrier, inc=1, device_id=device(shifted(at, s, 1)), device_id_type=MESH)
        return carry

    lax.fori_loop(1, PEERS, hello, 0)
    pl.semaphore_wait(barrier, PEERS + 1)

    def remote(src, dst, s, r, to):
        return pltpu.make_async_remote_copy(src_ref=src, dst_ref=dst, send_sem=s, recv_sem=r, device_id=device(to), device_id_type=MESH)

    started = []

    def go(copy):
        copy.start()
        started.append(copy)
        return copy

    pair = [go(remote(src, dst, pair_send.at[k], pair_recv.at[k], partner)) for k, (src, dst) in enumerate(((nt_h, nt2.at[1]), (gates_h, gates2)))]
    swaps = [go(remote(src, dst, rep_send.at[k], rep_recv.at[k], twin)) for k, (src, dst) in enumerate(((gm_h, gx), (um_h, ux), (dm_h, dx)))]

    their_columns = pl.ds(pl.multiple_of((1 - at["core"]) * 768, 128), 768)
    beside = [go(remote(src, dst, sib_send.at[k], sib_recv.at[k], sibling)) for k, (src, dst) in enumerate(((nt_h, nt_x), (cot_h.at[:, their_columns], cot_x)))]
    theirs = pl.ds(2 * (1 - at["core"]), 2)

    def load(src, dst, k):
        copy = pltpu.make_async_copy(src, dst, load_sem.at[k])
        copy.start()
        return copy

    sd_copy = load(sd_h, sd_v, 4)
    loads = {}
    for j in range(2):
        loads[j] = (load(sg_h.at[j], sg_v.at[j], j), load(su_h.at[j], su_v.at[j], 2 + j))
    for copy in first:
        copy.wait()

    def fill(k, gates):
        rows = slice(k * TOK, (k + 1) * TOK)
        gated[rows] = (hits[rows].astype(f32) * dot(gates.astype(bf16), owner[...])).astype(bf16)

    selves = [n_send, g_send, m_send, b_send]

    def send_rows(box, land, c, ssem, rsem, sign):
        def one(s, carry):
            remote(box.at[s], land.at[s], ssem.at[s], rsem.at[s], shifted(at, s, sign)).start()
            return carry
        if c == 0:
            pltpu.make_async_copy(box.at[0], land.at[0], self_sem.at[[k for k, sem in enumerate(selves) if sem is ssem][0]]).start()
        lax.fori_loop(max(1, c * GROUP), (c + 1) * GROUP, one, 0)

    def wait_rows(box, land, c, ssem, rsem, sign, sent):
        def one(s, carry):
            copy = remote(box.at[s], land.at[s], ssem.at[s], rsem.at[s], shifted(at, s, sign))
            if sent:
                copy.wait_send()
            else:
                copy.wait_recv()
            return carry
        if c == 0 and not sent:
            pltpu.make_async_copy(box.at[0], land.at[0], self_sem.at[[k for k, sem in enumerate(selves) if sem is ssem][0]]).wait()
        lax.fori_loop(max(1, c * GROUP), (c + 1) * GROUP, one, 0)

    chunks = range(SLOTS // CHUNK)

    def lanes_of(c):
        return slice(c * CHUNK, (c + 1) * CHUNK)

    def blocks_of(c):
        return slice(c * GROUP, (c + 1) * GROUP)

    def send_cotangents(c, left):
        rows = t_dot(left[:, lanes_of(c)], cot2[...].reshape(2 * TOK, D))
        out_g[blocks_of(c)] = rows.astype(bf16).reshape(GROUP, BLOCK, D)
        send_rows(out_g, arr_g, c, g_send, g_recv, 1)

    send_cotangents(0, hits)
    fill(0, gates_r[...])
    ntt[:, :TOK] = flip(nt_r[...])
    for copy in pair:
        copy.wait_recv()
    fill(1, gates2[...])
    for c in chunks:
        rows = t_dot(hits[:, lanes_of(c)], nt2[...].reshape(2 * TOK, D))
        out_n[blocks_of(c)] = rows.astype(bf16).reshape(GROUP, BLOCK, D)
        send_rows(out_n, arr_n, c, n_send, n_recv, 1)
    gate = t_dot(gated[:, :CHUNK], jnp.ones((2 * TOK, 128), bf16))
    gate_out[...] = gate.astype(bf16).reshape(GROUP, BLOCK, 128)
    gate_in[0] = gate_out[0]
    for s in range(1, GROUP):
        go(remote(gate_out.at[s], gate_in.at[s], gate_send.at[s], gate_recv.at[s], shifted(at, s, 1)))
    for c in chunks[1:]:
        send_cotangents(c, gated)

    sd_copy.wait()
    gh = jnp.zeros((TOK, 1024), f32)
    for j in range(4):
        gh = gh + dot_t(cot[:, j * 384 : (j + 1) * 384], sd_v[j])
    acc[...] = jnp.zeros((2 * TOK, D), f32)
    for j in range(4):
        for copy in loads[j]:
            copy.wait()
        cols = slice(j * 256, (j + 1) * 256)
        gate, up = dot(nt_r[...], sg_v[j % 2]), dot(nt_r[...], su_v[j % 2])
        act, slope = silu_parts(gate)
        shid[:, cols] = (act * up).astype(bf16)
        dgate = dgate_s[j] = (gh[:, cols] * up * slope).astype(bf16)
        dup = dup_s[j] = (gh[:, cols] * act).astype(bf16)
        acc[:TOK] += dot_t(dgate, sg_v[j % 2]) + dot_t(dup, su_v[j % 2])
        if j < 2:
            loads[j + 2] = (load(sg_h.at[j + 2], sg_v.at[j], j), load(su_h.at[j + 2], su_v.at[j], 2 + j))
    gnt_r[...] = acc[:TOK]
    resid_copy = load(resid_h, acc.at[pl.ds(0, TOK)], 5)
    for k, (src, dst) in enumerate(((dgate_s.at[theirs], dgate_x), (dup_s.at[theirs], dup_x), (shid, shid_x))):
        beside.append(go(remote(src, dst, sib_send.at[2 + k], sib_recv.at[2 + k], sibling)))
    resid_copy.wait()
    for j in range(4):
        cols = slice(j * 384, (j + 1) * 384)
        acc[:TOK, cols] += dot(shid[...], sd_v[j])
    acc[TOK:] = jnp.zeros((TOK, D), f32)
    for copy in beside:
        copy.wait_recv()
    ntt[:, TOK:] = flip(nt_x[...])
    shid_t = jnp.concatenate([flip(shid[...]), flip(shid_x[...])], axis=1)
    finals = []
    for k in range(2):
        j = 2 * at["core"] + k
        cols = pl.ds(pl.multiple_of(j * 384, 128), 384)
        sg_v[k] = dot(ntt[...], jnp.concatenate([dgate_s[j], dgate_x[k]], axis=0)).astype(bf16)
        su_v[k] = dot(ntt[...], jnp.concatenate([dup_s[j], dup_x[k]], axis=0)).astype(bf16)
        sd_v[k] = dot(shid_t, jnp.concatenate([cot2[0, :, cols], cot_x[:, k * 384 : (k + 1) * 384]], axis=0)).astype(bf16)
        for i, (src, dst) in enumerate(((sg_v, gsg_h), (su_v, gsu_h), (sd_v, gsd_h))):
            copy = pltpu.make_async_copy(src.at[k], dst.at[k], pull_sem.at[3 * k + i])
            copy.start()
            finals.append(copy)

    for copy in swaps:
        copy.wait_recv()
    halves = ((gm, um, dm), (gx, ux, dx))
    for c in chunks:
        wait_rows(out_n, arr_n, c, n_send, n_recv, 1, False)
        x = arr_n[blocks_of(c)].reshape(CHUNK, D)
        total = None
        for k, (g, u, d) in enumerate(halves):
            cols = slice(k * 256, (k + 1) * 256)
            gate, up = dot(x, g[...]), dot(x, u[...])
            act, slope = silu_parts(gate)
            hidden = (act * up).astype(bf16)
            hid[lanes_of(c), cols] = hidden
            act_s[lanes_of(c), cols] = act.astype(bf16)
            slope_s[lanes_of(c), cols] = (up * slope).astype(bf16)
            part = dot(hidden, d[...])
            total = part if total is None else total + part
        wait_rows(out_n, arr_n, c, n_send, n_recv, 1, True)
        out_n[blocks_of(c)] = total.astype(bf16).reshape(GROUP, BLOCK, D)
        send_rows(out_n, ret_m, c, m_send, m_recv, -1)
    for c in chunks:
        wait_rows(out_g, arr_g, c, g_send, g_recv, 1, False)
        if c == 0:
            for s in range(1, GROUP):
                remote(gate_out.at[s], gate_in.at[s], gate_send.at[s], gate_recv.at[s], shifted(at, s, 1)).wait_recv()
            gate = gate_in[...].reshape(CHUNK, 128)[:, :1].astype(f32)
            slot = (arr_g[blocks_of(0)].reshape(CHUNK, D).astype(f32) * gate).astype(bf16)
            arr_g[blocks_of(0)] = slot.reshape(GROUP, BLOCK, D)
        slot = arr_g[blocks_of(c)].reshape(CHUNK, D)
        total = None
        for k, (g, u, d) in enumerate(halves):
            cols = slice(k * 256, (k + 1) * 256)
            gh = dot_t(slot, d[...])
            dgate = (gh * slope_s[lanes_of(c), cols].astype(f32)).astype(bf16)
            dup = (gh * act_s[lanes_of(c), cols].astype(f32)).astype(bf16)
            slope_s[lanes_of(c), cols], act_s[lanes_of(c), cols] = dgate, dup
            part = dot_t(dgate, g[...]) + dot_t(dup, u[...])
            total = part if total is None else total + part
        wait_rows(out_g, arr_g, c, g_send, g_recv, 1, True)
        out_g[blocks_of(c)] = total.astype(bf16).reshape(GROUP, BLOCK, D)
        send_rows(out_g, ret_b, c, b_send, b_recv, -1)
    for copy in finals:
        copy.wait()
    for b in range(4):
        cols = slice(b * 384, (b + 1) * 384)
        xt = flip(jnp.concatenate([arr_n[blocks_of(c), :, cols].reshape(CHUNK, 384) for c in chunks], axis=0))
        gg = dot(xt, slope_s[...])
        gu = dot(xt, act_s[...])
        gg_o[cols], gu_o[cols] = gg[:, :256], gu[:, :256]
        sg_v[0, cols], sg_v[1, cols] = gg[:, 256:].astype(bf16), gu[:, 256:].astype(bf16)
    trade = [go(remote(sg_v, grecv_a, rep_send.at[3], rep_recv.at[3], twin))]
    hid_t = flip(hid[...])
    for b in range(4):
        cols = slice(b * 384, (b + 1) * 384)
        gd = dot(hid_t, jnp.concatenate([arr_g[blocks_of(c), :, cols].reshape(CHUNK, 384) for c in chunks], axis=0))
        gd_o[:, cols] = gd[:256]
        sd_v[0, b * 256 : (b + 1) * 256] = gd[256:].astype(bf16)
    trade.append(go(remote(sd_v.at[0], grecv_b, rep_send.at[4], rep_recv.at[4], twin)))

    picked = jnp.zeros((2 * TOK, 128), f32)
    for c in chunks:
        wait_rows(out_n, ret_m, c, m_send, m_recv, -1, False)
        rows = ret_m[blocks_of(c)].reshape(CHUNK, D)
        acc[...] += dot(gated[:, lanes_of(c)], rows)
        grads = dot_t(cot2[...].reshape(2 * TOK, D), rows) * hits[:, lanes_of(c)].astype(f32)
        high = grads.astype(bf16)
        low = (grads - high.astype(f32)).astype(bf16)
        own = owner[:, lanes_of(c)]
        picked = picked + dot_t(high, own) + dot_t(low, own)
    part_s[0] = acc[TOK:].astype(bf16)
    pick_s[...] = picked[TOK:]
    pair.append(go(remote(part_s.at[0], part_r.at[0], pair_send.at[2], pair_recv.at[2], partner)))
    pair.append(go(remote(pick_s, pick_r, pair_send.at[3], pair_recv.at[3], partner)))
    pair[2].wait_recv()
    out_r[...] = (acc[:TOK] + part_r[0].astype(f32)).astype(bf16)
    pair[3].wait_recv()
    picked = picked[:TOK] + pick_r[...]
    gates = gates_r[...]
    mean = jnp.sum(gates * picked, axis=-1, keepdims=True)
    gl = (gates * (picked - mean)).astype(bf16)
    misc_r[...] = dot(ntt[:, :TOK], gl)
    acc[:TOK] = gnt_r[...] + dot_t(gl, router_r[...])
    acc[TOK:] = jnp.zeros((TOK, D), f32)
    for c in chunks:
        wait_rows(out_g, ret_b, c, b_send, b_recv, -1, False)
        acc[...] += dot(hits[:, lanes_of(c)], ret_b[blocks_of(c)].reshape(CHUNK, D))
    part_s[1] = acc[TOK:].astype(bf16)
    pair.append(go(remote(part_s.at[1], part_r.at[1], pair_send.at[4], pair_recv.at[4], partner)))
    trade[0].wait_recv()
    gg_o[...] += grecv_a[0].astype(f32)
    gu_o[...] += grecv_a[1].astype(f32)
    trade[1].wait_recv()
    for b in range(4):
        gd_o[:, b * 384 : (b + 1) * 384] += grecv_b[b * 256 : (b + 1) * 256].astype(f32)
    outs = []
    for k, (src, dst) in enumerate(((gg_o, gg_h), (gu_o, gu_h), (gd_o, gd_h))):
        outs.append(pltpu.make_async_copy(src, dst, pull_sem.at[k]))
        outs[-1].start()
    pair[4].wait_recv()
    gnt_r[...] = acc[:TOK] + part_r[1].astype(f32)
    for c in chunks:
        wait_rows(out_n, ret_m, c, m_send, m_recv, -1, True)
        wait_rows(out_g, ret_b, c, b_send, b_recv, -1, True)
    for copy in outs:
        copy.wait()
    for copy in started:
        copy.wait_send()


def moe(nt, cot, cotp, resid, gates, router, hits, owner, mine, sg, su, sd):
    dma = pltpu.SemaphoreType.DMA
    vm = lambda shape, dtype=bf16: pltpu.VMEM(shape, dtype)
    rows = (PEERS, BLOCK, D)
    return pl.pallas_call(
        moe_kernel,
        out_shape=[sds((TOK, D)), sds((TOK, D), f32), sds((D, 128), f32), sds((D, 256), f32), sds((D, 256), f32), sds((256, D), f32)]
        + [sds((2, D, 256)), sds((2, D, 256)), sds((2, 1024, 384))],
        in_specs=[ANY] * 14,
        out_specs=[VM] * 3 + [ANY] * 6,
        scratch_shapes=[vm((TOK, 128), f32), vm((D, 128)), vm((2 * TOK, SLOTS)), vm((128, SLOTS)), vm((D, 256)), vm((D, 256)), vm((256, D))]
        + [vm((D, 256), f32), vm((D, 256), f32), vm((256, D), f32)]
        + [vm((2, TOK, D)), vm((2, TOK, D)), vm((TOK, 128), f32), vm((2 * TOK, SLOTS)), vm((GROUP, BLOCK, 128)), vm((GROUP, BLOCK, 128))]
        + [vm(rows)] * 6
        + [vm((D, 256)), vm((D, 256)), vm((256, D)), vm((SLOTS, 512)), vm((SLOTS, 512)), vm((SLOTS, 512)), vm((2 * TOK, D), f32)]
        + [vm((2, D, 256)), vm((1024, 384)), vm((2, TOK, D)), vm((2, TOK, D)), vm((TOK, 128), f32), vm((TOK, 128), f32)]
        + [vm((2, D, 256)), vm((2, D, 256)), vm((4, 1024, 384)), vm((TOK, 1024)), vm((D, 2 * TOK)), vm((TOK, D)), vm((TOK, 768)), vm((TOK, 1024))]
        + [vm((4, TOK, 256)), vm((4, TOK, 256)), vm((2, TOK, 256)), vm((2, TOK, 256)), dma((5,)), dma((5,))]
        + [dma((5,)), dma((5,)), dma((5,)), dma((5,))] + [dma((PEERS,))] * 8 + [dma((GROUP,)), dma((GROUP,)), dma((4,)), dma((6,)), dma((10,))],
        compiler_params=pltpu.CompilerParams(collective_id=3, has_side_effects=True, vmem_limit_bytes=127 << 19),
        name="moe",
    )(nt, cot, cotp, resid, gates, router, hits, owner, *mine, sg, su, sd)


SUMS = (256, 256, 128, 128, 128, 256, 256, 256, 384)


def sum_box(i):
    return core_box(i)[:5] + (SUMS[i],)


class Scatter(Links):
    def __init__(self, total, landing, spread, outs, own_sem, rsend, rrecv, send, recv, msend, mrecv):
        super().__init__()
        self.total, self.landing, self.spread, self.outs = total, landing, spread, outs
        self.own_sem, self.rsend, self.rrecv = own_sem, rsend, rrecv
        self.send, self.recv, self.msend, self.mrecv = send, recv, msend, mrecv

    def spot(self, i, done, where, half=None):
        return region(where, ORDERS[i], done, half=half)[1:]

    def add(self, i, where, ref, *spots):
        to = self.total[i]
        total = to[where].astype(f32)
        for spot in spots:
            total = total + ref[spot].astype(f32)
        to[where] = total.astype(bf16)

    def start(self, i, src):
        self.sent[i] = pltpu.make_async_copy(src, self.total[i], self.own_sem.at[i])
        self.sent[i].start()

    def message(self, i, side, number):
        axis, done = ORDERS[i][2], ORDERS[i][:2]
        step = STEPS[side]
        spot, k = ((self.near(axis, 2), side), (self.near(axis, step), 1 - side), (self.near(axis, step), side))[number]
        src = self.total[i].at[self.spot(i, done, spot, k)]
        dst = self.landing[i][0].at[side, number]
        self.sent[i, 2, side, number] = self.go(src, dst, self.rsend.at[i, side, number], self.rrecv.at[i, side, number], self.near(axis, step))

    def enter(self, i):
        if i in SHARED:
            self.sent[i].wait()
        for number in range(2):
            for side in range(2):
                self.message(i, side, number)

    def relay(self, i):
        axis, done = ORDERS[i][2], ORDERS[i][:2]
        for side in range(2):
            self.sent[i, 2, side, 0].wait_recv()
            self.add(i, self.spot(i, done, self.near(axis, STEPS[side]), side), self.landing[i][0], (side, 0))
            self.message(i, side, 2)

    def direct(self, i, phase):
        axis, done = ORDERS[i][phase], ORDERS[i][:phase]
        self.sent[i, phase] = [
            self.go(self.total[i].at[self.spot(i, done, self.near(axis, by))], self.landing[i][2 - phase].at[k], self.send.at[i, phase, k], self.recv.at[i, phase, k], self.near(axis, by))
            for k, by in enumerate(STEPS)
        ]

    def second(self, i):
        done = ORDERS[i][:2]
        for side in range(2):
            for number in (1, 2):
                self.sent[i, 2, side, number].wait_recv()
        for k in range(2):
            self.add(i, self.spot(i, done, self.at, k), self.landing[i][0], (k, 2), (1 - k, 1))
        self.direct(i, 1)

    def third(self, i):
        for copy in self.sent[i, 1]:
            copy.wait_recv()
        self.add(i, self.spot(i, ORDERS[i][:1], self.at), self.landing[i][1], 0, 1, 2)
        self.direct(i, 0)

    def spread_rows(self, i):
        for copy in self.sent[i, 0]:
            copy.wait_recv()
        chunk = self.total[i][self.spot(i, "", self.at)].astype(f32)
        for k in range(3):
            chunk = chunk + self.landing[i][2][k].astype(f32)
        size, take = rows_of(i), PIECE[i]
        to_row, from_row = iota((64, size), 0), iota((64, size), 1)
        pick = ((from_row // take) * 16 + from_row % take == to_row).astype(bf16)
        laid = dot(pick, chunk.astype(bf16)).astype(bf16)
        self.spread[i][...] = laid.reshape(4, 16, SUMS[i])
        own = pltpu.make_async_copy(self.spread[i].at[self.mine], self.outs[i].at[self.mine], self.own_sem.at[i])
        own.start()
        finals = [own]
        for k, to in enumerate(self.peers):
            quarter = to["core"] * 2 + to["y"] // 2
            finals.append(self.go(self.spread[i].at[quarter], self.outs[i].at[self.mine], self.msend.at[i, k], self.mrecv.at[i, k], to))
        self.sent[i, "final"] = finals

    def finish(self):
        for i in range(N):
            own, *copies = self.sent[i, "final"]
            own.wait()
            for copy in copies:
                copy.wait_recv()
        self.end()


def half_box(order):
    return {"xyz": (2, 2, 2), "yzx": (4, 2), "zxy": (2, 4)}[order]


def back_kernel(*refs):
    pulls, shared_h, weights = refs[:11], refs[11:14], refs[14:20]
    gtok_o, *outs = refs[20:30]
    total = refs[30:39]
    landing = [refs[39 + 3 * i : 42 + 3 * i] for i in range(N)]
    spread = refs[66:75]
    gnt, resid_r, cot, tokens, normed_r, q_r, kv_r, p_r, att_r, misc_in, misc_w = here = refs[75:86]
    left_s, right_s, gv_s, goo_s, gatt_s, turned, acc, gres, misc_s, slots = refs[86:96]
    normed_x, att_x, goo_x, left_x, right_x, gv_x, misc_x, slot_sem, pull_sem, sib_send, sib_recv, *sems = refs[96:]
    s = Scatter(total, landing, spread, outs, *sems)
    core = s.core
    loads = {}

    def load(j, parts):
        loads[j] = []
        at_lane = 0
        for k, (i, width) in enumerate(parts):
            src = weights[i].at[j] if width == WIDE[i] else weights[i].at[j, :, pl.ds(0, width)]
            copy = pltpu.make_async_copy(src, slots.at[j, :, pl.ds(at_lane, width)], slot_sem.at[j, k])
            copy.start()
            loads[j].append(copy)
            at_lane += width

    def loaded(j):
        for copy in loads[j]:
            copy.wait()

    def weight_grads(group, right):
        for k in range(2):
            for i, value in zip(group, right(2 * core + k, k)):
                total[i][k] = value.astype(bf16).reshape(sum_box(i)[1:])

    def tell(k, src, dst):
        s.sent["told", k] = s.go(src, dst, sib_send.at[k], sib_recv.at[k], s.sibling)

    def told(*which):
        for k in which:
            s.sent["told", k].wait_recv()

    theirs = pl.ds(2 * (1 - core), 2)
    s.pull(pulls, here, pull_sem)
    for i, src in zip(SHARED, shared_h):
        s.start(i, src)
    for j in range(4):
        load(j, [(3, 128), (4, 128), (5, 128)])
    s.greet()
    tell(0, pulls[4], normed_x)
    tell(1, pulls[8], att_x)
    for i in SHARED:
        s.enter(i)
    s.pulled()

    resid = resid_r[...]
    scale = rms_scale(resid)
    grad = gnt[...]
    lane = iota((TOK, 128), 1)
    misc_s[...] = misc_in[...] + t_dot((grad * resid * scale).astype(bf16), (lane == 65).astype(bf16))
    gres[...] = cot[...].astype(f32) + norm_back(grad, resid, scale, gain_row(misc_w[...], 65))
    acc[...] = jnp.zeros((TOK, D), f32)
    for j in range(4):
        goo_s[j] = gres[:, j * 384 : (j + 1) * 384].astype(bf16)
        loaded(j)
        acc[...] += dot_t(goo_s[j], slots[j])
        load(j, [(0, 256), (2, 128)])
    for j in range(4):
        gatt_s[j] = acc[:, j * 384 : (j + 1) * 384].astype(bf16)
    tell(2, goo_s.at[theirs], goo_x)
    turned[:, :TOK] = flip(normed_r[...])
    told(0)
    turned[:, TOK:] = flip(normed_x[...])
    for j in range(4):
        ga, q, kv, p = gatt_s[j], q_r[j], kv_r[j], p_r[j]
        ga3 = jnp.concatenate([ga[:, :128], ga[:, 128:256], ga[:, 256:]], axis=0)
        q3 = jnp.concatenate([q[:, :128], q[:, 128:256], q[:, 256:]], axis=0)
        gp = dot_t(ga3, kv[:, 128:])
        gs = (p * (gp - jnp.sum(p * gp, axis=-1, keepdims=True))).astype(bf16)
        gq3 = (dot(gs, kv[:, :128]) * SCALE).astype(bf16)
        gk = (t_dot(gs, q3) * SCALE).astype(bf16)
        gv_s[j] = t_dot(p.astype(bf16), ga3).astype(bf16)
        left_s[j] = jnp.concatenate([gq3[:128], gq3[128:256]], axis=1)
        right_s[j] = jnp.concatenate([gq3[256:], gk], axis=1)
    tell(3, left_s.at[theirs], left_x)
    tell(4, right_s.at[theirs], right_x)
    tell(5, gv_s.at[theirs], gv_x)
    for i in SHARED:
        s.relay(i)
    told(3, 4, 5)

    def both(mine, other):
        return dot(turned[...], jnp.concatenate([mine, other], axis=0))

    weight_grads(QKV, lambda j, k: (both(left_s[j], left_x[k]), both(right_s[j], right_x[k]), both(gv_s[j], gv_x[k])))
    for i in QKV:
        s.enter(i)
    acc[...] = jnp.zeros((TOK, D), f32)
    for j in range(4):
        loaded(j)
        acc[...] += dot_t(jnp.concatenate([left_s[j], gv_s[j]], axis=1), slots[j])
        load(j, [(1, 256)])
    for j in range(4):
        loaded(j)
        acc[...] += dot_t(right_s[j], slots[j, :, :256])
    source = tokens[...].astype(f32)
    scale = rms_scale(source)
    misc_s[...] += t_dot((acc[...] * source * scale).astype(bf16), (lane == 64).astype(bf16))
    tell(6, misc_s, misc_x)
    told(1, 2)
    for j in range(4):
        turned[j * 384 : (j + 1) * 384, :TOK] = flip(att_r[j])
        turned[j * 384 : (j + 1) * 384, TOK:] = flip(att_x[j])
    told(6)

    def out_grads(j, k):
        whole = both(goo_s[j], goo_x[k])
        misc = (misc_s[...] + misc_x[...]) * jnp.where(j == 0, 1.0, 0.0)
        return whole[:, :128], whole[:, 128:256], jnp.concatenate([whole[:, 256:], misc], axis=1)

    weight_grads(OUT, out_grads)
    for i in QKV:
        s.relay(i)
    for i in OUT:
        s.enter(i)
    gtok_o[...] = gres[...] + norm_back(acc[...], source, scale, gain_row(misc_w[...], 64))
    for i in SHARED:
        s.second(i)
    for i in QKV:
        s.second(i)
    for i in OUT:
        s.relay(i)
    for i in SHARED:
        s.third(i)
    for i in QKV:
        s.third(i)
    for i in OUT:
        s.second(i)
    for i in SHARED:
        s.spread_rows(i)
    for i in QKV:
        s.spread_rows(i)
    for i in OUT:
        s.third(i)
    for i in OUT:
        s.spread_rows(i)
    s.finish()


def back(*args, shared_grads, weights):
    grads = [g.reshape(sum_box(i)) for i, g in zip(SHARED, shared_grads)]
    vm = lambda shape, dtype=bf16: pltpu.VMEM(shape, dtype)
    dma = pltpu.SemaphoreType.DMA
    halves = [vm(sum_box(i)) for i in range(N)]
    scratch = list(halves)
    for i in range(N):
        tail = (rows_of(i), SUMS[i])
        scratch += [vm((2, 3) + half_box(ORDERS[i]) + tail), vm((3,) + axis_box(ORDERS[i][0]) + tail), vm((3,) + tail)]
    scratch += [vm((4, 16, w)) for w in SUMS]
    scratch += [vm(a.shape, a.dtype) for a in args]
    scratch += [vm((4, TOK, 256)), vm((4, TOK, 256)), vm((4, TOK, 128)), vm((4, TOK, 384)), vm((4, TOK, 384)), vm((D, 2 * TOK)), vm((TOK, D), f32), vm((TOK, D), f32), vm((D, 128), f32), vm((4, D, 384))]
    scratch += [vm((TOK, D)), vm((4, TOK, 384)), vm((2, TOK, 384)), vm((2, TOK, 256)), vm((2, TOK, 256)), vm((2, TOK, 128)), vm((D, 128), f32), dma((4, 3)), dma((11,)), dma((7,)), dma((7,))]
    scratch += [dma((N,)), dma((N, 2, 3)), dma((N, 2, 3)), dma((N, 2, 3)), dma((N, 2, 3)), dma((N, 3)), dma((N, 3))]
    return pl.pallas_call(
        back_kernel,
        out_shape=[sds((TOK, D), f32)] + [sds((4, 16, w)) for w in SUMS],
        in_specs=[ANY] * 20,
        out_specs=[VM] * 10,
        scratch_shapes=scratch,
        compiler_params=pltpu.CompilerParams(collective_id=2, has_side_effects=True, vmem_limit_bytes=63 << 20),
        name="back",
    )(*args, *grads, *weights)


def final_kernel(*refs):
    gtok, block, gg, gu, gd = refs[:5]
    outs = refs[5:14]
    block_o, gtok_o, gq_o, gk_o, gv_o, go_o, gsg_o, gsu_o, gsd_o, gr_o, g1_o, g2_o, gg_o, gu_o, gd_o = refs[14:]
    for src, dst in ((gtok, gtok_o), (block, block_o), (gg, gg_o), (gu, gu_o), (gd, gd_o)):
        dst[...] = src[...]
    for j in range(4):
        block = [outs[i][j].astype(f32)[: PIECE[i]] for i in range(N)]
        gq_o[:, j * 384 : j * 384 + 256] = block[0]
        gq_o[:, j * 384 + 256 : (j + 1) * 384] = block[1][:, :128]
        gk_o[:, j * 128 : (j + 1) * 128] = block[1][:, 128:]
        gv_o[:, j * 128 : (j + 1) * 128] = block[2]
        for p in range(3):
            go_o[:, j * 384 + p * 128 : j * 384 + (p + 1) * 128] = block[3 + p][:, :128]
        gsg_o[:, j * 256 : (j + 1) * 256] = block[6]
        gsu_o[:, j * 256 : (j + 1) * 256] = block[7]
        gsd_o[:, j * 384 : (j + 1) * 384] = block[8]
    misc = outs[5][0].astype(f32)[:12, 128:]
    gr_o[...] = misc[:, :64]
    eye = iota((12, 12), 0) == iota((12, 12), 1)
    for k, out in ((64, g1_o), (65, g2_o)):
        out[...] = jnp.sum(jnp.where(eye, misc[:, k : k + 1], 0.0), axis=0, keepdims=True)


def final(gtok, block, expert, pieces):
    shapes = ((TOK, D), (12, D), (12, 512), (12, 512), (12, D), (12, 1024), (12, 1024), (8, D), (12, 64), (1, 12), (1, 12), (D, 256), (D, 256), (256, D))
    return pl.pallas_call(
        final_kernel,
        out_shape=[sds((TOK, D))] + [sds(s, f32) for s in shapes],
        in_specs=[VM] * 14,
        out_specs=[VM] * 15,
        compiler_params=pltpu.CompilerParams(vmem_limit_bytes=63 << 20),
        name="final",
    )(gtok, block, *expert, *pieces)


def local(tokens, segment_ids, routes, cotangent, query_weight, key_weight, value_weight, output_weight, shared_gate, shared_up, shared_down, router_weight, first_gain, second_gain, expert_gate, expert_up, expert_down):
    (normed, q, kv, p, att, resid, nt, gates, misc_w, hits, owner, cotp), weights = front(
        tokens, segment_ids, routes.T, query_weight, key_weight, value_weight, output_weight, router_weight,
        first_gain[None], second_gain[None], shared_gate, shared_up, shared_down, cotangent,
    )
    mine = [expert_gate[0], expert_up[0], expert_down[0]]
    block, gnt, gmisc, gg, gu, gd, *shared_grads = moe(
        nt, cotangent, cotp, resid, gates, misc_w, hits, owner, mine, *weights[6:]
    )
    gtok, *pieces = back(
        gnt, resid, cotangent, tokens, normed, q, kv, p, att, gmisc, misc_w, shared_grads=shared_grads, weights=weights[:6]
    )
    *outs, g1, g2, gg, gu, gd = final(gtok, block, (gg, gu, gd), pieces)
    return *outs, g1[0], g2[0], gg[None], gu[None], gd[None]


def solution(mesh):
    in_specs = (
        P(("fsdp", "rep"), None),
        P(("fsdp", "rep"), None),
        P(("fsdp", "rep"), None),
        P(("fsdp", "rep"), None),
        P(("fsdp", "rep"), None),
        P(("fsdp", "rep"), None),
        P(("fsdp", "rep"), None),
        P(("fsdp", "rep"), None),
        P(("fsdp", "rep"), None),
        P(("fsdp", "rep"), None),
        P(("fsdp", "rep"), None),
        P(("fsdp", "rep"), None),
        P(("fsdp", "rep")),
        P(("fsdp", "rep")),
        P("fsdp", None, "rep"),
        P("fsdp", None, "rep"),
        P("fsdp", "rep", None),
    )
    out_specs = (
        P(("fsdp", "rep"), None),
        P(("fsdp", "rep"), None),
        P(("fsdp", "rep"), None),
        P(("fsdp", "rep"), None),
        P(("fsdp", "rep"), None),
        P(("fsdp", "rep"), None),
        P(("fsdp", "rep"), None),
        P(("fsdp", "rep"), None),
        P(("fsdp", "rep"), None),
        P(("fsdp", "rep"), None),
        P(("fsdp", "rep")),
        P(("fsdp", "rep")),
        P("fsdp", None, "rep"),
        P("fsdp", None, "rep"),
        P("fsdp", "rep", None),
    )
    return jax.shard_map(local, mesh=mesh, in_specs=in_specs, out_specs=out_specs, check_vma=False)
```

```python
import math

import jax
import jax.numpy as jnp
from jax import lax
from jax.experimental import pallas as pl
from jax.experimental.pallas import tpu as pltpu
from jax.sharding import PartitionSpec as P

MESH = pl.DeviceIdType.MESH
ANY = pl.BlockSpec(memory_space=pl.ANY)
VM = pl.BlockSpec(memory_space=pltpu.VMEM)


def place():
    f, r = lax.axis_index("fsdp"), lax.axis_index("rep")
    return dict(x=(f // 2) % 4, y=2 * r + (f // 8) % 2, z=f // 16, core=f % 2)


def device(at):
    return (((at["z"] * 2 + at["y"] % 2) * 4 + at["x"]) * 2 + at["core"], at["y"] // 2)


def moved(at, axis, by):
    return {**at, axis: (at[axis] + by) % (2 if axis == "core" else 4)}


def region(at, order, done, coordinate=None, half=None):
    first = done[0] if done else None
    spot = {}
    for axis in "xyz":
        whole = axis in done
        at_axis = at[axis]
        if axis == "y":
            if whole:
                spot["yhi"] = (half if (half is not None and first == "y") else slice(None))
                spot["ylo"] = slice(None)
            else:
                spot["yhi"], spot["ylo"] = at_axis // 2, at_axis % 2
        else:
            if whole:
                spot[axis] = pl.ds(2 * half, 2) if (half is not None and first == axis) else slice(None)
            else:
                spot[axis] = at_axis
    return (at["core"], spot["yhi"], spot["z"], spot["ylo"], spot["x"])


D = 1536
TOK = 128
TOP = 6
EXPERTS = 64
CAP = 24
SLOTS = EXPERTS * CAP
CHUNK = 384
epsilon = 1e-06
SCALE = 1.0 / math.sqrt(128)
f32, bf16, i32 = jnp.float32, jnp.bfloat16, jnp.int32


def dot(a, b):
    return jnp.dot(a, b, preferred_element_type=f32)


def dot_t(a, b):
    return lax.dot_general(a, b, (((1,), (1,)), ((), ())), preferred_element_type=f32)


def t_dot(a, b):
    return lax.dot_general(a, b, (((0,), (0,)), ((), ())), preferred_element_type=f32)


def flip(a):
    return a.astype(f32).T.astype(bf16)


def rms_scale(v):
    return lax.rsqrt(jnp.mean(v * v, axis=-1, keepdims=True) + epsilon)


def silu_parts(pre):
    s = jax.nn.sigmoid(pre)
    return pre * s, s * (1.0 + pre * (1.0 - s))


def norm_back(grad, source, scale, gain):
    weighted = grad * gain
    inner = jnp.mean(weighted * source, axis=-1, keepdims=True)
    return scale * weighted - source * (scale * scale * scale) * inner


def iota(shape, dim):
    return lax.broadcasted_iota(i32, shape, dim)


def gain_row(misc, lane):
    pick = (iota((16, 128), 1) == lane).astype(bf16)
    return dot_t(pick, misc)[0:1]


def chosen(routes):
    lanes = iota((TOK, 128), 1)
    hit = jnp.zeros((TOK, 128), f32)
    for k in range(TOP):
        hit = hit + (routes[:, k : k + 1] == lanes).astype(f32)
    return hit


def sds(shape, dtype=bf16):
    return jax.ShapeDtypeStruct(shape, dtype)


ORDERS = ("xyz", "yzx", "zxy") * 3
PIECE = (12, 12, 12, 12, 12, 12, 12, 12, 8)
WIDE = (256, 256, 256, 128, 128, 128, 256, 256, 384)
N = len(ORDERS)
QKV, OUT, SHARED = (0, 1, 2), (3, 4, 5), (6, 7, 8)
STEPS = (1, -1, 2)


def rows_of(i):
    return 4 * PIECE[i]


def core_box(i):
    return (2, 4, 2, 4, rows_of(i), WIDE[i])


def axis_box(axis):
    return (2, 2) if axis == "y" else (4,)


def partner_of(at):
    return {**at, "y": at["y"] + 1 - 2 * (at["y"] % 2)}


def owners(at):
    there = shifted(at, iota((1, SLOTS), 1) // BLOCK, 1)
    expert = ((there["z"] * 2 + at["y"] % 2) * 4 + there["x"]) * 2 + there["core"]
    return (iota((128, SLOTS), 0) == expert).astype(bf16)


class Links:
    def __init__(self):
        self.at = place()
        self.core = self.at["core"]
        self.mine = self.core * 2 + self.at["y"] // 2
        self.sibling = moved(self.at, "core", 1)
        self.peers = [self.sibling, moved(self.at, "y", 2), moved(self.sibling, "y", 2)]
        self.started, self.sent = [], {}
        self.places = {(axis, by): moved(self.at, axis, by) for axis in "xyz" for by in STEPS}
        self.devices = [(to, device(to)) for to in [*self.peers, *self.places.values()]]

    def near(self, axis, by):
        return self.places[axis, (by + 1) % 4 - 1]

    def near_sibling(self, axis, by):
        return {**(self.near(axis, by) if by else self.at), "core": self.sibling["core"]}

    def device_of(self, to):
        for known, number in self.devices:
            if known is to:
                return number
        return device(to)

    def pull(self, refs, held, sems):
        self.pulls = []
        for k, (src, dst) in enumerate(zip(refs, held)):
            self.pulls.append(pltpu.make_async_copy(src, dst, sems.at[k]))
            self.pulls[-1].start()

    def pulled(self):
        for copy in self.pulls:
            copy.wait()

    def greet(self):
        barrier = pltpu.get_barrier_semaphore()
        ring = [self.near(axis, by) for axis in "xyz" for by in STEPS if (axis, by) != ("y", 2)]
        for to in self.peers + ring:
            pl.semaphore_signal(barrier, inc=1, device_id=device(to), device_id_type=MESH)
        pl.semaphore_wait(barrier, len(self.peers) + len(ring))

    def remote(self, src, dst, s, r, to):
        return pltpu.make_async_remote_copy(src_ref=src, dst_ref=dst, send_sem=s, recv_sem=r, device_id=self.device_of(to), device_id_type=MESH)

    def go(self, *args):
        copy = self.remote(*args)
        copy.start()
        self.started.append(copy)
        return copy

    def end(self):
        for copy in self.started:
            copy.wait_send()


class Gather(Links):
    def __init__(self, shards, got, stage, bufs, mix_send, mix_recv, own_sem, send, recv, rsend, rrecv, dsend, drecv):
        super().__init__()
        self.shards, self.got, self.stage, self.bufs = shards, got, stage, bufs
        self.mix_send, self.mix_recv, self.own_sem = mix_send, mix_recv, own_sem
        self.send, self.recv, self.rsend, self.rrecv, self.dsend, self.drecv = send, recv, rsend, rrecv, dsend, drecv

    def here(self, i, done, spot=None, half=None):
        return self.bufs[i].at[region(self.at if spot is None else spot, ORDERS[i], done, half=half)]

    def mix(self, i):
        own = pltpu.make_async_copy(self.shards[i].at[self.mine], self.got[i].at[self.mine], self.own_sem.at[i])
        own.start()
        copies = []
        for k, to in enumerate(self.peers):
            quarter = to["core"] * 2 + to["y"] // 2
            copies.append(self.go(self.shards[i].at[quarter], self.got[i].at[self.mine], self.mix_send.at[i, k], self.mix_recv.at[i, k], to))
        self.sent[i, "mix"] = (own, copies)

    def direct(self, i, phase, src):
        axis, done = ORDERS[i][phase], ORDERS[i][:phase]
        self.sent[i, phase] = [
            self.go(src, self.here(i, done), self.send.at[i, phase, k], self.recv.at[i, phase, k], self.near(axis, by))
            for k, by in enumerate(STEPS)
        ]

    def enter(self, i):
        own, copies = self.sent[i, "mix"]
        own.wait()
        for copy in copies:
            copy.wait_recv()
        size, take = rows_of(i), PIECE[i]
        to_row, from_row = iota((size, 64), 0), iota((size, 64), 1)
        pick = ((to_row // take) * 16 + to_row % take == from_row).astype(bf16)
        self.stage[i][...] = dot(pick, self.got[i][...].reshape(64, WIDE[i])).astype(bf16)
        local = pltpu.make_async_copy(self.stage[i], self.here(i, ""), self.own_sem.at[i])
        local.start()
        self.sent[i, "own"] = local
        self.direct(i, 0, self.stage[i])

    def second(self, i):
        self.sent[i, "own"].wait()
        for copy in self.sent[i, 0]:
            copy.wait_recv()
        self.direct(i, 1, self.here(i, ORDERS[i][:1]))

    def third(self, i):
        for copy in self.sent[i, 1]:
            copy.wait_recv()
        axis, done = ORDERS[i][2], ORDERS[i][:2]
        src = self.here(i, done)
        self.sent[i, 2] = [self.go(src, src, self.rsend.at[i, k], self.rrecv.at[i, k], self.near(axis, STEPS[k])) for k in range(2)]
        self.go(src, src, self.dsend.at[i, 3], self.drecv.at[i, 3], self.sibling)

    def relay(self, i):
        axis, done = ORDERS[i][2], ORDERS[i][:2]
        halves = []
        for k in range(2):
            self.sent[i, 2][k].wait_recv()
            block = self.near(axis, -STEPS[k])
            part = self.here(i, done, block, half=k)
            halves.append(self.go(part, part, self.rsend.at[i, 2 + k], self.rrecv.at[i, 2 + k], self.near(axis, STEPS[k])))
            whole = self.here(i, done, block)
            self.go(whole, whole, self.dsend.at[i, k], self.drecv.at[i, k], self.sibling)
        self.sent[i, "far"] = halves

    def far(self, i):
        for copy in self.sent[i, "far"]:
            copy.wait_recv()
        whole = self.here(i, ORDERS[i][:2], self.near(ORDERS[i][2], 2))
        self.go(whole, whole, self.dsend.at[i, 2], self.drecv.at[i, 2], self.sibling)

    def done(self, i):
        axis, done = ORDERS[i][2], ORDERS[i][:2]
        for k, by in ((3, 0), (0, -1), (1, 1), (2, 2)):
            where = self.here(i, done, self.near_sibling(axis, by))
            self.remote(where, where, self.dsend.at[i, k], self.drecv.at[i, k], self.sibling).wait_recv()


def front_kernel(*refs):
    tokens, seg, routes, w_query, w_key, w_value, w_output, w_router, gain_one, gain_two = refs[:10]
    cot = refs[13]
    results, outs = refs[14:26], refs[26:35]
    normed_o, q_o, kv_o, p_o, att_o, resid_o, nt_o, gates_o, misc_o, hits_o, owner_o, cot_o = made = refs[35:47]
    shards, got, stage = refs[47:56], refs[56:65], refs[65:74]
    held = refs[74:80]
    code_s, code_r, pair_send, pair_recv, made_sem, out_sem, *sems = refs[80:]
    zero = jnp.zeros((4, 16, 384), bf16)
    for shard in shards:
        shard[...] = zero[:, :, : shard.shape[2]]
    eye = iota((12, 12), 0) == iota((12, 12), 1)
    router = w_router[...]
    for j in range(4):
        for p in range(3):
            at_lane = j * 384 + p * 128
            block = w_query[:, at_lane : at_lane + 128]
            if p < 2:
                shards[0][j, :12, p * 128 : (p + 1) * 128] = block
            else:
                shards[1][j, :12, :128] = block
            shards[3 + p][j, :12] = w_output[:, at_lane : at_lane + 128]
        shards[1][j, :12, 128:] = w_key[:, j * 128 : (j + 1) * 128]
        shards[2][j, :12, :128] = w_value[:, j * 128 : (j + 1) * 128]
        shards[2][j, :12, 128:192] = router
        for k, gain in enumerate((gain_one, gain_two)):
            column = jnp.sum(jnp.where(eye, gain[...].astype(f32), 0.0), axis=1, keepdims=True)
            shards[2][j, :12, 192 + k : 193 + k] = column.astype(bf16)
        for i, weight in zip(SHARED, refs[10:13]):
            shards[i][j, : PIECE[i]] = weight[:, j * WIDE[i] : (j + 1) * WIDE[i]]
    g = Gather(shards, got, stage, list(held) + list(outs[6:]), *sems)
    g.greet()
    for i in range(N):
        g.mix(i)
    source = tokens[...].astype(f32)
    row = jnp.broadcast_to(seg[...].astype(f32), (TOK, TOK))
    allowed = (row == row.T) & (iota((TOK, TOK), 1) <= iota((TOK, TOK), 0))
    allowed = jnp.concatenate([allowed.astype(f32)] * 3, axis=0)
    hit = jnp.zeros((TOK, TOK), f32)
    for k in range(TOP):
        hit = hit + (routes[k : k + 1] == iota((TOK, TOK), 0)).astype(f32)
    hit = hit.T
    earlier = (iota((TOK, TOK), 1) < iota((TOK, TOK), 0)).astype(bf16)
    code_s[...] = hit * (dot(earlier, hit.astype(bf16)) + 1.0)
    partner = partner_of(g.at)
    code_copy = g.go(code_s, code_r, pair_send.at[0], pair_recv.at[0], partner)
    scaled = source * rms_scale(source)
    for group in (QKV, OUT, SHARED):
        for i in group:
            g.enter(i)
    for i in QKV:
        g.second(i)
    for i in QKV:
        g.third(i)
    for group in (OUT, SHARED):
        for i in group:
            g.second(i)
    owner_o[...] = owners(g.at)
    spot = iota((1, SLOTS), 1) % BLOCK

    def fill(k, code):
        wide = dot(code.astype(bf16), owner_o[...])
        hits_o[k * TOK : (k + 1) * TOK] = ((wide == (spot - k * CAP + 1).astype(f32)) & (wide > 0)).astype(f32).astype(bf16)

    fill(0, code_s[...])
    for i in QKV:
        g.relay(i)
    for group in (OUT, SHARED):
        for i in group:
            g.third(i)
    for i in QKV:
        g.far(i)
    for i in OUT:
        g.relay(i)
    code_copy.wait_recv()
    fill(1, code_r[...])
    for i in QKV:
        g.done(i)
    keeps = []
    def hand_out(*which):
        for k in which:
            copy = pltpu.make_async_copy(made[k], results[k], made_sem.at[k])
            copy.start()
            keeps.append(copy)

    def weight(i, j):
        return held[i][j // 2, j % 2].reshape(D, WIDE[i])

    def keep(i):
        copy = pltpu.make_async_copy(held[i], outs[i], out_sem.at[i])
        copy.start()
        keeps.append(copy)

    normed_o[...] = (scaled * gain_row(weight(2, 0)[:, 128:], 64)).astype(bf16)
    for i in OUT:
        g.far(i)
    for j in range(4):
        normed = normed_o[...]
        q01 = dot(normed, weight(0, j)).astype(bf16)
        q2k = dot(normed, weight(1, j)).astype(bf16)
        v = dot(normed, weight(2, j)[:, :128]).astype(bf16)
        q_o[j] = jnp.concatenate([q01, q2k[:, :128]], axis=1)
        kv_o[j] = jnp.concatenate([q2k[:, 128:], v], axis=1)
        q3 = jnp.concatenate([q01[:, :128], q01[:, 128:], q2k[:, :128]], axis=0)
        scores = jnp.where(allowed > 0, dot_t(q3, q2k[:, 128:]) * SCALE, -1e30)
        expo = jnp.exp(scores - jnp.max(scores, axis=-1, keepdims=True))
        p = expo / jnp.sum(expo, axis=-1, keepdims=True)
        p_o[j] = p
        mixed = dot(p.astype(bf16), v).astype(bf16)
        att_o[j] = jnp.concatenate([mixed[:128], mixed[128:256], mixed[256:]], axis=1)
        if j == 0:
            for i in SHARED:
                g.relay(i)
            cot_copy = g.go(cot, cot_o, pair_send.at[1], pair_recv.at[1], partner)
        if j == 3:
            for i in SHARED:
                g.far(i)
    for i in QKV:
        keep(i)
    hand_out(0, 1, 2, 3, 4)
    hand_out(9, 10)
    for i in OUT:
        g.done(i)
    attended = jnp.concatenate([att_o[j] for j in range(4)], axis=1)
    for j in range(4):
        for p in range(3):
            cols = slice(j * 384 + p * 128, j * 384 + (p + 1) * 128)
            resid_o[:, cols] = source[:, cols] + dot(attended, weight(3 + p, j))
    for i in OUT:
        keep(i)
    resid = resid_o[...]
    misc = weight(2, 0)[:, 128:]
    misc_o[...] = misc
    nt = (resid * rms_scale(resid) * gain_row(misc, 65)).astype(bf16)
    nt_o[...] = nt
    logits = dot(nt, misc)
    masked = jnp.where(hit > 0, logits, -1e30)
    expo = jnp.where(hit > 0, jnp.exp(masked - jnp.max(masked, axis=-1, keepdims=True)), 0.0)
    gates_o[...] = expo / jnp.sum(expo, axis=-1, keepdims=True)
    cot_copy.wait_recv()
    hand_out(5, 6, 7, 8, 11)
    for i in SHARED:
        g.done(i)
    for copy in keeps:
        copy.wait()
    g.end()


def front(*args):
    dma = pltpu.SemaphoreType.DMA
    full = lambda i: (2,) + core_box(i)
    made = [sds((TOK, D)), sds((4, TOK, 384)), sds((4, TOK, 256)), sds((4, 384, TOK), f32), sds((4, TOK, 384)), sds((TOK, D), f32), sds((TOK, D)), sds((TOK, 128), f32), sds((D, 128)), sds((2 * TOK, SLOTS)), sds((128, SLOTS)), sds((TOK, D))]
    res = pl.pallas_call(
        front_kernel,
        out_shape=made + [sds(full(i)) for i in range(N)],
        in_specs=[VM] * 14,
        out_specs=[ANY] * (12 + N),
        scratch_shapes=[pltpu.VMEM(a.shape, a.dtype) for a in made]
        + [pltpu.VMEM((4, 16, WIDE[i]), bf16) for i in range(N)] * 2
        + [pltpu.VMEM((rows_of(i), WIDE[i]), bf16) for i in range(N)]
        + [pltpu.VMEM(full(i), bf16) for i in QKV + OUT]
        + [pltpu.VMEM((TOK, 128), f32), pltpu.VMEM((TOK, 128), f32), dma((2,)), dma((2,)), dma((12,))]
        + [dma((6,)), dma((N, 3)), dma((N, 3)), dma((N,)), dma((N, 2, 3)), dma((N, 2, 3)), dma((N, 4)), dma((N, 4)), dma((N, 4)), dma((N, 4))],
        compiler_params=pltpu.CompilerParams(collective_id=1, has_side_effects=True, vmem_limit_bytes=60 << 20),
        name="front",
    )(*args)
    return res[:12], [o.reshape(4, 32 * rows_of(i), WIDE[i]) for i, o in enumerate(res[12:])]


STRIDE = 5
PEERS = 32
BLOCK = 2 * CAP
GROUP = CHUNK // BLOCK


def shift_of(s):
    t = (s * STRIDE) % PEERS
    return t // 8, (t // 2) % 4, t % 2


def shifted(at, s, sign):
    dz, dx, dc = shift_of(s)
    other = (at["core"] + dc) % 2
    way = 1 - 2 * at["core"] if sign == 1 else 2 * other - 1
    return {**at, "z": (at["z"] + way * dz + 4) % 4, "x": (at["x"] + way * dx + 4) % 4, "core": other}


def moe_kernel(*refs):
    nt_h, cot_h, cotp_h, resid_h = refs[:4]
    pulls, (sg_h, su_h, sd_h) = refs[4:11], refs[11:14]
    gates_h, router_h, hits_h, owner_h, gm_h, um_h, dm_h = pulls
    out_r, gnt_r, misc_r, gg_h, gu_h, gd_h, gsg_h, gsu_h, gsd_h = refs[14:23]
    gates_r, router_r, hits, owner, gm, um, dm = here = refs[23:30]
    (
        gg_o, gu_o, gd_o, nt2, cot2, gates2, gated, gate_out, gate_in, out_n, out_g, arr_n, arr_g, ret_m, ret_b,
        gx, ux, dx, hid, act_s, slope_s, acc, grecv_a, grecv_b, part_s, part_r, pick_s, pick_r,
        sg_v, su_v, sd_v, shid, ntt, nt_x, cot_x, shid_x, dgate_s, dup_s, dgate_x, dup_x, sib_send, sib_recv,
        pair_send, pair_recv, rep_send, rep_recv, n_send, n_recv, g_send, g_recv, m_send, m_recv, b_send, b_recv,
        gate_send, gate_recv, self_sem, load_sem, pull_sem,
    ) = refs[30:]
    at = place()
    partner = partner_of(at)
    sibling = moved(at, "core", 1)
    twin = moved(at, "y", 2)
    nt_r, cot = nt2.at[0], cot2.at[0]
    first = [
        pltpu.make_async_copy(src, dst, pull_sem.at[k])
        for k, (src, dst) in enumerate([*zip(pulls, here), (nt_h, nt_r), (cot_h, cot), (cotp_h, cot2.at[1])])
    ]
    for copy in first:
        copy.start()
    barrier = pltpu.get_barrier_semaphore()
    for to in (partner, twin):
        pl.semaphore_signal(barrier, inc=1, device_id=device(to), device_id_type=MESH)

    def hello(s, carry):
        pl.semaphore_signal(barrier, inc=1, device_id=device(shifted(at, s, 1)), device_id_type=MESH)
        return carry

    lax.fori_loop(1, PEERS, hello, 0)
    pl.semaphore_wait(barrier, PEERS + 1)

    def remote(src, dst, s, r, to):
        return pltpu.make_async_remote_copy(src_ref=src, dst_ref=dst, send_sem=s, recv_sem=r, device_id=device(to), device_id_type=MESH)

    started = []

    def go(copy):
        copy.start()
        started.append(copy)
        return copy

    pair = [go(remote(src, dst, pair_send.at[k], pair_recv.at[k], partner)) for k, (src, dst) in enumerate(((nt_h, nt2.at[1]), (gates_h, gates2)))]
    swaps = [go(remote(src, dst, rep_send.at[k], rep_recv.at[k], twin)) for k, (src, dst) in enumerate(((gm_h, gx), (um_h, ux), (dm_h, dx)))]

    their_columns = pl.ds(pl.multiple_of((1 - at["core"]) * 768, 128), 768)
    beside = [go(remote(src, dst, sib_send.at[k], sib_recv.at[k], sibling)) for k, (src, dst) in enumerate(((nt_h, nt_x), (cot_h.at[:, their_columns], cot_x)))]
    theirs = pl.ds(2 * (1 - at["core"]), 2)

    def load(src, dst, k):
        copy = pltpu.make_async_copy(src, dst, load_sem.at[k])
        copy.start()
        return copy

    sd_copy = load(sd_h, sd_v, 4)
    loads = {}
    for j in range(2):
        loads[j] = (load(sg_h.at[j], sg_v.at[j], j), load(su_h.at[j], su_v.at[j], 2 + j))
    for copy in first:
        copy.wait()

    def fill(k, gates):
        rows = slice(k * TOK, (k + 1) * TOK)
        gated[rows] = (hits[rows].astype(f32) * dot(gates.astype(bf16), owner[...])).astype(bf16)

    selves = [n_send, g_send, m_send, b_send]

    def send_rows(box, land, c, ssem, rsem, sign):
        def one(s, carry):
            remote(box.at[s], land.at[s], ssem.at[s], rsem.at[s], shifted(at, s, sign)).start()
            return carry
        if c == 0:
            pltpu.make_async_copy(box.at[0], land.at[0], self_sem.at[[k for k, sem in enumerate(selves) if sem is ssem][0]]).start()
        lax.fori_loop(max(1, c * GROUP), (c + 1) * GROUP, one, 0)

    def wait_rows(box, land, c, ssem, rsem, sign, sent):
        def one(s, carry):
            copy = remote(box.at[s], land.at[s], ssem.at[s], rsem.at[s], shifted(at, s, sign))
            if sent:
                copy.wait_send()
            else:
                copy.wait_recv()
            return carry
        if c == 0 and not sent:
            pltpu.make_async_copy(box.at[0], land.at[0], self_sem.at[[k for k, sem in enumerate(selves) if sem is ssem][0]]).wait()
        lax.fori_loop(max(1, c * GROUP), (c + 1) * GROUP, one, 0)

    chunks = range(SLOTS // CHUNK)

    def lanes_of(c):
        return slice(c * CHUNK, (c + 1) * CHUNK)

    def blocks_of(c):
        return slice(c * GROUP, (c + 1) * GROUP)

    def send_cotangents(c, left):
        rows = t_dot(left[:, lanes_of(c)], cot2[...].reshape(2 * TOK, D))
        out_g[blocks_of(c)] = rows.astype(bf16).reshape(GROUP, BLOCK, D)
        send_rows(out_g, arr_g, c, g_send, g_recv, 1)

    send_cotangents(0, hits)
    fill(0, gates_r[...])
    ntt[:, :TOK] = flip(nt_r[...])
    for copy in pair:
        copy.wait_recv()
    fill(1, gates2[...])
    for c in chunks:
        rows = t_dot(hits[:, lanes_of(c)], nt2[...].reshape(2 * TOK, D))
        out_n[blocks_of(c)] = rows.astype(bf16).reshape(GROUP, BLOCK, D)
        send_rows(out_n, arr_n, c, n_send, n_recv, 1)
    gate = t_dot(gated[:, :CHUNK], jnp.ones((2 * TOK, 128), bf16))
    gate_out[...] = gate.astype(bf16).reshape(GROUP, BLOCK, 128)
    gate_in[0] = gate_out[0]
    for s in range(1, GROUP):
        go(remote(gate_out.at[s], gate_in.at[s], gate_send.at[s], gate_recv.at[s], shifted(at, s, 1)))
    for c in chunks[1:]:
        send_cotangents(c, gated)

    sd_copy.wait()
    gh = jnp.zeros((TOK, 1024), f32)
    for j in range(4):
        gh = gh + dot_t(cot[:, j * 384 : (j + 1) * 384], sd_v[j])
    acc[...] = jnp.zeros((2 * TOK, D), f32)
    for j in range(4):
        for copy in loads[j]:
            copy.wait()
        cols = slice(j * 256, (j + 1) * 256)
        gate, up = dot(nt_r[...], sg_v[j % 2]), dot(nt_r[...], su_v[j % 2])
        act, slope = silu_parts(gate)
        shid[:, cols] = (act * up).astype(bf16)
        dgate = dgate_s[j] = (gh[:, cols] * up * slope).astype(bf16)
        dup = dup_s[j] = (gh[:, cols] * act).astype(bf16)
        acc[:TOK] += dot_t(dgate, sg_v[j % 2]) + dot_t(dup, su_v[j % 2])
        if j < 2:
            loads[j + 2] = (load(sg_h.at[j + 2], sg_v.at[j], j), load(su_h.at[j + 2], su_v.at[j], 2 + j))
    gnt_r[...] = acc[:TOK]
    resid_copy = load(resid_h, acc.at[pl.ds(0, TOK)], 5)
    for k, (src, dst) in enumerate(((dgate_s.at[theirs], dgate_x), (dup_s.at[theirs], dup_x), (shid, shid_x))):
        beside.append(go(remote(src, dst, sib_send.at[2 + k], sib_recv.at[2 + k], sibling)))
    resid_copy.wait()
    for j in range(4):
        cols = slice(j * 384, (j + 1) * 384)
        acc[:TOK, cols] += dot(shid[...], sd_v[j])
    acc[TOK:] = jnp.zeros((TOK, D), f32)
    for copy in beside:
        copy.wait_recv()
    ntt[:, TOK:] = flip(nt_x[...])
    shid_t = jnp.concatenate([flip(shid[...]), flip(shid_x[...])], axis=1)
    finals = []
    for k in range(2):
        j = 2 * at["core"] + k
        cols = pl.ds(pl.multiple_of(j * 384, 128), 384)
        sg_v[k] = dot(ntt[...], jnp.concatenate([dgate_s[j], dgate_x[k]], axis=0)).astype(bf16)
        su_v[k] = dot(ntt[...], jnp.concatenate([dup_s[j], dup_x[k]], axis=0)).astype(bf16)
        sd_v[k] = dot(shid_t, jnp.concatenate([cot2[0, :, cols], cot_x[:, k * 384 : (k + 1) * 384]], axis=0)).astype(bf16)
        for i, (src, dst) in enumerate(((sg_v, gsg_h), (su_v, gsu_h), (sd_v, gsd_h))):
            copy = pltpu.make_async_copy(src.at[k], dst.at[k], pull_sem.at[3 * k + i])
            copy.start()
            finals.append(copy)

    for copy in swaps:
        copy.wait_recv()
    halves = ((gm, um, dm), (gx, ux, dx))
    for c in chunks:
        wait_rows(out_n, arr_n, c, n_send, n_recv, 1, False)
        x = arr_n[blocks_of(c)].reshape(CHUNK, D)
        total = None
        for k, (g, u, d) in enumerate(halves):
            cols = slice(k * 256, (k + 1) * 256)
            gate, up = dot(x, g[...]), dot(x, u[...])
            act, slope = silu_parts(gate)
            hidden = (act * up).astype(bf16)
            hid[lanes_of(c), cols] = hidden
            act_s[lanes_of(c), cols] = act.astype(bf16)
            slope_s[lanes_of(c), cols] = (up * slope).astype(bf16)
            part = dot(hidden, d[...])
            total = part if total is None else total + part
        wait_rows(out_n, arr_n, c, n_send, n_recv, 1, True)
        out_n[blocks_of(c)] = total.astype(bf16).reshape(GROUP, BLOCK, D)
        send_rows(out_n, ret_m, c, m_send, m_recv, -1)
    for c in chunks:
        wait_rows(out_g, arr_g, c, g_send, g_recv, 1, False)
        if c == 0:
            for s in range(1, GROUP):
                remote(gate_out.at[s], gate_in.at[s], gate_send.at[s], gate_recv.at[s], shifted(at, s, 1)).wait_recv()
            gate = gate_in[...].reshape(CHUNK, 128)[:, :1].astype(f32)
            slot = (arr_g[blocks_of(0)].reshape(CHUNK, D).astype(f32) * gate).astype(bf16)
            arr_g[blocks_of(0)] = slot.reshape(GROUP, BLOCK, D)
        slot = arr_g[blocks_of(c)].reshape(CHUNK, D)
        total = None
        for k, (g, u, d) in enumerate(halves):
            cols = slice(k * 256, (k + 1) * 256)
            gh = dot_t(slot, d[...])
            dgate = (gh * slope_s[lanes_of(c), cols].astype(f32)).astype(bf16)
            dup = (gh * act_s[lanes_of(c), cols].astype(f32)).astype(bf16)
            slope_s[lanes_of(c), cols], act_s[lanes_of(c), cols] = dgate, dup
            part = dot_t(dgate, g[...]) + dot_t(dup, u[...])
            total = part if total is None else total + part
        wait_rows(out_g, arr_g, c, g_send, g_recv, 1, True)
        out_g[blocks_of(c)] = total.astype(bf16).reshape(GROUP, BLOCK, D)
        send_rows(out_g, ret_b, c, b_send, b_recv, -1)
    for copy in finals:
        copy.wait()
    for b in range(4):
        cols = slice(b * 384, (b + 1) * 384)
        xt = flip(jnp.concatenate([arr_n[blocks_of(c), :, cols].reshape(CHUNK, 384) for c in chunks], axis=0))
        gg = dot(xt, slope_s[...])
        gu = dot(xt, act_s[...])
        gg_o[cols], gu_o[cols] = gg[:, :256], gu[:, :256]
        sg_v[0, cols], sg_v[1, cols] = gg[:, 256:].astype(bf16), gu[:, 256:].astype(bf16)
    trade = [go(remote(sg_v, grecv_a, rep_send.at[3], rep_recv.at[3], twin))]
    hid_t = flip(hid[...])
    for b in range(4):
        cols = slice(b * 384, (b + 1) * 384)
        gd = dot(hid_t, jnp.concatenate([arr_g[blocks_of(c), :, cols].reshape(CHUNK, 384) for c in chunks], axis=0))
        gd_o[:, cols] = gd[:256]
        sd_v[0, b * 256 : (b + 1) * 256] = gd[256:].astype(bf16)
    trade.append(go(remote(sd_v.at[0], grecv_b, rep_send.at[4], rep_recv.at[4], twin)))

    picked = jnp.zeros((2 * TOK, 128), f32)
    for c in chunks:
        wait_rows(out_n, ret_m, c, m_send, m_recv, -1, False)
        rows = ret_m[blocks_of(c)].reshape(CHUNK, D)
        acc[...] += dot(gated[:, lanes_of(c)], rows)
        grads = dot_t(cot2[...].reshape(2 * TOK, D), rows) * hits[:, lanes_of(c)].astype(f32)
        high = grads.astype(bf16)
        low = (grads - high.astype(f32)).astype(bf16)
        own = owner[:, lanes_of(c)]
        picked = picked + dot_t(high, own) + dot_t(low, own)
    part_s[0] = acc[TOK:].astype(bf16)
    pick_s[...] = picked[TOK:]
    pair.append(go(remote(part_s.at[0], part_r.at[0], pair_send.at[2], pair_recv.at[2], partner)))
    pair.append(go(remote(pick_s, pick_r, pair_send.at[3], pair_recv.at[3], partner)))
    pair[2].wait_recv()
    out_r[...] = (acc[:TOK] + part_r[0].astype(f32)).astype(bf16)
    pair[3].wait_recv()
    picked = picked[:TOK] + pick_r[...]
    gates = gates_r[...]
    mean = jnp.sum(gates * picked, axis=-1, keepdims=True)
    gl = (gates * (picked - mean)).astype(bf16)
    misc_r[...] = dot(ntt[:, :TOK], gl)
    acc[:TOK] = gnt_r[...] + dot_t(gl, router_r[...])
    acc[TOK:] = jnp.zeros((TOK, D), f32)
    for c in chunks:
        wait_rows(out_g, ret_b, c, b_send, b_recv, -1, False)
        acc[...] += dot(hits[:, lanes_of(c)], ret_b[blocks_of(c)].reshape(CHUNK, D))
    part_s[1] = acc[TOK:].astype(bf16)
    pair.append(go(remote(part_s.at[1], part_r.at[1], pair_send.at[4], pair_recv.at[4], partner)))
    trade[0].wait_recv()
    gg_o[...] += grecv_a[0].astype(f32)
    gu_o[...] += grecv_a[1].astype(f32)
    trade[1].wait_recv()
    for b in range(4):
        gd_o[:, b * 384 : (b + 1) * 384] += grecv_b[b * 256 : (b + 1) * 256].astype(f32)
    outs = []
    for k, (src, dst) in enumerate(((gg_o, gg_h), (gu_o, gu_h), (gd_o, gd_h))):
        outs.append(pltpu.make_async_copy(src, dst, pull_sem.at[k]))
        outs[-1].start()
    pair[4].wait_recv()
    gnt_r[...] = acc[:TOK] + part_r[1].astype(f32)
    for c in chunks:
        wait_rows(out_n, ret_m, c, m_send, m_recv, -1, True)
        wait_rows(out_g, ret_b, c, b_send, b_recv, -1, True)
    for copy in outs:
        copy.wait()
    for copy in started:
        copy.wait_send()


def moe(nt, cot, cotp, resid, gates, router, hits, owner, mine, sg, su, sd):
    dma = pltpu.SemaphoreType.DMA
    vm = lambda shape, dtype=bf16: pltpu.VMEM(shape, dtype)
    rows = (PEERS, BLOCK, D)
    return pl.pallas_call(
        moe_kernel,
        out_shape=[sds((TOK, D)), sds((TOK, D), f32), sds((D, 128), f32), sds((D, 256), f32), sds((D, 256), f32), sds((256, D), f32)]
        + [sds((2, D, 256)), sds((2, D, 256)), sds((2, 1024, 384))],
        in_specs=[ANY] * 14,
        out_specs=[VM] * 3 + [ANY] * 6,
        scratch_shapes=[vm((TOK, 128), f32), vm((D, 128)), vm((2 * TOK, SLOTS)), vm((128, SLOTS)), vm((D, 256)), vm((D, 256)), vm((256, D))]
        + [vm((D, 256), f32), vm((D, 256), f32), vm((256, D), f32)]
        + [vm((2, TOK, D)), vm((2, TOK, D)), vm((TOK, 128), f32), vm((2 * TOK, SLOTS)), vm((GROUP, BLOCK, 128)), vm((GROUP, BLOCK, 128))]
        + [vm(rows)] * 6
        + [vm((D, 256)), vm((D, 256)), vm((256, D)), vm((SLOTS, 512)), vm((SLOTS, 512)), vm((SLOTS, 512)), vm((2 * TOK, D), f32)]
        + [vm((2, D, 256)), vm((1024, 384)), vm((2, TOK, D)), vm((2, TOK, D)), vm((TOK, 128), f32), vm((TOK, 128), f32)]
        + [vm((2, D, 256)), vm((2, D, 256)), vm((4, 1024, 384)), vm((TOK, 1024)), vm((D, 2 * TOK)), vm((TOK, D)), vm((TOK, 768)), vm((TOK, 1024))]
        + [vm((4, TOK, 256)), vm((4, TOK, 256)), vm((2, TOK, 256)), vm((2, TOK, 256)), dma((5,)), dma((5,))]
        + [dma((5,)), dma((5,)), dma((5,)), dma((5,))] + [dma((PEERS,))] * 8 + [dma((GROUP,)), dma((GROUP,)), dma((4,)), dma((6,)), dma((10,))],
        compiler_params=pltpu.CompilerParams(collective_id=3, has_side_effects=True, vmem_limit_bytes=127 << 19),
        name="moe",
    )(nt, cot, cotp, resid, gates, router, hits, owner, *mine, sg, su, sd)


SUMS = (256, 256, 128, 128, 128, 256, 256, 256, 384)


def sum_box(i):
    return core_box(i)[:5] + (SUMS[i],)


class Scatter(Links):
    def __init__(self, total, landing, spread, outs, own_sem, rsend, rrecv, send, recv, msend, mrecv):
        super().__init__()
        self.total, self.landing, self.spread, self.outs = total, landing, spread, outs
        self.own_sem, self.rsend, self.rrecv = own_sem, rsend, rrecv
        self.send, self.recv, self.msend, self.mrecv = send, recv, msend, mrecv

    def spot(self, i, done, where, half=None):
        return region(where, ORDERS[i], done, half=half)[1:]

    def add(self, i, where, ref, *spots):
        to = self.total[i]
        total = to[where].astype(f32)
        for spot in spots:
            total = total + ref[spot].astype(f32)
        to[where] = total.astype(bf16)

    def start(self, i, src):
        self.sent[i] = pltpu.make_async_copy(src, self.total[i], self.own_sem.at[i])
        self.sent[i].start()

    def message(self, i, side, number):
        axis, done = ORDERS[i][2], ORDERS[i][:2]
        step = STEPS[side]
        spot, k = ((self.near(axis, 2), side), (self.near(axis, step), 1 - side), (self.near(axis, step), side))[number]
        src = self.total[i].at[self.spot(i, done, spot, k)]
        dst = self.landing[i][0].at[side, number]
        self.sent[i, 2, side, number] = self.go(src, dst, self.rsend.at[i, side, number], self.rrecv.at[i, side, number], self.near(axis, step))

    def enter(self, i):
        if i in SHARED:
            self.sent[i].wait()
        for number in range(2):
            for side in range(2):
                self.message(i, side, number)

    def relay(self, i):
        axis, done = ORDERS[i][2], ORDERS[i][:2]
        for side in range(2):
            self.sent[i, 2, side, 0].wait_recv()
            self.add(i, self.spot(i, done, self.near(axis, STEPS[side]), side), self.landing[i][0], (side, 0))
            self.message(i, side, 2)

    def direct(self, i, phase):
        axis, done = ORDERS[i][phase], ORDERS[i][:phase]
        self.sent[i, phase] = [
            self.go(self.total[i].at[self.spot(i, done, self.near(axis, by))], self.landing[i][2 - phase].at[k], self.send.at[i, phase, k], self.recv.at[i, phase, k], self.near(axis, by))
            for k, by in enumerate(STEPS)
        ]

    def second(self, i):
        done = ORDERS[i][:2]
        for side in range(2):
            for number in (1, 2):
                self.sent[i, 2, side, number].wait_recv()
        for k in range(2):
            self.add(i, self.spot(i, done, self.at, k), self.landing[i][0], (k, 2), (1 - k, 1))
        self.direct(i, 1)

    def third(self, i):
        for copy in self.sent[i, 1]:
            copy.wait_recv()
        self.add(i, self.spot(i, ORDERS[i][:1], self.at), self.landing[i][1], 0, 1, 2)
        self.direct(i, 0)

    def spread_rows(self, i):
        for copy in self.sent[i, 0]:
            copy.wait_recv()
        chunk = self.total[i][self.spot(i, "", self.at)].astype(f32)
        for k in range(3):
            chunk = chunk + self.landing[i][2][k].astype(f32)
        size, take = rows_of(i), PIECE[i]
        to_row, from_row = iota((64, size), 0), iota((64, size), 1)
        pick = ((from_row // take) * 16 + from_row % take == to_row).astype(bf16)
        laid = dot(pick, chunk.astype(bf16)).astype(bf16)
        self.spread[i][...] = laid.reshape(4, 16, SUMS[i])
        own = pltpu.make_async_copy(self.spread[i].at[self.mine], self.outs[i].at[self.mine], self.own_sem.at[i])
        own.start()
        finals = [own]
        for k, to in enumerate(self.peers):
            quarter = to["core"] * 2 + to["y"] // 2
            finals.append(self.go(self.spread[i].at[quarter], self.outs[i].at[self.mine], self.msend.at[i, k], self.mrecv.at[i, k], to))
        self.sent[i, "final"] = finals

    def finish(self):
        for i in range(N):
            own, *copies = self.sent[i, "final"]
            own.wait()
            for copy in copies:
                copy.wait_recv()
        self.end()


def half_box(order):
    return {"xyz": (2, 2, 2), "yzx": (4, 2), "zxy": (2, 4)}[order]


def back_kernel(*refs):
    pulls, shared_h, weights = refs[:11], refs[11:14], refs[14:20]
    gtok_o, *outs = refs[20:30]
    total = refs[30:39]
    landing = [refs[39 + 3 * i : 42 + 3 * i] for i in range(N)]
    spread = refs[66:75]
    gnt, resid_r, cot, tokens, normed_r, q_r, kv_r, p_r, att_r, misc_in, misc_w = here = refs[75:86]
    left_s, right_s, gv_s, goo_s, gatt_s, turned, acc, gres, misc_s, slots = refs[86:96]
    normed_x, att_x, goo_x, left_x, right_x, gv_x, misc_x, slot_sem, pull_sem, sib_send, sib_recv, *sems = refs[96:]
    s = Scatter(total, landing, spread, outs, *sems)
    core = s.core
    loads = {}

    def load(j, parts):
        loads[j] = []
        at_lane = 0
        for k, (i, width) in enumerate(parts):
            src = weights[i].at[j] if width == WIDE[i] else weights[i].at[j, :, pl.ds(0, width)]
            copy = pltpu.make_async_copy(src, slots.at[j, :, pl.ds(at_lane, width)], slot_sem.at[j, k])
            copy.start()
            loads[j].append(copy)
            at_lane += width

    def loaded(j):
        for copy in loads[j]:
            copy.wait()

    def weight_grads(group, right):
        for k in range(2):
            for i, value in zip(group, right(2 * core + k, k)):
                total[i][k] = value.astype(bf16).reshape(sum_box(i)[1:])

    def tell(k, src, dst):
        s.sent["told", k] = s.go(src, dst, sib_send.at[k], sib_recv.at[k], s.sibling)

    def told(*which):
        for k in which:
            s.sent["told", k].wait_recv()

    theirs = pl.ds(2 * (1 - core), 2)
    s.pull(pulls, here, pull_sem)
    for i, src in zip(SHARED, shared_h):
        s.start(i, src)
    for j in range(4):
        load(j, [(3, 128), (4, 128), (5, 128)])
    s.greet()
    tell(0, pulls[4], normed_x)
    tell(1, pulls[8], att_x)
    for i in SHARED:
        s.enter(i)
    s.pulled()

    resid = resid_r[...]
    scale = rms_scale(resid)
    grad = gnt[...]
    lane = iota((TOK, 128), 1)
    gres[...] = cot[...].astype(f32) + norm_back(grad, resid, scale, gain_row(misc_w[...], 65))
    acc[...] = jnp.zeros((TOK, D), f32)
    for j in range(4):
        goo_s[j] = gres[:, j * 384 : (j + 1) * 384].astype(bf16)
        loaded(j)
        acc[...] += dot_t(goo_s[j], slots[j])
        load(j, [(0, 256), (2, 128)])
    for j in range(4):
        gatt_s[j] = acc[:, j * 384 : (j + 1) * 384].astype(bf16)
    tell(2, goo_s.at[theirs], goo_x)
    turned[:, :TOK] = flip(normed_r[...])
    told(0)
    turned[:, TOK:] = flip(normed_x[...])
    for j in range(4):
        ga, q, kv, p = gatt_s[j], q_r[j], kv_r[j], p_r[j]
        ga3 = jnp.concatenate([ga[:, :128], ga[:, 128:256], ga[:, 256:]], axis=0)
        q3 = jnp.concatenate([q[:, :128], q[:, 128:256], q[:, 256:]], axis=0)
        gp = dot_t(ga3, kv[:, 128:])
        gs = (p * (gp - jnp.sum(p * gp, axis=-1, keepdims=True))).astype(bf16)
        gq3 = (dot(gs, kv[:, :128]) * SCALE).astype(bf16)
        gk = (t_dot(gs, q3) * SCALE).astype(bf16)
        gv_s[j] = t_dot(p.astype(bf16), ga3).astype(bf16)
        left_s[j] = jnp.concatenate([gq3[:128], gq3[128:256]], axis=1)
        right_s[j] = jnp.concatenate([gq3[256:], gk], axis=1)
    tell(3, left_s.at[theirs], left_x)
    tell(4, right_s.at[theirs], right_x)
    tell(5, gv_s.at[theirs], gv_x)
    for i in SHARED:
        s.relay(i)
    told(3, 4, 5)

    def both(mine, other):
        return dot(turned[...], jnp.concatenate([mine, other], axis=0))

    weight_grads(QKV, lambda j, k: (both(left_s[j], left_x[k]), both(right_s[j], right_x[k]), both(gv_s[j], gv_x[k])))
    for i in QKV:
        s.enter(i)
    resid = resid_r[...]
    misc_s[...] = misc_in[...] + t_dot((gnt[...] * resid * rms_scale(resid)).astype(bf16), (lane == 65).astype(bf16))
    acc[...] = jnp.zeros((TOK, D), f32)
    for j in range(4):
        loaded(j)
        acc[...] += dot_t(jnp.concatenate([left_s[j], gv_s[j]], axis=1), slots[j])
        load(j, [(1, 256)])
    for j in range(4):
        loaded(j)
        acc[...] += dot_t(right_s[j], slots[j, :, :256])
    source = tokens[...].astype(f32)
    scale = rms_scale(source)
    misc_s[...] += t_dot((acc[...] * source * scale).astype(bf16), (lane == 64).astype(bf16))
    tell(6, misc_s, misc_x)
    told(1, 2)
    for j in range(4):
        turned[j * 384 : (j + 1) * 384, :TOK] = flip(att_r[j])
        turned[j * 384 : (j + 1) * 384, TOK:] = flip(att_x[j])
    told(6)

    def out_grads(j, k):
        whole = both(goo_s[j], goo_x[k])
        misc = (misc_s[...] + misc_x[...]) * jnp.where(j == 0, 1.0, 0.0)
        return whole[:, :128], whole[:, 128:256], jnp.concatenate([whole[:, 256:], misc], axis=1)

    weight_grads(OUT, out_grads)
    for i in QKV:
        s.relay(i)
    for i in OUT:
        s.enter(i)
    gtok_o[...] = gres[...] + norm_back(acc[...], source, scale, gain_row(misc_w[...], 64))
    for i in SHARED:
        s.second(i)
    for i in QKV:
        s.second(i)
    for i in OUT:
        s.relay(i)
    for i in SHARED:
        s.third(i)
    for i in QKV:
        s.third(i)
    for i in OUT:
        s.second(i)
    for i in SHARED:
        s.spread_rows(i)
    for i in QKV:
        s.spread_rows(i)
    for i in OUT:
        s.third(i)
    for i in OUT:
        s.spread_rows(i)
    s.finish()


def back(*args, shared_grads, weights):
    grads = [g.reshape(sum_box(i)) for i, g in zip(SHARED, shared_grads)]
    vm = lambda shape, dtype=bf16: pltpu.VMEM(shape, dtype)
    dma = pltpu.SemaphoreType.DMA
    halves = [vm(sum_box(i)) for i in range(N)]
    scratch = list(halves)
    for i in range(N):
        tail = (rows_of(i), SUMS[i])
        scratch += [vm((2, 3) + half_box(ORDERS[i]) + tail), vm((3,) + axis_box(ORDERS[i][0]) + tail), vm((3,) + tail)]
    scratch += [vm((4, 16, w)) for w in SUMS]
    scratch += [vm(a.shape, a.dtype) for a in args]
    scratch += [vm((4, TOK, 256)), vm((4, TOK, 256)), vm((4, TOK, 128)), vm((4, TOK, 384)), vm((4, TOK, 384)), vm((D, 2 * TOK)), vm((TOK, D), f32), vm((TOK, D), f32), vm((D, 128), f32), vm((4, D, 384))]
    scratch += [vm((TOK, D)), vm((4, TOK, 384)), vm((2, TOK, 384)), vm((2, TOK, 256)), vm((2, TOK, 256)), vm((2, TOK, 128)), vm((D, 128), f32), dma((4, 3)), dma((11,)), dma((7,)), dma((7,))]
    scratch += [dma((N,)), dma((N, 2, 3)), dma((N, 2, 3)), dma((N, 2, 3)), dma((N, 2, 3)), dma((N, 3)), dma((N, 3))]
    return pl.pallas_call(
        back_kernel,
        out_shape=[sds((TOK, D), f32)] + [sds((4, 16, w)) for w in SUMS],
        in_specs=[ANY] * 20,
        out_specs=[VM] * 10,
        scratch_shapes=scratch,
        compiler_params=pltpu.CompilerParams(collective_id=2, has_side_effects=True, vmem_limit_bytes=63 << 20),
        name="back",
    )(*args, *grads, *weights)


def final_kernel(*refs):
    gtok, block, gg, gu, gd = refs[:5]
    outs = refs[5:14]
    block_o, gtok_o, gq_o, gk_o, gv_o, go_o, gsg_o, gsu_o, gsd_o, gr_o, g1_o, g2_o, gg_o, gu_o, gd_o = refs[14:]
    for src, dst in ((gtok, gtok_o), (block, block_o), (gg, gg_o), (gu, gu_o), (gd, gd_o)):
        dst[...] = src[...]
    for j in range(4):
        block = [outs[i][j].astype(f32)[: PIECE[i]] for i in range(N)]
        gq_o[:, j * 384 : j * 384 + 256] = block[0]
        gq_o[:, j * 384 + 256 : (j + 1) * 384] = block[1][:, :128]
        gk_o[:, j * 128 : (j + 1) * 128] = block[1][:, 128:]
        gv_o[:, j * 128 : (j + 1) * 128] = block[2]
        for p in range(3):
            go_o[:, j * 384 + p * 128 : j * 384 + (p + 1) * 128] = block[3 + p][:, :128]
        gsg_o[:, j * 256 : (j + 1) * 256] = block[6]
        gsu_o[:, j * 256 : (j + 1) * 256] = block[7]
        gsd_o[:, j * 384 : (j + 1) * 384] = block[8]
    misc = outs[5][0].astype(f32)[:12, 128:]
    gr_o[...] = misc[:, :64]
    eye = iota((12, 12), 0) == iota((12, 12), 1)
    for k, out in ((64, g1_o), (65, g2_o)):
        out[...] = jnp.sum(jnp.where(eye, misc[:, k : k + 1], 0.0), axis=0, keepdims=True)


def final(gtok, block, expert, pieces):
    shapes = ((TOK, D), (12, D), (12, 512), (12, 512), (12, D), (12, 1024), (12, 1024), (8, D), (12, 64), (1, 12), (1, 12), (D, 256), (D, 256), (256, D))
    return pl.pallas_call(
        final_kernel,
        out_shape=[sds((TOK, D))] + [sds(s, f32) for s in shapes],
        in_specs=[VM] * 14,
        out_specs=[VM] * 15,
        compiler_params=pltpu.CompilerParams(vmem_limit_bytes=63 << 20),
        name="final",
    )(gtok, block, *expert, *pieces)


def local(tokens, segment_ids, routes, cotangent, query_weight, key_weight, value_weight, output_weight, shared_gate, shared_up, shared_down, router_weight, first_gain, second_gain, expert_gate, expert_up, expert_down):
    (normed, q, kv, p, att, resid, nt, gates, misc_w, hits, owner, cotp), weights = front(
        tokens, segment_ids, routes.T, query_weight, key_weight, value_weight, output_weight, router_weight,
        first_gain[None], second_gain[None], shared_gate, shared_up, shared_down, cotangent,
    )
    mine = [expert_gate[0], expert_up[0], expert_down[0]]
    block, gnt, gmisc, gg, gu, gd, *shared_grads = moe(
        nt, cotangent, cotp, resid, gates, misc_w, hits, owner, mine, *weights[6:]
    )
    gtok, *pieces = back(
        gnt, resid, cotangent, tokens, normed, q, kv, p, att, gmisc, misc_w, shared_grads=shared_grads, weights=weights[:6]
    )
    *outs, g1, g2, gg, gu, gd = final(gtok, block, (gg, gu, gd), pieces)
    return *outs, g1[0], g2[0], gg[None], gu[None], gd[None]


def solution(mesh):
    in_specs = (
        P(("fsdp", "rep"), None),
        P(("fsdp", "rep"), None),
        P(("fsdp", "rep"), None),
        P(("fsdp", "rep"), None),
        P(("fsdp", "rep"), None),
        P(("fsdp", "rep"), None),
        P(("fsdp", "rep"), None),
        P(("fsdp", "rep"), None),
        P(("fsdp", "rep"), None),
        P(("fsdp", "rep"), None),
        P(("fsdp", "rep"), None),
        P(("fsdp", "rep"), None),
        P(("fsdp", "rep")),
        P(("fsdp", "rep")),
        P("fsdp", None, "rep"),
        P("fsdp", None, "rep"),
        P("fsdp", "rep", None),
    )
    out_specs = (
        P(("fsdp", "rep"), None),
        P(("fsdp", "rep"), None),
        P(("fsdp", "rep"), None),
        P(("fsdp", "rep"), None),
        P(("fsdp", "rep"), None),
        P(("fsdp", "rep"), None),
        P(("fsdp", "rep"), None),
        P(("fsdp", "rep"), None),
        P(("fsdp", "rep"), None),
        P(("fsdp", "rep"), None),
        P(("fsdp", "rep")),
        P(("fsdp", "rep")),
        P("fsdp", None, "rep"),
        P("fsdp", None, "rep"),
        P("fsdp", "rep", None),
    )
    return jax.shard_map(local, mesh=mesh, in_specs=in_specs, out_specs=out_specs, check_vma=False)
```

```python
import math

import jax
import jax.numpy as jnp
from jax import lax
from jax.experimental import pallas as pl
from jax.experimental.pallas import tpu as pltpu
from jax.sharding import PartitionSpec as P

MESH = pl.DeviceIdType.MESH
ANY = pl.BlockSpec(memory_space=pl.ANY)
VM = pl.BlockSpec(memory_space=pltpu.VMEM)


def place():
    f, r = lax.axis_index("fsdp"), lax.axis_index("rep")
    return dict(x=(f // 2) % 4, y=2 * r + (f // 8) % 2, z=f // 16, core=f % 2)


def device(at):
    return (((at["z"] * 2 + at["y"] % 2) * 4 + at["x"]) * 2 + at["core"], at["y"] // 2)


def moved(at, axis, by):
    return {**at, axis: (at[axis] + by) % (2 if axis == "core" else 4)}


def region(at, order, done, coordinate=None, half=None):
    first = done[0] if done else None
    spot = {}
    for axis in "xyz":
        whole = axis in done
        at_axis = at[axis]
        if axis == "y":
            if whole:
                spot["yhi"] = (half if (half is not None and first == "y") else slice(None))
                spot["ylo"] = slice(None)
            else:
                spot["yhi"], spot["ylo"] = at_axis // 2, at_axis % 2
        else:
            if whole:
                spot[axis] = pl.ds(2 * half, 2) if (half is not None and first == axis) else slice(None)
            else:
                spot[axis] = at_axis
    return (at["core"], spot["yhi"], spot["z"], spot["ylo"], spot["x"])


D = 1536
TOK = 128
TOP = 6
EXPERTS = 64
CAP = 24
SLOTS = EXPERTS * CAP
CHUNK = 384
epsilon = 1e-06
SCALE = 1.0 / math.sqrt(128)
f32, bf16, i32 = jnp.float32, jnp.bfloat16, jnp.int32


def dot(a, b):
    return jnp.dot(a, b, preferred_element_type=f32)


def dot_t(a, b):
    return lax.dot_general(a, b, (((1,), (1,)), ((), ())), preferred_element_type=f32)


def t_dot(a, b):
    return lax.dot_general(a, b, (((0,), (0,)), ((), ())), preferred_element_type=f32)


def flip(a):
    return a.astype(f32).T.astype(bf16)


def rms_scale(v):
    return lax.rsqrt(jnp.mean(v * v, axis=-1, keepdims=True) + epsilon)


def silu_parts(pre):
    s = jax.nn.sigmoid(pre)
    return pre * s, s * (1.0 + pre * (1.0 - s))


def norm_back(grad, source, scale, gain):
    weighted = grad * gain
    inner = jnp.mean(weighted * source, axis=-1, keepdims=True)
    return scale * weighted - source * (scale * scale * scale) * inner


def iota(shape, dim):
    return lax.broadcasted_iota(i32, shape, dim)


def gain_row(misc, lane):
    pick = (iota((16, 128), 1) == lane).astype(bf16)
    return dot_t(pick, misc)[0:1]


def chosen(routes):
    lanes = iota((TOK, 128), 1)
    hit = jnp.zeros((TOK, 128), f32)
    for k in range(TOP):
        hit = hit + (routes[:, k : k + 1] == lanes).astype(f32)
    return hit


def sds(shape, dtype=bf16):
    return jax.ShapeDtypeStruct(shape, dtype)


ORDERS = ("xyz", "yzx", "zxy") * 3
PIECE = (12, 12, 12, 12, 12, 12, 12, 12, 8)
WIDE = (256, 256, 256, 128, 128, 128, 256, 256, 384)
N = len(ORDERS)
QKV, OUT, SHARED = (0, 1, 2), (3, 4, 5), (6, 7, 8)
STEPS = (1, -1, 2)


def rows_of(i):
    return 4 * PIECE[i]


def core_box(i):
    return (2, 4, 2, 4, rows_of(i), WIDE[i])


def axis_box(axis):
    return (2, 2) if axis == "y" else (4,)


def partner_of(at):
    return {**at, "y": at["y"] + 1 - 2 * (at["y"] % 2)}


def owners(at):
    there = shifted(at, iota((1, SLOTS), 1) // BLOCK, 1)
    expert = ((there["z"] * 2 + at["y"] % 2) * 4 + there["x"]) * 2 + there["core"]
    return (iota((128, SLOTS), 0) == expert).astype(bf16)


class Links:
    def __init__(self):
        self.at = place()
        self.core = self.at["core"]
        self.mine = self.core * 2 + self.at["y"] // 2
        self.sibling = moved(self.at, "core", 1)
        self.peers = [self.sibling, moved(self.at, "y", 2), moved(self.sibling, "y", 2)]
        self.started, self.sent = [], {}
        self.places = {(axis, by): moved(self.at, axis, by) for axis in "xyz" for by in STEPS}
        self.devices = [(to, device(to)) for to in [*self.peers, *self.places.values()]]

    def near(self, axis, by):
        return self.places[axis, (by + 1) % 4 - 1]

    def near_sibling(self, axis, by):
        return {**(self.near(axis, by) if by else self.at), "core": self.sibling["core"]}

    def device_of(self, to):
        for known, number in self.devices:
            if known is to:
                return number
        return device(to)

    def pull(self, refs, held, sems):
        self.pulls = []
        for k, (src, dst) in enumerate(zip(refs, held)):
            self.pulls.append(pltpu.make_async_copy(src, dst, sems.at[k]))
            self.pulls[-1].start()

    def pulled(self):
        for copy in self.pulls:
            copy.wait()

    def greet(self):
        barrier = pltpu.get_barrier_semaphore()
        ring = [self.near(axis, by) for axis in "xyz" for by in STEPS if (axis, by) != ("y", 2)]
        for to in self.peers + ring:
            pl.semaphore_signal(barrier, inc=1, device_id=device(to), device_id_type=MESH)
        pl.semaphore_wait(barrier, len(self.peers) + len(ring))

    def remote(self, src, dst, s, r, to):
        return pltpu.make_async_remote_copy(src_ref=src, dst_ref=dst, send_sem=s, recv_sem=r, device_id=self.device_of(to), device_id_type=MESH)

    def go(self, *args):
        copy = self.remote(*args)
        copy.start()
        self.started.append(copy)
        return copy

    def end(self):
        for copy in self.started:
            copy.wait_send()


class Gather(Links):
    def __init__(self, shards, got, stage, bufs, mix_send, mix_recv, own_sem, send, recv, rsend, rrecv, dsend, drecv):
        super().__init__()
        self.shards, self.got, self.stage, self.bufs = shards, got, stage, bufs
        self.mix_send, self.mix_recv, self.own_sem = mix_send, mix_recv, own_sem
        self.send, self.recv, self.rsend, self.rrecv, self.dsend, self.drecv = send, recv, rsend, rrecv, dsend, drecv

    def here(self, i, done, spot=None, half=None):
        return self.bufs[i].at[region(self.at if spot is None else spot, ORDERS[i], done, half=half)]

    def mix(self, i):
        own = pltpu.make_async_copy(self.shards[i].at[self.mine], self.got[i].at[self.mine], self.own_sem.at[i])
        own.start()
        copies = []
        for k, to in enumerate(self.peers):
            quarter = to["core"] * 2 + to["y"] // 2
            copies.append(self.go(self.shards[i].at[quarter], self.got[i].at[self.mine], self.mix_send.at[i, k], self.mix_recv.at[i, k], to))
        self.sent[i, "mix"] = (own, copies)

    def direct(self, i, phase, src):
        axis, done = ORDERS[i][phase], ORDERS[i][:phase]
        self.sent[i, phase] = [
            self.go(src, self.here(i, done), self.send.at[i, phase, k], self.recv.at[i, phase, k], self.near(axis, by))
            for k, by in enumerate(STEPS)
        ]

    def enter(self, i):
        own, copies = self.sent[i, "mix"]
        own.wait()
        for copy in copies:
            copy.wait_recv()
        size, take = rows_of(i), PIECE[i]
        to_row, from_row = iota((size, 64), 0), iota((size, 64), 1)
        pick = ((to_row // take) * 16 + to_row % take == from_row).astype(bf16)
        self.stage[i][...] = dot(pick, self.got[i][...].reshape(64, WIDE[i])).astype(bf16)
        local = pltpu.make_async_copy(self.stage[i], self.here(i, ""), self.own_sem.at[i])
        local.start()
        self.sent[i, "own"] = local
        self.direct(i, 0, self.stage[i])

    def second(self, i):
        self.sent[i, "own"].wait()
        for copy in self.sent[i, 0]:
            copy.wait_recv()
        self.direct(i, 1, self.here(i, ORDERS[i][:1]))

    def third(self, i):
        for copy in self.sent[i, 1]:
            copy.wait_recv()
        axis, done = ORDERS[i][2], ORDERS[i][:2]
        src = self.here(i, done)
        self.sent[i, 2] = [self.go(src, src, self.rsend.at[i, k], self.rrecv.at[i, k], self.near(axis, STEPS[k])) for k in range(2)]
        self.go(src, src, self.dsend.at[i, 3], self.drecv.at[i, 3], self.sibling)

    def relay(self, i):
        axis, done = ORDERS[i][2], ORDERS[i][:2]
        halves = []
        for k in range(2):
            self.sent[i, 2][k].wait_recv()
            block = self.near(axis, -STEPS[k])
            part = self.here(i, done, block, half=k)
            halves.append(self.go(part, part, self.rsend.at[i, 2 + k], self.rrecv.at[i, 2 + k], self.near(axis, STEPS[k])))
            whole = self.here(i, done, block)
            self.go(whole, whole, self.dsend.at[i, k], self.drecv.at[i, k], self.sibling)
        self.sent[i, "far"] = halves

    def far(self, i):
        for copy in self.sent[i, "far"]:
            copy.wait_recv()
        whole = self.here(i, ORDERS[i][:2], self.near(ORDERS[i][2], 2))
        self.go(whole, whole, self.dsend.at[i, 2], self.drecv.at[i, 2], self.sibling)

    def done(self, i):
        axis, done = ORDERS[i][2], ORDERS[i][:2]
        for k, by in ((3, 0), (0, -1), (1, 1), (2, 2)):
            where = self.here(i, done, self.near_sibling(axis, by))
            self.remote(where, where, self.dsend.at[i, k], self.drecv.at[i, k], self.sibling).wait_recv()


def front_kernel(*refs):
    tokens, seg, routes, w_query, w_key, w_value, w_output, w_router, gain_one, gain_two = refs[:10]
    cot = refs[13]
    results, outs = refs[14:26], refs[26:35]
    normed_o, q_o, kv_o, p_o, att_o, resid_o, nt_o, gates_o, misc_o, hits_o, owner_o, cot_o = made = refs[35:47]
    shards, got, stage = refs[47:56], refs[56:65], refs[65:74]
    held = refs[74:80]
    code_s, code_r, pair_send, pair_recv, made_sem, out_sem, *sems = refs[80:]
    zero = jnp.zeros((4, 16, 384), bf16)
    for shard in shards:
        shard[...] = zero[:, :, : shard.shape[2]]
    eye = iota((12, 12), 0) == iota((12, 12), 1)
    router = w_router[...]
    for j in range(4):
        for p in range(3):
            at_lane = j * 384 + p * 128
            block = w_query[:, at_lane : at_lane + 128]
            if p < 2:
                shards[0][j, :12, p * 128 : (p + 1) * 128] = block
            else:
                shards[1][j, :12, :128] = block
            shards[3 + p][j, :12] = w_output[:, at_lane : at_lane + 128]
        shards[1][j, :12, 128:] = w_key[:, j * 128 : (j + 1) * 128]
        shards[2][j, :12, :128] = w_value[:, j * 128 : (j + 1) * 128]
        shards[2][j, :12, 128:192] = router
        for k, gain in enumerate((gain_one, gain_two)):
            column = jnp.sum(jnp.where(eye, gain[...].astype(f32), 0.0), axis=1, keepdims=True)
            shards[2][j, :12, 192 + k : 193 + k] = column.astype(bf16)
        for i, weight in zip(SHARED, refs[10:13]):
            shards[i][j, : PIECE[i]] = weight[:, j * WIDE[i] : (j + 1) * WIDE[i]]
    g = Gather(shards, got, stage, list(held) + list(outs[6:]), *sems)
    g.greet()
    for i in range(N):
        g.mix(i)
    source = tokens[...].astype(f32)
    row = jnp.broadcast_to(seg[...].astype(f32), (TOK, TOK))
    allowed = (row == row.T) & (iota((TOK, TOK), 1) <= iota((TOK, TOK), 0))
    allowed = jnp.concatenate([allowed.astype(f32)] * 3, axis=0)
    hit = jnp.zeros((TOK, TOK), f32)
    for k in range(TOP):
        hit = hit + (routes[k : k + 1] == iota((TOK, TOK), 0)).astype(f32)
    hit = hit.T
    earlier = (iota((TOK, TOK), 1) < iota((TOK, TOK), 0)).astype(bf16)
    code_s[...] = hit * (dot(earlier, hit.astype(bf16)) + 1.0)
    partner = partner_of(g.at)
    code_copy = g.go(code_s, code_r, pair_send.at[0], pair_recv.at[0], partner)
    scaled = source * rms_scale(source)
    for group in (QKV, OUT, SHARED):
        for i in group:
            g.enter(i)
    for i in QKV:
        g.second(i)
    for i in QKV:
        g.third(i)
    for group in (OUT, SHARED):
        for i in group:
            g.second(i)
    owner_o[...] = owners(g.at)
    spot = iota((1, SLOTS), 1) % BLOCK

    def fill(k, code):
        wide = dot(code.astype(bf16), owner_o[...])
        hits_o[k * TOK : (k + 1) * TOK] = ((wide == (spot - k * CAP + 1).astype(f32)) & (wide > 0)).astype(f32).astype(bf16)

    fill(0, code_s[...])
    for i in QKV:
        g.relay(i)
    for group in (OUT, SHARED):
        for i in group:
            g.third(i)
    for i in QKV:
        g.far(i)
    for i in OUT:
        g.relay(i)
    code_copy.wait_recv()
    fill(1, code_r[...])
    for i in QKV:
        g.done(i)
    keeps = []
    def hand_out(*which):
        for k in which:
            copy = pltpu.make_async_copy(made[k], results[k], made_sem.at[k])
            copy.start()
            keeps.append(copy)

    def weight(i, j):
        return held[i][j // 2, j % 2].reshape(D, WIDE[i])

    def keep(i):
        copy = pltpu.make_async_copy(held[i], outs[i], out_sem.at[i])
        copy.start()
        keeps.append(copy)

    normed_o[...] = (scaled * gain_row(weight(2, 0)[:, 128:], 64)).astype(bf16)
    for j in range(4):
        normed = normed_o[...]
        q01 = dot(normed, weight(0, j)).astype(bf16)
        q2k = dot(normed, weight(1, j)).astype(bf16)
        v = dot(normed, weight(2, j)[:, :128]).astype(bf16)
        q_o[j] = jnp.concatenate([q01, q2k[:, :128]], axis=1)
        kv_o[j] = jnp.concatenate([q2k[:, 128:], v], axis=1)
        q3 = jnp.concatenate([q01[:, :128], q01[:, 128:], q2k[:, :128]], axis=0)
        scores = jnp.where(allowed > 0, dot_t(q3, q2k[:, 128:]) * SCALE, -1e30)
        expo = jnp.exp(scores - jnp.max(scores, axis=-1, keepdims=True))
        p = expo / jnp.sum(expo, axis=-1, keepdims=True)
        p_o[j] = p
        mixed = dot(p.astype(bf16), v).astype(bf16)
        att_o[j] = jnp.concatenate([mixed[:128], mixed[128:256], mixed[256:]], axis=1)
        if j == 0:
            for i in OUT:
                g.far(i)
            for i in SHARED:
                g.relay(i)
            cot_copy = g.go(cot, cot_o, pair_send.at[1], pair_recv.at[1], partner)
        if j == 3:
            for i in SHARED:
                g.far(i)
    for i in QKV:
        keep(i)
    hand_out(0, 1, 2, 3, 4)
    hand_out(9, 10)
    for i in OUT:
        g.done(i)
    attended = jnp.concatenate([att_o[j] for j in range(4)], axis=1)
    for j in range(4):
        for p in range(3):
            cols = slice(j * 384 + p * 128, j * 384 + (p + 1) * 128)
            resid_o[:, cols] = source[:, cols] + dot(attended, weight(3 + p, j))
    for i in OUT:
        keep(i)
    resid = resid_o[...]
    misc = weight(2, 0)[:, 128:]
    misc_o[...] = misc
    nt = (resid * rms_scale(resid) * gain_row(misc, 65)).astype(bf16)
    nt_o[...] = nt
    logits = dot(nt, misc)
    masked = jnp.where(hit > 0, logits, -1e30)
    expo = jnp.where(hit > 0, jnp.exp(masked - jnp.max(masked, axis=-1, keepdims=True)), 0.0)
    gates_o[...] = expo / jnp.sum(expo, axis=-1, keepdims=True)
    cot_copy.wait_recv()
    hand_out(5, 6, 7, 8, 11)
    for i in SHARED:
        g.done(i)
    for copy in keeps:
        copy.wait()
    g.end()


def front(*args):
    dma = pltpu.SemaphoreType.DMA
    full = lambda i: (2,) + core_box(i)
    made = [sds((TOK, D)), sds((4, TOK, 384)), sds((4, TOK, 256)), sds((4, 384, TOK), f32), sds((4, TOK, 384)), sds((TOK, D), f32), sds((TOK, D)), sds((TOK, 128), f32), sds((D, 128)), sds((2 * TOK, SLOTS)), sds((128, SLOTS)), sds((TOK, D))]
    res = pl.pallas_call(
        front_kernel,
        out_shape=made + [sds(full(i)) for i in range(N)],
        in_specs=[VM] * 14,
        out_specs=[ANY] * (12 + N),
        scratch_shapes=[pltpu.VMEM(a.shape, a.dtype) for a in made]
        + [pltpu.VMEM((4, 16, WIDE[i]), bf16) for i in range(N)] * 2
        + [pltpu.VMEM((rows_of(i), WIDE[i]), bf16) for i in range(N)]
        + [pltpu.VMEM(full(i), bf16) for i in QKV + OUT]
        + [pltpu.VMEM((TOK, 128), f32), pltpu.VMEM((TOK, 128), f32), dma((2,)), dma((2,)), dma((12,))]
        + [dma((6,)), dma((N, 3)), dma((N, 3)), dma((N,)), dma((N, 2, 3)), dma((N, 2, 3)), dma((N, 4)), dma((N, 4)), dma((N, 4)), dma((N, 4))],
        compiler_params=pltpu.CompilerParams(collective_id=1, has_side_effects=True, vmem_limit_bytes=60 << 20),
        name="front",
    )(*args)
    return res[:12], [o.reshape(4, 32 * rows_of(i), WIDE[i]) for i, o in enumerate(res[12:])]


STRIDE = 5
PEERS = 32
BLOCK = 2 * CAP
GROUP = CHUNK // BLOCK


def shift_of(s):
    t = (s * STRIDE) % PEERS
    return t // 8, (t // 2) % 4, t % 2


def shifted(at, s, sign):
    dz, dx, dc = shift_of(s)
    other = (at["core"] + dc) % 2
    way = 1 - 2 * at["core"] if sign == 1 else 2 * other - 1
    return {**at, "z": (at["z"] + way * dz + 4) % 4, "x": (at["x"] + way * dx + 4) % 4, "core": other}


def moe_kernel(*refs):
    nt_h, cot_h, cotp_h, resid_h = refs[:4]
    pulls, (sg_h, su_h, sd_h) = refs[4:11], refs[11:14]
    gates_h, router_h, hits_h, owner_h, gm_h, um_h, dm_h = pulls
    out_r, gnt_r, misc_r, gg_h, gu_h, gd_h, gsg_h, gsu_h, gsd_h = refs[14:23]
    gates_r, router_r, hits, owner, gm, um, dm = here = refs[23:30]
    (
        gg_o, gu_o, gd_o, nt2, cot2, gates2, gated, gate_out, gate_in, out_n, out_g, arr_n, arr_g, ret_m, ret_b,
        gx, ux, dx, hid, act_s, slope_s, acc, grecv_a, grecv_b, part_s, part_r, pick_s, pick_r,
        sg_v, su_v, sd_v, shid, ntt, nt_x, cot_x, shid_x, dgate_s, dup_s, dgate_x, dup_x, sib_send, sib_recv,
        pair_send, pair_recv, rep_send, rep_recv, n_send, n_recv, g_send, g_recv, m_send, m_recv, b_send, b_recv,
        gate_send, gate_recv, self_sem, load_sem, pull_sem,
    ) = refs[30:]
    at = place()
    partner = partner_of(at)
    sibling = moved(at, "core", 1)
    twin = moved(at, "y", 2)
    nt_r, cot = nt2.at[0], cot2.at[0]
    first = [
        pltpu.make_async_copy(src, dst, pull_sem.at[k])
        for k, (src, dst) in enumerate([*zip(pulls, here), (nt_h, nt_r), (cot_h, cot), (cotp_h, cot2.at[1])])
    ]
    for copy in first:
        copy.start()
    barrier = pltpu.get_barrier_semaphore()
    for to in (partner, twin):
        pl.semaphore_signal(barrier, inc=1, device_id=device(to), device_id_type=MESH)

    def hello(s, carry):
        pl.semaphore_signal(barrier, inc=1, device_id=device(shifted(at, s, 1)), device_id_type=MESH)
        return carry

    lax.fori_loop(1, PEERS, hello, 0)
    pl.semaphore_wait(barrier, PEERS + 1)

    def remote(src, dst, s, r, to):
        return pltpu.make_async_remote_copy(src_ref=src, dst_ref=dst, send_sem=s, recv_sem=r, device_id=device(to), device_id_type=MESH)

    started = []

    def go(copy):
        copy.start()
        started.append(copy)
        return copy

    pair = [go(remote(src, dst, pair_send.at[k], pair_recv.at[k], partner)) for k, (src, dst) in enumerate(((nt_h, nt2.at[1]), (gates_h, gates2)))]
    swaps = [go(remote(src, dst, rep_send.at[k], rep_recv.at[k], twin)) for k, (src, dst) in enumerate(((gm_h, gx), (um_h, ux), (dm_h, dx)))]

    their_columns = pl.ds(pl.multiple_of((1 - at["core"]) * 768, 128), 768)
    beside = [go(remote(src, dst, sib_send.at[k], sib_recv.at[k], sibling)) for k, (src, dst) in enumerate(((nt_h, nt_x), (cot_h.at[:, their_columns], cot_x)))]
    theirs = pl.ds(2 * (1 - at["core"]), 2)

    def load(src, dst, k):
        copy = pltpu.make_async_copy(src, dst, load_sem.at[k])
        copy.start()
        return copy

    sd_copy = load(sd_h, sd_v, 4)
    loads = {}
    for j in range(2):
        loads[j] = (load(sg_h.at[j], sg_v.at[j], j), load(su_h.at[j], su_v.at[j], 2 + j))
    for copy in first:
        copy.wait()

    def fill(k, gates):
        rows = slice(k * TOK, (k + 1) * TOK)
        gated[rows] = (hits[rows].astype(f32) * dot(gates.astype(bf16), owner[...])).astype(bf16)

    selves = [n_send, g_send, m_send, b_send]

    def send_rows(box, land, c, ssem, rsem, sign):
        def one(s, carry):
            remote(box.at[s], land.at[s], ssem.at[s], rsem.at[s], shifted(at, s, sign)).start()
            return carry
        if c == 0:
            pltpu.make_async_copy(box.at[0], land.at[0], self_sem.at[[k for k, sem in enumerate(selves) if sem is ssem][0]]).start()
        lax.fori_loop(max(1, c * GROUP), (c + 1) * GROUP, one, 0)

    def wait_rows(box, land, c, ssem, rsem, sign, sent):
        def one(s, carry):
            copy = remote(box.at[s], land.at[s], ssem.at[s], rsem.at[s], shifted(at, s, sign))
            if sent:
                copy.wait_send()
            else:
                copy.wait_recv()
            return carry
        if c == 0 and not sent:
            pltpu.make_async_copy(box.at[0], land.at[0], self_sem.at[[k for k, sem in enumerate(selves) if sem is ssem][0]]).wait()
        lax.fori_loop(max(1, c * GROUP), (c + 1) * GROUP, one, 0)

    chunks = range(SLOTS // CHUNK)

    def lanes_of(c):
        return slice(c * CHUNK, (c + 1) * CHUNK)

    def blocks_of(c):
        return slice(c * GROUP, (c + 1) * GROUP)

    def send_cotangents(c, left):
        rows = t_dot(left[:, lanes_of(c)], cot2[...].reshape(2 * TOK, D))
        out_g[blocks_of(c)] = rows.astype(bf16).reshape(GROUP, BLOCK, D)
        send_rows(out_g, arr_g, c, g_send, g_recv, 1)

    send_cotangents(0, hits)
    fill(0, gates_r[...])
    ntt[:, :TOK] = flip(nt_r[...])
    for copy in pair:
        copy.wait_recv()
    fill(1, gates2[...])
    for c in chunks:
        rows = t_dot(hits[:, lanes_of(c)], nt2[...].reshape(2 * TOK, D))
        out_n[blocks_of(c)] = rows.astype(bf16).reshape(GROUP, BLOCK, D)
        send_rows(out_n, arr_n, c, n_send, n_recv, 1)
    gate = t_dot(gated[:, :CHUNK], jnp.ones((2 * TOK, 128), bf16))
    gate_out[...] = gate.astype(bf16).reshape(GROUP, BLOCK, 128)
    gate_in[0] = gate_out[0]
    for s in range(1, GROUP):
        go(remote(gate_out.at[s], gate_in.at[s], gate_send.at[s], gate_recv.at[s], shifted(at, s, 1)))
    for c in chunks[1:]:
        send_cotangents(c, gated)

    sd_copy.wait()
    gh = jnp.zeros((TOK, 1024), f32)
    for j in range(4):
        gh = gh + dot_t(cot[:, j * 384 : (j + 1) * 384], sd_v[j])
    acc[...] = jnp.zeros((2 * TOK, D), f32)
    for j in range(4):
        for copy in loads[j]:
            copy.wait()
        cols = slice(j * 256, (j + 1) * 256)
        gate, up = dot(nt_r[...], sg_v[j % 2]), dot(nt_r[...], su_v[j % 2])
        act, slope = silu_parts(gate)
        shid[:, cols] = (act * up).astype(bf16)
        dgate = dgate_s[j] = (gh[:, cols] * up * slope).astype(bf16)
        dup = dup_s[j] = (gh[:, cols] * act).astype(bf16)
        acc[:TOK] += dot_t(dgate, sg_v[j % 2]) + dot_t(dup, su_v[j % 2])
        if j < 2:
            loads[j + 2] = (load(sg_h.at[j + 2], sg_v.at[j], j), load(su_h.at[j + 2], su_v.at[j], 2 + j))
    gnt_r[...] = acc[:TOK]
    resid_copy = load(resid_h, acc.at[pl.ds(0, TOK)], 5)
    for k, (src, dst) in enumerate(((dgate_s.at[theirs], dgate_x), (dup_s.at[theirs], dup_x), (shid, shid_x))):
        beside.append(go(remote(src, dst, sib_send.at[2 + k], sib_recv.at[2 + k], sibling)))
    resid_copy.wait()
    for j in range(4):
        cols = slice(j * 384, (j + 1) * 384)
        acc[:TOK, cols] += dot(shid[...], sd_v[j])
    acc[TOK:] = jnp.zeros((TOK, D), f32)
    for copy in beside:
        copy.wait_recv()
    ntt[:, TOK:] = flip(nt_x[...])
    shid_t = jnp.concatenate([flip(shid[...]), flip(shid_x[...])], axis=1)
    finals = []
    for k in range(2):
        j = 2 * at["core"] + k
        cols = pl.ds(pl.multiple_of(j * 384, 128), 384)
        sg_v[k] = dot(ntt[...], jnp.concatenate([dgate_s[j], dgate_x[k]], axis=0)).astype(bf16)
        su_v[k] = dot(ntt[...], jnp.concatenate([dup_s[j], dup_x[k]], axis=0)).astype(bf16)
        sd_v[k] = dot(shid_t, jnp.concatenate([cot2[0, :, cols], cot_x[:, k * 384 : (k + 1) * 384]], axis=0)).astype(bf16)
        for i, (src, dst) in enumerate(((sg_v, gsg_h), (su_v, gsu_h), (sd_v, gsd_h))):
            copy = pltpu.make_async_copy(src.at[k], dst.at[k], pull_sem.at[3 * k + i])
            copy.start()
            finals.append(copy)

    for copy in swaps:
        copy.wait_recv()
    halves = ((gm, um, dm), (gx, ux, dx))
    for c in chunks:
        wait_rows(out_n, arr_n, c, n_send, n_recv, 1, False)
        x = arr_n[blocks_of(c)].reshape(CHUNK, D)
        total = None
        for k, (g, u, d) in enumerate(halves):
            cols = slice(k * 256, (k + 1) * 256)
            gate, up = dot(x, g[...]), dot(x, u[...])
            act, slope = silu_parts(gate)
            hidden = (act * up).astype(bf16)
            hid[lanes_of(c), cols] = hidden
            act_s[lanes_of(c), cols] = act.astype(bf16)
            slope_s[lanes_of(c), cols] = (up * slope).astype(bf16)
            part = dot(hidden, d[...])
            total = part if total is None else total + part
        wait_rows(out_n, arr_n, c, n_send, n_recv, 1, True)
        out_n[blocks_of(c)] = total.astype(bf16).reshape(GROUP, BLOCK, D)
        send_rows(out_n, ret_m, c, m_send, m_recv, -1)
    for c in chunks:
        wait_rows(out_g, arr_g, c, g_send, g_recv, 1, False)
        if c == 0:
            for s in range(1, GROUP):
                remote(gate_out.at[s], gate_in.at[s], gate_send.at[s], gate_recv.at[s], shifted(at, s, 1)).wait_recv()
            gate = gate_in[...].reshape(CHUNK, 128)[:, :1].astype(f32)
            slot = (arr_g[blocks_of(0)].reshape(CHUNK, D).astype(f32) * gate).astype(bf16)
            arr_g[blocks_of(0)] = slot.reshape(GROUP, BLOCK, D)
        slot = arr_g[blocks_of(c)].reshape(CHUNK, D)
        total = None
        for k, (g, u, d) in enumerate(halves):
            cols = slice(k * 256, (k + 1) * 256)
            gh = dot_t(slot, d[...])
            dgate = (gh * slope_s[lanes_of(c), cols].astype(f32)).astype(bf16)
            dup = (gh * act_s[lanes_of(c), cols].astype(f32)).astype(bf16)
            slope_s[lanes_of(c), cols], act_s[lanes_of(c), cols] = dgate, dup
            part = dot_t(dgate, g[...]) + dot_t(dup, u[...])
            total = part if total is None else total + part
        wait_rows(out_g, arr_g, c, g_send, g_recv, 1, True)
        out_g[blocks_of(c)] = total.astype(bf16).reshape(GROUP, BLOCK, D)
        send_rows(out_g, ret_b, c, b_send, b_recv, -1)
    for copy in finals:
        copy.wait()
    for b in range(4):
        cols = slice(b * 384, (b + 1) * 384)
        xt = flip(jnp.concatenate([arr_n[blocks_of(c), :, cols].reshape(CHUNK, 384) for c in chunks], axis=0))
        gg = dot(xt, slope_s[...])
        gu = dot(xt, act_s[...])
        gg_o[cols], gu_o[cols] = gg[:, :256], gu[:, :256]
        sg_v[0, cols], sg_v[1, cols] = gg[:, 256:].astype(bf16), gu[:, 256:].astype(bf16)
    trade = [go(remote(sg_v, grecv_a, rep_send.at[3], rep_recv.at[3], twin))]
    hid_t = flip(hid[...])
    for b in range(4):
        cols = slice(b * 384, (b + 1) * 384)
        gd = dot(hid_t, jnp.concatenate([arr_g[blocks_of(c), :, cols].reshape(CHUNK, 384) for c in chunks], axis=0))
        gd_o[:, cols] = gd[:256]
        sd_v[0, b * 256 : (b + 1) * 256] = gd[256:].astype(bf16)
    trade.append(go(remote(sd_v.at[0], grecv_b, rep_send.at[4], rep_recv.at[4], twin)))

    picked = jnp.zeros((2 * TOK, 128), f32)
    for c in chunks:
        wait_rows(out_n, ret_m, c, m_send, m_recv, -1, False)
        rows = ret_m[blocks_of(c)].reshape(CHUNK, D)
        acc[...] += dot(gated[:, lanes_of(c)], rows)
        grads = dot_t(cot2[...].reshape(2 * TOK, D), rows) * hits[:, lanes_of(c)].astype(f32)
        high = grads.astype(bf16)
        low = (grads - high.astype(f32)).astype(bf16)
        own = owner[:, lanes_of(c)]
        picked = picked + dot_t(high, own) + dot_t(low, own)
    part_s[0] = acc[TOK:].astype(bf16)
    pick_s[...] = picked[TOK:]
    pair.append(go(remote(part_s.at[0], part_r.at[0], pair_send.at[2], pair_recv.at[2], partner)))
    pair.append(go(remote(pick_s, pick_r, pair_send.at[3], pair_recv.at[3], partner)))
    pair[2].wait_recv()
    out_r[...] = (acc[:TOK] + part_r[0].astype(f32)).astype(bf16)
    pair[3].wait_recv()
    picked = picked[:TOK] + pick_r[...]
    gates = gates_r[...]
    mean = jnp.sum(gates * picked, axis=-1, keepdims=True)
    gl = (gates * (picked - mean)).astype(bf16)
    misc_r[...] = dot(ntt[:, :TOK], gl)
    acc[:TOK] = gnt_r[...] + dot_t(gl, router_r[...])
    acc[TOK:] = jnp.zeros((TOK, D), f32)
    for c in chunks:
        wait_rows(out_g, ret_b, c, b_send, b_recv, -1, False)
        acc[...] += dot(hits[:, lanes_of(c)], ret_b[blocks_of(c)].reshape(CHUNK, D))
    part_s[1] = acc[TOK:].astype(bf16)
    pair.append(go(remote(part_s.at[1], part_r.at[1], pair_send.at[4], pair_recv.at[4], partner)))
    trade[0].wait_recv()
    gg_o[...] += grecv_a[0].astype(f32)
    gu_o[...] += grecv_a[1].astype(f32)
    trade[1].wait_recv()
    for b in range(4):
        gd_o[:, b * 384 : (b + 1) * 384] += grecv_b[b * 256 : (b + 1) * 256].astype(f32)
    outs = []
    for k, (src, dst) in enumerate(((gg_o, gg_h), (gu_o, gu_h), (gd_o, gd_h))):
        outs.append(pltpu.make_async_copy(src, dst, pull_sem.at[k]))
        outs[-1].start()
    pair[4].wait_recv()
    gnt_r[...] = acc[:TOK] + part_r[1].astype(f32)
    for c in chunks:
        wait_rows(out_n, ret_m, c, m_send, m_recv, -1, True)
        wait_rows(out_g, ret_b, c, b_send, b_recv, -1, True)
    for copy in outs:
        copy.wait()
    for copy in started:
        copy.wait_send()


def moe(nt, cot, cotp, resid, gates, router, hits, owner, mine, sg, su, sd):
    dma = pltpu.SemaphoreType.DMA
    vm = lambda shape, dtype=bf16: pltpu.VMEM(shape, dtype)
    rows = (PEERS, BLOCK, D)
    return pl.pallas_call(
        moe_kernel,
        out_shape=[sds((TOK, D)), sds((TOK, D), f32), sds((D, 128), f32), sds((D, 256), f32), sds((D, 256), f32), sds((256, D), f32)]
        + [sds((2, D, 256)), sds((2, D, 256)), sds((2, 1024, 384))],
        in_specs=[ANY] * 14,
        out_specs=[VM] * 3 + [ANY] * 6,
        scratch_shapes=[vm((TOK, 128), f32), vm((D, 128)), vm((2 * TOK, SLOTS)), vm((128, SLOTS)), vm((D, 256)), vm((D, 256)), vm((256, D))]
        + [vm((D, 256), f32), vm((D, 256), f32), vm((256, D), f32)]
        + [vm((2, TOK, D)), vm((2, TOK, D)), vm((TOK, 128), f32), vm((2 * TOK, SLOTS)), vm((GROUP, BLOCK, 128)), vm((GROUP, BLOCK, 128))]
        + [vm(rows)] * 6
        + [vm((D, 256)), vm((D, 256)), vm((256, D)), vm((SLOTS, 512)), vm((SLOTS, 512)), vm((SLOTS, 512)), vm((2 * TOK, D), f32)]
        + [vm((2, D, 256)), vm((1024, 384)), vm((2, TOK, D)), vm((2, TOK, D)), vm((TOK, 128), f32), vm((TOK, 128), f32)]
        + [vm((2, D, 256)), vm((2, D, 256)), vm((4, 1024, 384)), vm((TOK, 1024)), vm((D, 2 * TOK)), vm((TOK, D)), vm((TOK, 768)), vm((TOK, 1024))]
        + [vm((4, TOK, 256)), vm((4, TOK, 256)), vm((2, TOK, 256)), vm((2, TOK, 256)), dma((5,)), dma((5,))]
        + [dma((5,)), dma((5,)), dma((5,)), dma((5,))] + [dma((PEERS,))] * 8 + [dma((GROUP,)), dma((GROUP,)), dma((4,)), dma((6,)), dma((10,))],
        compiler_params=pltpu.CompilerParams(collective_id=3, has_side_effects=True, vmem_limit_bytes=127 << 19),
        name="moe",
    )(nt, cot, cotp, resid, gates, router, hits, owner, *mine, sg, su, sd)


SUMS = (256, 256, 128, 128, 128, 256, 256, 256, 384)


def sum_box(i):
    return core_box(i)[:5] + (SUMS[i],)


class Scatter(Links):
    def __init__(self, total, landing, spread, outs, own_sem, rsend, rrecv, send, recv, msend, mrecv):
        super().__init__()
        self.total, self.landing, self.spread, self.outs = total, landing, spread, outs
        self.own_sem, self.rsend, self.rrecv = own_sem, rsend, rrecv
        self.send, self.recv, self.msend, self.mrecv = send, recv, msend, mrecv

    def spot(self, i, done, where, half=None):
        return region(where, ORDERS[i], done, half=half)[1:]

    def add(self, i, where, ref, *spots):
        to = self.total[i]
        total = to[where].astype(f32)
        for spot in spots:
            total = total + ref[spot].astype(f32)
        to[where] = total.astype(bf16)

    def start(self, i, src):
        self.sent[i] = pltpu.make_async_copy(src, self.total[i], self.own_sem.at[i])
        self.sent[i].start()

    def message(self, i, side, number):
        axis, done = ORDERS[i][2], ORDERS[i][:2]
        step = STEPS[side]
        spot, k = ((self.near(axis, 2), side), (self.near(axis, step), 1 - side), (self.near(axis, step), side))[number]
        src = self.total[i].at[self.spot(i, done, spot, k)]
        dst = self.landing[i][0].at[side, number]
        self.sent[i, 2, side, number] = self.go(src, dst, self.rsend.at[i, side, number], self.rrecv.at[i, side, number], self.near(axis, step))

    def enter(self, i):
        if i in SHARED:
            self.sent[i].wait()
        for number in range(2):
            for side in range(2):
                self.message(i, side, number)

    def relay(self, i):
        axis, done = ORDERS[i][2], ORDERS[i][:2]
        for side in range(2):
            self.sent[i, 2, side, 0].wait_recv()
            self.add(i, self.spot(i, done, self.near(axis, STEPS[side]), side), self.landing[i][0], (side, 0))
            self.message(i, side, 2)

    def direct(self, i, phase):
        axis, done = ORDERS[i][phase], ORDERS[i][:phase]
        self.sent[i, phase] = [
            self.go(self.total[i].at[self.spot(i, done, self.near(axis, by))], self.landing[i][2 - phase].at[k], self.send.at[i, phase, k], self.recv.at[i, phase, k], self.near(axis, by))
            for k, by in enumerate(STEPS)
        ]

    def second(self, i):
        done = ORDERS[i][:2]
        for side in range(2):
            for number in (1, 2):
                self.sent[i, 2, side, number].wait_recv()
        for k in range(2):
            self.add(i, self.spot(i, done, self.at, k), self.landing[i][0], (k, 2), (1 - k, 1))
        self.direct(i, 1)

    def third(self, i):
        for copy in self.sent[i, 1]:
            copy.wait_recv()
        self.add(i, self.spot(i, ORDERS[i][:1], self.at), self.landing[i][1], 0, 1, 2)
        self.direct(i, 0)

    def spread_rows(self, i):
        for copy in self.sent[i, 0]:
            copy.wait_recv()
        chunk = self.total[i][self.spot(i, "", self.at)].astype(f32)
        for k in range(3):
            chunk = chunk + self.landing[i][2][k].astype(f32)
        size, take = rows_of(i), PIECE[i]
        to_row, from_row = iota((64, size), 0), iota((64, size), 1)
        pick = ((from_row // take) * 16 + from_row % take == to_row).astype(bf16)
        laid = dot(pick, chunk.astype(bf16)).astype(bf16)
        self.spread[i][...] = laid.reshape(4, 16, SUMS[i])
        own = pltpu.make_async_copy(self.spread[i].at[self.mine], self.outs[i].at[self.mine], self.own_sem.at[i])
        own.start()
        finals = [own]
        for k, to in enumerate(self.peers):
            quarter = to["core"] * 2 + to["y"] // 2
            finals.append(self.go(self.spread[i].at[quarter], self.outs[i].at[self.mine], self.msend.at[i, k], self.mrecv.at[i, k], to))
        self.sent[i, "final"] = finals

    def finish(self):
        for i in range(N):
            own, *copies = self.sent[i, "final"]
            own.wait()
            for copy in copies:
                copy.wait_recv()
        self.end()


def half_box(order):
    return {"xyz": (2, 2, 2), "yzx": (4, 2), "zxy": (2, 4)}[order]


def back_kernel(*refs):
    pulls, shared_h, weights = refs[:11], refs[11:14], refs[14:20]
    gtok_o, *outs = refs[20:30]
    total = refs[30:39]
    landing = [refs[39 + 3 * i : 42 + 3 * i] for i in range(N)]
    spread = refs[66:75]
    gnt, resid_r, cot, tokens, normed_r, q_r, kv_r, p_r, att_r, misc_in, misc_w = here = refs[75:86]
    left_s, right_s, gv_s, goo_s, gatt_s, turned, acc, gres, misc_s, slots = refs[86:96]
    normed_x, att_x, goo_x, left_x, right_x, gv_x, misc_x, slot_sem, pull_sem, sib_send, sib_recv, *sems = refs[96:]
    s = Scatter(total, landing, spread, outs, *sems)
    core = s.core
    loads = {}

    def load(j, parts):
        loads[j] = []
        at_lane = 0
        for k, (i, width) in enumerate(parts):
            src = weights[i].at[j] if width == WIDE[i] else weights[i].at[j, :, pl.ds(0, width)]
            copy = pltpu.make_async_copy(src, slots.at[j, :, pl.ds(at_lane, width)], slot_sem.at[j, k])
            copy.start()
            loads[j].append(copy)
            at_lane += width

    def loaded(j):
        for copy in loads[j]:
            copy.wait()

    def weight_grads(group, right):
        for k in range(2):
            for i, value in zip(group, right(2 * core + k, k)):
                total[i][k] = value.astype(bf16).reshape(sum_box(i)[1:])

    def tell(k, src, dst):
        s.sent["told", k] = s.go(src, dst, sib_send.at[k], sib_recv.at[k], s.sibling)

    def told(*which):
        for k in which:
            s.sent["told", k].wait_recv()

    theirs = pl.ds(2 * (1 - core), 2)
    s.pull(pulls, here, pull_sem)
    for i, src in zip(SHARED, shared_h):
        s.start(i, src)
    for j in range(4):
        load(j, [(3, 128), (4, 128), (5, 128)])
    s.greet()
    tell(0, pulls[4], normed_x)
    tell(1, pulls[8], att_x)
    for i in SHARED:
        s.enter(i)
    s.pulled()

    resid = resid_r[...]
    scale = rms_scale(resid)
    grad = gnt[...]
    lane = iota((TOK, 128), 1)
    gres[...] = cot[...].astype(f32) + norm_back(grad, resid, scale, gain_row(misc_w[...], 65))
    acc[...] = jnp.zeros((TOK, D), f32)
    for j in range(4):
        goo_s[j] = gres[:, j * 384 : (j + 1) * 384].astype(bf16)
        loaded(j)
        acc[...] += dot_t(goo_s[j], slots[j])
        load(j, [(0, 256), (2, 128)])
    for j in range(4):
        gatt_s[j] = acc[:, j * 384 : (j + 1) * 384].astype(bf16)
    tell(2, goo_s.at[theirs], goo_x)
    turned[:, :TOK] = flip(normed_r[...])
    told(0)
    turned[:, TOK:] = flip(normed_x[...])
    for j in range(4):
        ga, q, kv, p = gatt_s[j], q_r[j], kv_r[j], p_r[j]
        ga3 = jnp.concatenate([ga[:, :128], ga[:, 128:256], ga[:, 256:]], axis=0)
        q3 = jnp.concatenate([q[:, :128], q[:, 128:256], q[:, 256:]], axis=0)
        gp = dot_t(ga3, kv[:, 128:])
        gs = (p * (gp - jnp.sum(p * gp, axis=-1, keepdims=True))).astype(bf16)
        gq3 = (dot(gs, kv[:, :128]) * SCALE).astype(bf16)
        gk = (t_dot(gs, q3) * SCALE).astype(bf16)
        gv_s[j] = t_dot(p.astype(bf16), ga3).astype(bf16)
        left_s[j] = jnp.concatenate([gq3[:128], gq3[128:256]], axis=1)
        right_s[j] = jnp.concatenate([gq3[256:], gk], axis=1)
    tell(3, left_s.at[theirs], left_x)
    tell(4, right_s.at[theirs], right_x)
    tell(5, gv_s.at[theirs], gv_x)
    for i in SHARED:
        s.relay(i)
    told(3, 4, 5)

    def both(mine, other):
        return dot(turned[...], jnp.concatenate([mine, other], axis=0))

    weight_grads(QKV, lambda j, k: (both(left_s[j], left_x[k]), both(right_s[j], right_x[k]), both(gv_s[j], gv_x[k])))
    for i in QKV:
        s.enter(i)
    resid = resid_r[...]
    misc_s[...] = misc_in[...] + t_dot((gnt[...] * resid * rms_scale(resid)).astype(bf16), (lane == 65).astype(bf16))
    acc[...] = jnp.zeros((TOK, D), f32)
    for j in range(4):
        loaded(j)
        acc[...] += dot_t(jnp.concatenate([left_s[j], gv_s[j]], axis=1), slots[j])
        load(j, [(1, 256)])
    for j in range(4):
        loaded(j)
        acc[...] += dot_t(right_s[j], slots[j, :, :256])
    source = tokens[...].astype(f32)
    scale = rms_scale(source)
    misc_s[...] += t_dot((acc[...] * source * scale).astype(bf16), (lane == 64).astype(bf16))
    tell(6, misc_s, misc_x)
    told(1, 2)
    for j in range(4):
        turned[j * 384 : (j + 1) * 384, :TOK] = flip(att_r[j])
        turned[j * 384 : (j + 1) * 384, TOK:] = flip(att_x[j])
    told(6)

    def out_grads(j, k):
        whole = both(goo_s[j], goo_x[k])
        misc = (misc_s[...] + misc_x[...]) * jnp.where(j == 0, 1.0, 0.0)
        return whole[:, :128], whole[:, 128:256], jnp.concatenate([whole[:, 256:], misc], axis=1)

    weight_grads(OUT, out_grads)
    for i in QKV:
        s.relay(i)
    for i in OUT:
        s.enter(i)
    gtok_o[...] = gres[...] + norm_back(acc[...], source, scale, gain_row(misc_w[...], 64))
    for i in SHARED:
        s.second(i)
    for i in OUT:
        s.relay(i)
    for i in SHARED:
        s.third(i)
    for i in QKV:
        s.second(i)
    for i in SHARED:
        s.spread_rows(i)
    for i in OUT:
        s.second(i)
    for i in QKV:
        s.third(i)
    for i in OUT:
        s.third(i)
    for i in QKV:
        s.spread_rows(i)
    for i in OUT:
        s.spread_rows(i)
    s.finish()


def back(*args, shared_grads, weights):
    grads = [g.reshape(sum_box(i)) for i, g in zip(SHARED, shared_grads)]
    vm = lambda shape, dtype=bf16: pltpu.VMEM(shape, dtype)
    dma = pltpu.SemaphoreType.DMA
    halves = [vm(sum_box(i)) for i in range(N)]
    scratch = list(halves)
    for i in range(N):
        tail = (rows_of(i), SUMS[i])
        scratch += [vm((2, 3) + half_box(ORDERS[i]) + tail), vm((3,) + axis_box(ORDERS[i][0]) + tail), vm((3,) + tail)]
    scratch += [vm((4, 16, w)) for w in SUMS]
    scratch += [vm(a.shape, a.dtype) for a in args]
    scratch += [vm((4, TOK, 256)), vm((4, TOK, 256)), vm((4, TOK, 128)), vm((4, TOK, 384)), vm((4, TOK, 384)), vm((D, 2 * TOK)), vm((TOK, D), f32), vm((TOK, D), f32), vm((D, 128), f32), vm((4, D, 384))]
    scratch += [vm((TOK, D)), vm((4, TOK, 384)), vm((2, TOK, 384)), vm((2, TOK, 256)), vm((2, TOK, 256)), vm((2, TOK, 128)), vm((D, 128), f32), dma((4, 3)), dma((11,)), dma((7,)), dma((7,))]
    scratch += [dma((N,)), dma((N, 2, 3)), dma((N, 2, 3)), dma((N, 2, 3)), dma((N, 2, 3)), dma((N, 3)), dma((N, 3))]
    return pl.pallas_call(
        back_kernel,
        out_shape=[sds((TOK, D), f32)] + [sds((4, 16, w)) for w in SUMS],
        in_specs=[ANY] * 20,
        out_specs=[VM] * 10,
        scratch_shapes=scratch,
        compiler_params=pltpu.CompilerParams(collective_id=2, has_side_effects=True, vmem_limit_bytes=63 << 20),
        name="back",
    )(*args, *grads, *weights)


def final_kernel(*refs):
    gtok, block, gg, gu, gd = refs[:5]
    outs = refs[5:14]
    block_o, gtok_o, gq_o, gk_o, gv_o, go_o, gsg_o, gsu_o, gsd_o, gr_o, g1_o, g2_o, gg_o, gu_o, gd_o = refs[14:29]
    held, into, away = refs[29:34], refs[34], refs[35]
    large = ((gg, gg_o), (gu, gu_o), (gd, gd_o), (gtok, gtok_o), (block, block_o))
    loads = [pltpu.make_async_copy(src, mid, into.at[k]) for k, ((src, dst), mid) in enumerate(zip(large, held))]
    copies = [pltpu.make_async_copy(mid, dst, away.at[k]) for k, ((src, dst), mid) in enumerate(zip(large, held))]
    for load in loads:
        load.start()
    for load, copy in zip(loads, copies):
        load.wait()
        copy.start()
    for j in range(4):
        block = [outs[i][j].astype(f32)[: PIECE[i]] for i in range(N)]
        gq_o[:, j * 384 : j * 384 + 256] = block[0]
        gq_o[:, j * 384 + 256 : (j + 1) * 384] = block[1][:, :128]
        gk_o[:, j * 128 : (j + 1) * 128] = block[1][:, 128:]
        gv_o[:, j * 128 : (j + 1) * 128] = block[2]
        for p in range(3):
            go_o[:, j * 384 + p * 128 : j * 384 + (p + 1) * 128] = block[3 + p][:, :128]
        gsg_o[:, j * 256 : (j + 1) * 256] = block[6]
        gsu_o[:, j * 256 : (j + 1) * 256] = block[7]
        gsd_o[:, j * 384 : (j + 1) * 384] = block[8]
    misc = outs[5][0].astype(f32)[:12, 128:]
    gr_o[...] = misc[:, :64]
    eye = iota((12, 12), 0) == iota((12, 12), 1)
    for k, out in ((64, g1_o), (65, g2_o)):
        out[...] = jnp.sum(jnp.where(eye, misc[:, k : k + 1], 0.0), axis=0, keepdims=True)
    for copy in copies:
        copy.wait()


def final(gtok, block, expert, pieces):
    shapes = ((TOK, D), (12, D), (12, 512), (12, 512), (12, D), (12, 1024), (12, 1024), (8, D), (12, 64), (1, 12), (1, 12), (D, 256), (D, 256), (256, D))
    return pl.pallas_call(
        final_kernel,
        out_shape=[sds((TOK, D))] + [sds(s, f32) for s in shapes],
        in_specs=[ANY] * 5 + [VM] * 9,
        out_specs=[ANY] * 2 + [VM] * 10 + [ANY] * 3,
        scratch_shapes=[pltpu.VMEM(a.shape, a.dtype) for a in (*expert, gtok, block)] + [pltpu.SemaphoreType.DMA((5,))] * 2,
        compiler_params=pltpu.CompilerParams(vmem_limit_bytes=63 << 20),
        name="final",
    )(gtok, block, *expert, *pieces)


def local(tokens, segment_ids, routes, cotangent, query_weight, key_weight, value_weight, output_weight, shared_gate, shared_up, shared_down, router_weight, first_gain, second_gain, expert_gate, expert_up, expert_down):
    (normed, q, kv, p, att, resid, nt, gates, misc_w, hits, owner, cotp), weights = front(
        tokens, segment_ids, routes.T, query_weight, key_weight, value_weight, output_weight, router_weight,
        first_gain[None], second_gain[None], shared_gate, shared_up, shared_down, cotangent,
    )
    mine = [expert_gate[0], expert_up[0], expert_down[0]]
    block, gnt, gmisc, gg, gu, gd, *shared_grads = moe(
        nt, cotangent, cotp, resid, gates, misc_w, hits, owner, mine, *weights[6:]
    )
    gtok, *pieces = back(
        gnt, resid, cotangent, tokens, normed, q, kv, p, att, gmisc, misc_w, shared_grads=shared_grads, weights=weights[:6]
    )
    *outs, g1, g2, gg, gu, gd = final(gtok, block, (gg, gu, gd), pieces)
    return *outs, g1[0], g2[0], gg[None], gu[None], gd[None]


def solution(mesh):
    in_specs = (
        P(("fsdp", "rep"), None),
        P(("fsdp", "rep"), None),
        P(("fsdp", "rep"), None),
        P(("fsdp", "rep"), None),
        P(("fsdp", "rep"), None),
        P(("fsdp", "rep"), None),
        P(("fsdp", "rep"), None),
        P(("fsdp", "rep"), None),
        P(("fsdp", "rep"), None),
        P(("fsdp", "rep"), None),
        P(("fsdp", "rep"), None),
        P(("fsdp", "rep"), None),
        P(("fsdp", "rep")),
        P(("fsdp", "rep")),
        P("fsdp", None, "rep"),
        P("fsdp", None, "rep"),
        P("fsdp", "rep", None),
    )
    out_specs = (
        P(("fsdp", "rep"), None),
        P(("fsdp", "rep"), None),
        P(("fsdp", "rep"), None),
        P(("fsdp", "rep"), None),
        P(("fsdp", "rep"), None),
        P(("fsdp", "rep"), None),
        P(("fsdp", "rep"), None),
        P(("fsdp", "rep"), None),
        P(("fsdp", "rep"), None),
        P(("fsdp", "rep"), None),
        P(("fsdp", "rep")),
        P(("fsdp", "rep")),
        P("fsdp", None, "rep"),
        P("fsdp", None, "rep"),
        P("fsdp", "rep", None),
    )
    return jax.shard_map(local, mesh=mesh, in_specs=in_specs, out_specs=out_specs, check_vma=False)
```
